512 devices in a mesh: scene: 8 (over y), space: 64 (over x, z, core).
Axes of the slice: x: 4, y: 8, z: 8, core: 2. Of those that a mesh axis runs over, the one named last changes fastest.
Arguments:
- features: bfloat16 [8, 256, 64, 128], P('scene', 'space'), may hold values from -40 to 40, as said below
- active: int32 [8, 256], P('scene', 'space'), may hold values from 0 to 1, as said below
- neighbor_owner: int32 [8, 256, 26], P('scene', 'space'), may hold values from -1 to 63, as said below
- record_position: int32 [8, 256, 26], P('scene', 'space'), may hold values from 0 to 9, as said below
- send_list: int32 [8, 64, 64, 10], P('scene', 'space'), may hold values from -1 to 23, as said below
- conv_first: bfloat16 [27, 128, 128], replicated, may hold values from -0.109375 to 0.109375
- conv_second: bfloat16 [27, 128, 128], replicated, may hold values from -0.109375 to 0.109375
- gain_first: float32 [128], replicated, may hold values from 0.4 to 1.6
- bias_first: float32 [128], replicated, may hold values from -3 to 3
- gain_second: float32 [128], replicated, may hold values from 0.4 to 1.6
- bias_second: float32 [128], replicated, may hold values from -3 to 3
- grad_output: bfloat16 [8, 256, 64, 128], P('scene', 'space'), may hold values from -6 to 6, as said below
Outputs:
- block_output: bfloat16 [8, 256, 64, 128], P('scene', 'space')
- grad_input: bfloat16 [8, 256, 64, 128], P('scene', 'space')
- grad_conv_first: bfloat16 [3456, 128], P('space')
- grad_conv_second: bfloat16 [3456, 128], P('space')
The draws below stay inside these ranges and needn't reach their ends.
Inputs may be any that keep to these rules, and one draw needn't show every extreme that they name: `features`: finite values. `grad_output`: finite values. Each device's active bricks fill its first slots; in every scene some device has all 4 slots active. `neighbor_owner`: -1 where a slot is inactive or its neighbour in that direction is absent; otherwise the neighbour is an active brick whose owner's index differs from the slot's own device by 0, 1, 3, 4 or 5 in either direction, and adjacency is mutual with the opposite direction. `record_position`: 0 where there is no neighbour; the records from one owner to one device are numbered from 0 without gaps. send_list[s, p, k] = slot * 6 + face of the plane that device s sends as record k to device p within a scene, -1 for unused entries; each list holds at most 10 records and some list holds exactly 10 in every scene.
All inputs are finite; a program needn't handle non-finite values.
Results may differ from the reference program's by a relative error of at most 0.0051.
Values may be sent and summed in bfloat16 or wider, within the bound.
No kernel may reach another device: no remote copies, remote signals or barrier semaphores. Data moves between devices by JAX's collectives and lax.ppermute only.
A program may use at most 128 MiB of HBM per device.

```python
import jax
import jax.numpy as jnp
from jax import lax

C = 128
GROUPS = 32
EDGE = 4
SLOTS = 4
ROW_SPAN = 4
SCENES = 8
PEERS = 64
BRICKS = 256
VOX = 64
CAP = 10


def leading_axis_drawn(direction):
    for dimension in range(3):
        if direction[dimension] != 0:
            return dimension
    return 0


def scene_layout(key):
    load_key, pick_key = jax.random.split(key)
    device_ids = jnp.arange(PEERS, dtype=jnp.int32)
    load_count = jax.random.randint(load_key, (PEERS,), 0, SLOTS + 1)
    chosen = jax.random.randint(pick_key, (), 0, PEERS - ROW_SPAN)
    forced = (device_ids == chosen) | (device_ids == chosen + ROW_SPAN)
    load_count = jnp.where(forced, SLOTS, load_count)
    slot_ids = jnp.arange(SLOTS, dtype=jnp.int32)
    active_slot = slot_ids[None, :] < load_count[:, None]
    coord_x = jnp.broadcast_to(slot_ids[None, :], (PEERS, SLOTS))
    coord_y = jnp.broadcast_to((device_ids % ROW_SPAN)[:, None], (PEERS, SLOTS))
    coord_z = jnp.broadcast_to((device_ids // ROW_SPAN)[:, None], (PEERS, SLOTS))
    grid_depth = PEERS // ROW_SPAN
    owner_list = []
    plane_list = []
    for ordinal in range(27):
        if ordinal == 13:
            continue
        direction = (ordinal // 9 - 1, ordinal // 3 % 3 - 1, ordinal % 3 - 1)
        leading = leading_axis_drawn(direction)
        face_id = 2 * leading + (0 if direction[leading] > 0 else 1)
        near_x = coord_x + direction[0]
        near_y = coord_y + direction[1]
        near_z = coord_z + direction[2]
        inside = (near_x >= 0) & (near_x < SLOTS) & (near_y >= 0) & (near_y < ROW_SPAN) & (near_z >= 0) & (near_z < grid_depth)
        near_dev = jnp.clip(near_y + ROW_SPAN * near_z, 0, PEERS - 1)
        near_slot = jnp.clip(near_x, 0, SLOTS - 1)
        present = inside & active_slot & active_slot[near_dev, near_slot]
        owner_list.append(jnp.where(present, near_dev, -1))
        plane_list.append(near_slot * 6 + face_id)
    owners = jnp.stack(owner_list, axis=-1).astype(jnp.int32)
    planes = jnp.stack(plane_list, axis=-1).astype(jnp.int32)
    entry_count = SLOTS * 26
    owner_rows = owners.reshape(PEERS, entry_count)
    entry_ids = jnp.arange(entry_count, dtype=jnp.int32)
    earlier = entry_ids[None, :] < entry_ids[:, None]
    matching = owner_rows[:, :, None] == owner_rows[:, None, :]
    record_rank = jnp.sum((matching & earlier[None]).astype(jnp.int32), axis=2).reshape(PEERS, SLOTS, 26)
    position = jnp.where(owners >= 0, record_rank, 0).astype(jnp.int32)
    source_dev = jnp.where(owners >= 0, owners, PEERS)
    target_dev = jnp.broadcast_to(device_ids[:, None, None], owners.shape)
    send_table = jnp.full((PEERS, PEERS, CAP), -1, jnp.int32).at[source_dev, target_dev, position].set(planes, mode='drop')
    return (active_slot.astype(jnp.int32).reshape(PEERS * SLOTS), owners.reshape(PEERS * SLOTS, 26), position.reshape(PEERS * SLOTS, 26), send_table)


def scene_batch(key):
    scene_keys = jax.random.split(key, SCENES)
    return jax.vmap(scene_layout)(scene_keys)


def draw_active(key, part):
    return scene_batch(key)[0]


def draw_neighbor_owner(key, part):
    return scene_batch(key)[1]


def draw_record_position(key, part):
    return scene_batch(key)[2]


def draw_send_list(key, part):
    return scene_batch(key)[3]


def draw_features(key, part):
    key = jax.random.fold_in(key, 11)
    noise_key, channel_key = jax.random.split(key)
    device_pos = (jnp.arange(BRICKS) // SLOTS).astype(jnp.float32) / (PEERS - 1)
    channel_scale = 10.0 ** (jax.random.uniform(channel_key, (C,), jnp.float32) - 0.5)
    row_scale = 0.3 * 10.0 ** device_pos
    base = jax.random.truncated_normal(noise_key, -4.0, 4.0, (SCENES, BRICKS, VOX, C), jnp.float32)
    return (base * row_scale[None, :, None, None] * channel_scale).astype(jnp.bfloat16)


def draw_grad_output(key, part):
    key = jax.random.fold_in(key, 23)
    noise_key, sign_key, size_key = jax.random.split(key, 3)
    channel_sign = jnp.where(jax.random.bernoulli(sign_key, 0.5, (C,)), 1.0, -1.0).astype(jnp.float32)
    scene_sign = jnp.where(jnp.arange(SCENES) % 2 == 0, 1.0, -1.0).astype(jnp.float32)
    magnitude = jax.random.uniform(size_key, (C,), jnp.float32, 2.0, 3.2)
    noise = 0.8 * jax.random.truncated_normal(noise_key, -3.5, 3.5, (SCENES, BRICKS, VOX, C), jnp.float32)
    offset = scene_sign[:, None] * (channel_sign * magnitude)[None, :]
    values = noise + offset[:, None, None, :]
    return jnp.clip(values, -6.0, 6.0).astype(jnp.bfloat16)


def normal_values(rng, extent, deviation, most, kind=jnp.bfloat16):
    return jnp.clip(deviation * jax.random.normal(rng, extent, jnp.float32), -most, most).astype(kind)


def setup_inputs(seed: int = 0) -> dict:
    arg_keys = jax.random.split(jax.random.key(seed), 13)
    return {
        "features": draw_features(jax.random.fold_in(arg_keys[12], 71), 0),
        "active": draw_active(jax.random.fold_in(arg_keys[12], 71), 0),
        "neighbor_owner": draw_neighbor_owner(jax.random.fold_in(arg_keys[12], 71), 0),
        "record_position": draw_record_position(jax.random.fold_in(arg_keys[12], 71), 0),
        "send_list": draw_send_list(jax.random.fold_in(arg_keys[12], 71), 0),
        "conv_first": normal_values(arg_keys[5], (27, C, C), (27 * C) ** -0.5, 0.109375),
        "conv_second": normal_values(arg_keys[6], (27, C, C), (27 * C) ** -0.5, 0.109375),
        "gain_first": jnp.clip(1.0 + 0.12 * jax.random.normal(arg_keys[7], (C,), jnp.float32), 0.4, 1.6),
        "bias_first": normal_values(arg_keys[8], (C,), 0.5, 3.0, jnp.float32),
        "gain_second": jnp.clip(1.0 + 0.12 * jax.random.normal(arg_keys[9], (C,), jnp.float32), 0.4, 1.6),
        "bias_second": normal_values(arg_keys[10], (C,), 0.5, 3.0, jnp.float32),
        "grad_output": draw_grad_output(jax.random.fold_in(arg_keys[12], 71), 0),
    }


directions = [(ordinal // 9 - 1, ordinal // 3 % 3 - 1, ordinal % 3 - 1) for ordinal in range(27) if ordinal != 13]
norm_eps = 1e-05

def leading_axis(direction):
    for dimension in range(3):
        if direction[dimension] != 0:
            return dimension
    return 0

def end_planes(brick_field, brick_edge):
    slot_count, channels = (brick_field.shape[0], brick_field.shape[2])
    brick_cube = brick_field.reshape(slot_count, brick_edge, brick_edge, brick_edge, channels)
    layers = [brick_cube[:, 0], brick_cube[:, -1], brick_cube[:, :, 0], brick_cube[:, :, -1], brick_cube[:, :, :, 0], brick_cube[:, :, :, -1]]
    return jnp.stack(layers, axis=1).reshape(slot_count * 6, brick_edge * brick_edge, channels)

def place_record(padded, record, direction, brick_edge):
    leading = leading_axis(direction)
    record = record.reshape(record.shape[0], brick_edge, brick_edge, record.shape[-1])
    source = [slice(None)]
    for dimension in range(3):
        if dimension == leading:
            continue
        if direction[dimension] == 0:
            source.append(slice(None))
        elif direction[dimension] > 0:
            source.append(slice(0, 1))
        else:
            source.append(slice(brick_edge - 1, brick_edge))
    source.append(slice(None))
    slab_piece = jnp.expand_dims(record[tuple(source)], leading + 1)
    target = [slice(None)]
    for dimension in range(3):
        if direction[dimension] == 0:
            target.append(slice(1, brick_edge + 1))
        elif direction[dimension] > 0:
            target.append(slice(brick_edge + 1, brick_edge + 2))
        else:
            target.append(slice(0, 1))
    target.append(slice(None))
    return padded.at[tuple(target)].set(slab_piece)

def surround(brick_field, records, owners, brick_edge):
    slot_count, channels = (brick_field.shape[0], brick_field.shape[2])
    wide_edge = brick_edge + 2
    padded = jnp.zeros((slot_count, wide_edge, wide_edge, wide_edge, channels), brick_field.dtype)
    inner = brick_field.reshape(slot_count, brick_edge, brick_edge, brick_edge, channels)
    padded = padded.at[:, 1:brick_edge + 1, 1:brick_edge + 1, 1:brick_edge + 1].set(inner)
    for number, direction in enumerate(directions):
        picked = records[:, number]
        picked = jnp.where((owners[:, number] >= 0)[:, None, None], picked, jnp.zeros_like(picked))
        padded = place_record(padded, picked, direction, brick_edge)
    return padded

def unfold(padded, brick_edge, flipped):
    slot_count, channels = (padded.shape[0], padded.shape[-1])
    columns = []
    for ordinal in range(27):
        offset_x, offset_y, offset_z = (ordinal // 9, ordinal // 3 % 3, ordinal % 3)
        if flipped:
            offset_x, offset_y, offset_z = (2 - offset_x, 2 - offset_y, 2 - offset_z)
        window = padded[:, offset_x:offset_x + brick_edge, offset_y:offset_y + brick_edge, offset_z:offset_z + brick_edge]
        columns.append(window.reshape(slot_count * brick_edge ** 3, channels))
    return jnp.concatenate(columns, axis=1)

def group_sums(values):
    per_channel = lax.optimization_barrier(jnp.sum(values, axis=(0, 1)))
    return per_channel.reshape(GROUPS, -1).sum(axis=1)

def scene_halo(brick_field, owners, positions, sendlist):
    brick_count, channels = (brick_field.shape[0], brick_field.shape[2])
    planes = end_planes(brick_field, EDGE).reshape(brick_count // SLOTS, SLOTS * 6, EDGE * EDGE, channels)
    device_of = (jnp.arange(brick_count) // SLOTS).astype(jnp.int32)
    safe_owner = jnp.maximum(owners, 0).astype(jnp.int32)
    plane_ids = jnp.maximum(sendlist[safe_owner, device_of[:, None], positions], 0).astype(jnp.int32)
    records = planes[safe_owner, plane_ids]
    return surround(brick_field, records, owners, EDGE)

def norm_forward(values, weight, gain_row, bias_row):
    per_group = values.shape[2] // GROUPS
    masked = values * weight[:, None, None]
    count = jnp.sum(weight) * (values.shape[1] * per_group)
    group_mean = group_sums(masked) / count
    inverse_std = lax.rsqrt(group_sums(masked * values) / count - group_mean * group_mean + norm_eps)
    channel_inv = jnp.repeat(inverse_std, per_group)
    centred = (values - jnp.repeat(group_mean, per_group)) * channel_inv
    shifted = centred * gain_row + bias_row
    return (centred, shifted, channel_inv, count)

def norm_backward(grad_act, centred, shifted, channel_inv, gain_row, weight, count):
    per_group = centred.shape[2] // GROUPS
    sigmoid_value = jax.nn.sigmoid(shifted)
    grad_centred = grad_act * weight[:, None, None] * sigmoid_value * (1.0 + shifted * (1.0 - sigmoid_value)) * gain_row
    sum_grad = group_sums(grad_centred) / count
    sum_cross = group_sums(grad_centred * centred) / count
    return weight[:, None, None] * channel_inv * (grad_centred - jnp.repeat(sum_grad, per_group) - centred * jnp.repeat(sum_cross, per_group))

def scene_block(scene_items, conv_first, conv_second, gain_first, bias_first, gain_second, bias_second):
    features, active, owners, positions, sendlist, grad_output = scene_items
    brick_count, voxels, channels = features.shape
    weight = active.astype(jnp.float32)
    weight_first = conv_first.reshape(27 * channels, channels)
    weight_second = conv_second.reshape(27 * channels, channels)
    back_first = jnp.transpose(conv_first, (0, 2, 1)).reshape(27 * channels, channels)
    back_second = jnp.transpose(conv_second, (0, 2, 1)).reshape(27 * channels, channels)
    input_wide = features.astype(jnp.float32)
    centred_a, shifted_a, inv_a, count_a = norm_forward(input_wide, weight, gain_first, bias_first)
    act_first = (jax.nn.silu(shifted_a) * weight[:, None, None]).astype(jnp.bfloat16)
    cols_first = unfold(scene_halo(act_first, owners, positions, sendlist), EDGE, False)
    middle = jnp.dot(cols_first, weight_first, preferred_element_type=jnp.float32).reshape(brick_count, voxels, channels)
    centred_b, shifted_b, inv_b, count_b = norm_forward(middle, weight, gain_second, bias_second)
    act_second = (jax.nn.silu(shifted_b) * weight[:, None, None]).astype(jnp.bfloat16)
    cols_second = unfold(scene_halo(act_second, owners, positions, sendlist), EDGE, False)
    conv_out = jnp.dot(cols_second, weight_second, preferred_element_type=jnp.float32).reshape(brick_count, voxels, channels)
    block_output = ((input_wide + conv_out) * weight[:, None, None]).astype(jnp.bfloat16)
    grad_top = jnp.where(weight[:, None, None] > 0.0, grad_output, jnp.zeros_like(grad_output))
    grad_flat = grad_top.reshape(brick_count * voxels, channels)
    grad_second_w = lax.dot_general(cols_second, grad_flat, (((0,), (0,)), ((), ())), preferred_element_type=jnp.float32)
    cols_grad = unfold(scene_halo(grad_top, owners, positions, sendlist), EDGE, True)
    grad_act_second = jnp.dot(cols_grad, back_second, preferred_element_type=jnp.float32).reshape(brick_count, voxels, channels)
    grad_middle = norm_backward(grad_act_second, centred_b, shifted_b, inv_b, gain_second, weight, count_b).astype(jnp.bfloat16)
    grad_first_w = lax.dot_general(cols_first, grad_middle.reshape(brick_count * voxels, channels), (((0,), (0,)), ((), ())), preferred_element_type=jnp.float32)
    cols_middle = unfold(scene_halo(grad_middle, owners, positions, sendlist), EDGE, True)
    grad_act_first = jnp.dot(cols_middle, back_first, preferred_element_type=jnp.float32).reshape(brick_count, voxels, channels)
    grad_input = (grad_top.astype(jnp.float32) + norm_backward(grad_act_first, centred_a, shifted_a, inv_a, gain_first, weight, count_a)).astype(jnp.bfloat16)
    return (block_output, grad_input, grad_first_w, grad_second_w)

def reference(features, active, neighbor_owner, record_position, send_list, conv_first, conv_second, gain_first, bias_first, gain_second, bias_second, grad_output):

    def per_scene(scene_items):
        return scene_block(scene_items, conv_first, conv_second, gain_first, bias_first, gain_second, bias_second)
    outputs = lax.map(per_scene, (features, active, neighbor_owner, record_position, send_list, grad_output))
    block_output, grad_input, grad_first_w, grad_second_w = outputs
    grad_conv_first = lax.optimization_barrier(jnp.sum(grad_first_w, axis=0)).astype(jnp.bfloat16)
    grad_conv_second = lax.optimization_barrier(jnp.sum(grad_second_w, axis=0)).astype(jnp.bfloat16)
    return (block_output, grad_input, grad_conv_first, grad_conv_second)
```

```python
import jax
import jax.numpy as jnp
from jax import lax
from jax.experimental import pallas as pl
from jax.experimental.pallas import tpu as pltpu
from jax.sharding import PartitionSpec as P

EDGE = 4
SLOTS = 4
VOX = 64
C = 128
CAP = 10
PEERS = 64
PLANE = 16
SHARE = 54
GROUP_COUNT = 64 * 4
EPS = 1e-05

directions = [
    (ordinal // 9 - 1, ordinal // 3 % 3 - 1, ordinal % 3 - 1)
    for ordinal in range(27)
    if ordinal != 13
]
offsets = (1, -1, 3, -3, 4, -4, 5, -5)
LANES = 11
ZERO_PLANE = 3 * CAP

f32 = jnp.float32
bf16 = jnp.bfloat16
VMEM_BYTES = 40 * 1024 * 1024


def group_total(row):
    lane = lax.broadcasted_iota(jnp.int32, row.shape, 1)
    row = row + jnp.where(lane % 2 == 0, pltpu.roll(row, C - 1, 1), pltpu.roll(row, 1, 1))
    return row + jnp.where(lane % 4 < 2, pltpu.roll(row, C - 2, 1), pltpu.roll(row, 2, 1))


def pack_stats(rows):
    rows = [jnp.broadcast_to(row, (8, C)) for row in rows]
    lane = lax.broadcasted_iota(jnp.int32, (8, C), 1)
    packed = jnp.zeros((8, C), f32)
    for n, row in enumerate(rows):
        packed = jnp.where(lane % 4 == n, group_total(row), packed)
    return packed


def unpack_stat(packed, n):
    lane = lax.broadcasted_iota(jnp.int32, packed.shape, 1)
    return group_total(jnp.where(lane % 4 == n, packed, 0.0))


def total_of(stats_ref):
    return jnp.broadcast_to(jnp.sum(stats_ref[...], axis=0, keepdims=True), (8, C))


def norm_stats(stats_ref):
    packed = total_of(stats_ref)
    count = unpack_stat(packed, 2) * (GROUP_COUNT / 4)
    mean = unpack_stat(packed, 0) / count
    inv = lax.rsqrt(unpack_stat(packed, 1) / count - mean * mean + EPS)
    return mean[0:1], inv[0:1], count[0:1]


def sigmoid(n):
    return 1.0 / (1.0 + jnp.exp(-n))


def slot_weight(active_ref, s):
    return active_ref[0, s].astype(f32)


def planes_of(src, dst):
    for s in range(SLOTS):
        dst[6 * s] = src[s, 0:16]
        dst[6 * s + 1] = src[s, 48:64]
        for a in range(4):
            dst[6 * s + 2, 4 * a : 4 * a + 4] = src[s, 16 * a : 16 * a + 4]
            dst[6 * s + 3, 4 * a : 4 * a + 4] = src[s, 16 * a + 12 : 16 * a + 16]
        dst[6 * s + 4] = src[s, pl.ds(0, 16, stride=4)]
        dst[6 * s + 5] = src[s, pl.ds(3, 16, stride=4)]


def fill_sends(list_ref, me, planes_a, planes_b, outs):
    for out, offset in zip(outs, (0,) + offsets):
        target = jnp.clip(me + offset, 0, PEERS - 1)
        for k in range(CAP):
            plane = jnp.maximum(list_ref[target, k], 0)
            out[k] = planes_a[plane].astype(out.dtype)
            out[CAP + k] = planes_b[plane].astype(out.dtype)


def lane_start(offset):
    return (5 - offset) * CAP


def place_halo(pad, table, own_ref, pos_ref, me):
    def one_slot(s, carry):
        for n, (d0, d1, d2) in enumerate(directions):
            owner = own_ref[s, n]
            index = jnp.where(owner >= 0, (owner - me + 5) * CAP + pos_ref[s, n], ZERO_PLANE)
            cells = [(5 if d > 0 else 0, 0 if d > 0 else 3) for d in (d0, d1, d2)]
            (a_to, _), (b_to, b_from), (c_to, c_from) = cells

            def row(r, count=1):
                return table[index, r : r + count]

            if d0 != 0:
                if d1 == 0 and d2 == 0:
                    for b in range(4):
                        pad[s, a_to, 1 + b, 1:5] = row(4 * b, 4)
                elif d2 == 0:
                    pad[s, a_to, b_to, 1:5] = row(4 * b_from, 4)
                elif d1 == 0:
                    for b in range(4):
                        pad[s, a_to, 1 + b, c_to : c_to + 1] = row(4 * b + c_from)
                else:
                    pad[s, a_to, b_to, c_to : c_to + 1] = row(4 * b_from + c_from)
            elif d1 != 0:
                for a in range(4):
                    if d2 == 0:
                        pad[s, 1 + a, b_to, 1:5] = row(4 * a, 4)
                    else:
                        pad[s, 1 + a, b_to, c_to : c_to + 1] = row(4 * a + c_from)
            else:
                for a in range(4):
                    for b in range(4):
                        pad[s, 1 + a, 1 + b, c_to : c_to + 1] = row(4 * a + b)
        return carry

    lax.fori_loop(0, SLOTS, one_slot, 0)


def place_interior(pad, field):
    for s in range(SLOTS):
        for a in range(4):
            for b in range(4):
                pad[s, 1 + a, 1 + b, 1:5] = field[s, 16 * a + 4 * b : 16 * a + 4 * b + 4]


def windows_of(pad, cols):
    def one_layer(t, carry):
        s, a = t // 6, t % 6
        sub = lax.broadcasted_iota(jnp.int32, (8, C), 0)
        layer = [pad[s, a, b] for b in range(6)]
        for k2 in range(3):
            low = [pltpu.roll(v, (8 - k2) % 8, 0) if k2 else v for v in layer]
            high = [pltpu.roll(v, 4 - k2, 0) for v in layer]
            pair = [jnp.where(sub < 4, low[b], high[b + 1]) for b in range(5)]
            for k1 in range(3):
                tile = jnp.concatenate([pair[k1], pair[k1 + 2]], axis=0)
                cols[3 * k1 + k2, s, a] = tile.astype(bf16)
        return carry

    lax.fori_loop(0, SLOTS * 6, one_layer, 0)


def window(cols, k0, k1, k2):
    return cols[3 * k1 + k2, :, k0 : k0 + 4].reshape(SLOTS * VOX, C)


def conv(cols, weight):
    total = jnp.zeros((SLOTS * VOX, C), f32)
    for k0 in range(3):
        left = jnp.concatenate([window(cols, k0, j // 3, j % 3) for j in range(9)], axis=1)
        right = weight[9 * k0 : 9 * k0 + 9].reshape(9 * C, C)
        total = total + jnp.dot(left, right, preferred_element_type=f32)
    return total


def conv_back(cols, weight):
    total = jnp.zeros((SLOTS * VOX, C), f32)
    for k0 in range(3):
        left = jnp.concatenate(
            [window(cols, 2 - k0, 2 - j // 3, 2 - j % 3) for j in range(9)], axis=1
        )
        right = jnp.concatenate([weight[9 * k0 + j] for j in range(9)], axis=1)
        total = total + lax.dot_general(
            left, right, (((1,), (1,)), ((), ())), preferred_element_type=f32
        )
    return total


def weight_grad(cols, grad, out):
    for k0 in range(3):
        left = jnp.concatenate([window(cols, k0, j // 3, j % 3) for j in range(9)], axis=1)
        out[9 * C * k0 : 9 * C * (k0 + 1)] = lax.dot_general(
            left, grad, (((0,), (0,)), ((), ())), preferred_element_type=f32
        )


def send_kernel(feat, gout, active, send_list, stats, *rest):
    outs, (wide_f, wide_g, planes_f, planes_g) = rest[:9], rest[9:]
    me = lax.axis_index("space")
    wide_f[...] = feat[...].astype(f32)
    wide_g[...] = gout[...].astype(f32)
    planes_of(wide_f, planes_f)
    planes_of(wide_g, planes_g)
    fill_sends(send_list, me, planes_f, planes_g, outs)
    total = jnp.zeros((1, C), f32)
    squares = jnp.zeros((1, C), f32)
    slots = 0.0
    for s in range(SLOTS):
        w = slot_weight(active, s)
        x = wide_f[s]
        total = total + w * jnp.sum(x, axis=0, keepdims=True)
        squares = squares + w * jnp.sum(x * x, axis=0, keepdims=True)
        slots = slots + w
    packed = pack_stats([total, squares, jnp.full((1, C), slots, f32)])
    stats[...] = jnp.broadcast_to(packed[0:1], (PEERS, C))


def first_kernel(
    feat, gout, active, owners, positions, send_list, stats1, gain1, bias1, w1, w2, *rest
):
    tables, rest = rest[:9], rest[9:]
    middle, gas, cols_a, stats2 = rest[:4]
    outs, (table_f, table_g, pad, cols_g, act, planes_m, planes_g) = rest[4:13], rest[13:]
    me = lax.axis_index("space")
    mean, inv, _ = norm_stats(stats1)

    def act_of(x):
        n = (x - mean) * inv * gain1[...] + bias1[...]
        return n * sigmoid(n)

    for tab, offset in zip(tables, (0,) + offsets):
        start = lane_start(offset)
        table_f[start : start + CAP] = act_of(tab[0:CAP].astype(f32))
        table_g[start : start + CAP] = tab[CAP : 2 * CAP].astype(f32)
    table_f[ZERO_PLANE] = jnp.zeros((PLANE, C), f32)
    table_g[ZERO_PLANE] = jnp.zeros((PLANE, C), f32)
    for s in range(SLOTS):
        act[s] = slot_weight(active, s) * act_of(feat[s].astype(f32))
    place_interior(pad, act)
    place_halo(pad, table_f, owners, positions, me)
    windows_of(pad, cols_a)
    middle[...] = conv(cols_a, w1).reshape(SLOTS, VOX, C)
    for s in range(SLOTS):
        act[s] = jnp.where(active[0, s] > 0, gout[s].astype(f32), 0.0)
    place_interior(pad, act)
    place_halo(pad, table_g, owners, positions, me)
    windows_of(pad, cols_g)
    gas[...] = conv_back(cols_g, w2).reshape(SLOTS, VOX, C)
    planes_of(middle, planes_m)
    planes_of(gas, planes_g)
    fill_sends(send_list, me, planes_m, planes_g, outs)
    total = jnp.zeros((1, C), f32)
    squares = jnp.zeros((1, C), f32)
    slots = 0.0
    for s in range(SLOTS):
        w = slot_weight(active, s)
        x = middle[s]
        total = total + w * jnp.sum(x, axis=0, keepdims=True)
        squares = squares + w * jnp.sum(x * x, axis=0, keepdims=True)
        slots = slots + w
    packed = pack_stats([total, squares, jnp.full((1, C), slots, f32)])
    stats2[...] = jnp.broadcast_to(packed[0:1], (PEERS, C))


def second_kernel(
    feat, gout, active, owners, positions, middle, gas, stats2, gain2, bias2, w2, *rest
):
    tables, rest = rest[:9], rest[9:]
    block, stats3, grad_w, table, pad, cols, act = rest
    me = lax.axis_index("space")
    mean, inv, _ = norm_stats(stats2)
    gain = gain2[...]
    bias = bias2[...]
    for tab, offset in zip(tables, (0,) + offsets):
        start = lane_start(offset)
        n = (tab[0:CAP] - mean) * inv * gain + bias
        table[start : start + CAP] = n * sigmoid(n)
    table[ZERO_PLANE] = jnp.zeros((PLANE, C), f32)
    sum_q = jnp.zeros((1, C), f32)
    sum_c = jnp.zeros((1, C), f32)
    for s in range(SLOTS):
        w = slot_weight(active, s)
        hat = (middle[s] - mean) * inv
        n = hat * gain + bias
        sg = sigmoid(n)
        act[s] = w * (n * sg)
        q = gas[s] * w * sg * (1.0 + n * (1.0 - sg)) * gain
        sum_q = sum_q + jnp.sum(q, axis=0, keepdims=True)
        sum_c = sum_c + jnp.sum(q * hat, axis=0, keepdims=True)
    packed = pack_stats([sum_q, sum_c])
    stats3[...] = jnp.broadcast_to(packed[0:1], (PEERS, C))
    place_interior(pad, act)
    place_halo(pad, table, owners, positions, me)
    windows_of(pad, cols)
    out = conv(cols, w2).reshape(SLOTS, VOX, C)
    for s in range(SLOTS):
        w = slot_weight(active, s)
        block[s] = ((feat[s].astype(f32) + out[s]) * w).astype(bf16)
        act[s] = jnp.where(active[0, s] > 0, gout[s].astype(f32), 0.0)
    weight_grad(cols, act[...].astype(bf16).reshape(SLOTS * VOX, C), grad_w)


def third_kernel(
    feat,
    active,
    owners,
    positions,
    middle,
    gas,
    stats1,
    stats2,
    stats3,
    gain1,
    bias1,
    gain2,
    bias2,
    w1,
    cols_a,
    grad_w2,
    *rest,
):
    tables, rest = rest[:9], rest[9:]
    q1, share, table, pad, cols, act, grad_w1 = rest
    me = lax.axis_index("space")
    mean, inv, count = norm_stats(stats2)
    gain = gain2[...]
    bias = bias2[...]
    packed = total_of(stats3)
    mean_q = unpack_stat(packed, 0)[0:1] / count
    mean_c = unpack_stat(packed, 1)[0:1] / count

    def grad_of(x, g):
        hat = (x - mean) * inv
        n = hat * gain + bias
        sg = sigmoid(n)
        q = g * sg * (1.0 + n * (1.0 - sg)) * gain
        return (inv * (q - mean_q - hat * mean_c)).astype(bf16).astype(f32)

    for tab, offset in zip(tables, (0,) + offsets):
        start = lane_start(offset)
        table[start : start + CAP] = grad_of(tab[0:CAP], tab[CAP : 2 * CAP])
    table[ZERO_PLANE] = jnp.zeros((PLANE, C), f32)
    for s in range(SLOTS):
        act[s] = slot_weight(active, s) * grad_of(middle[s], gas[s])
    place_interior(pad, act)
    place_halo(pad, table, owners, positions, me)
    windows_of(pad, cols)
    gaf = conv_back(cols, w1).reshape(SLOTS, VOX, C)
    mean1, inv1, _ = norm_stats(stats1)
    sum_q = jnp.zeros((1, C), f32)
    sum_c = jnp.zeros((1, C), f32)
    for s in range(SLOTS):
        hat = (feat[s].astype(f32) - mean1) * inv1
        n = hat * gain1[...] + bias1[...]
        sg = sigmoid(n)
        q = gaf[s] * slot_weight(active, s) * sg * (1.0 + n * (1.0 - sg)) * gain1[...]
        q1[s] = q
        sum_q = sum_q + jnp.sum(q, axis=0, keepdims=True)
        sum_c = sum_c + jnp.sum(q * hat, axis=0, keepdims=True)
    packed = pack_stats([sum_q, sum_c])
    weight_grad(cols_a, act[...].astype(bf16).reshape(SLOTS * VOX, C), grad_w1)
    for p in range(PEERS):
        core, chip = p % 2, p // 2
        share[core, chip, 0:SHARE] = grad_w1[SHARE * p : SHARE * (p + 1)]
        share[core, chip, 56 : 56 + SHARE] = grad_w2[SHARE * p : SHARE * (p + 1)]
        share[core, chip, SHARE : SHARE + 1] = packed[0:1]
        share[core, chip, SHARE + 1 : SHARE + 2] = packed[0:1]
        share[core, chip, 56 + SHARE : 112] = jnp.zeros((2, C), f32)


def last_kernel(feat, gout, active, stats1, q1, parts, gain1, grad_in, rows):
    total = parts[0]
    for n in range(1, 32):
        total = total + parts[n]
    mean1, inv1, count = norm_stats(stats1)
    packed = jnp.broadcast_to(total[SHARE : SHARE + 1], (8, C))
    mean_q = unpack_stat(packed, 0)[0:1] / count
    mean_c = unpack_stat(packed, 1)[0:1] / count
    for s in range(SLOTS):
        hat = (feat[s].astype(f32) - mean1) * inv1
        back = slot_weight(active, s) * inv1 * (q1[s] - mean_q - hat * mean_c)
        top = jnp.where(active[0, s] > 0, gout[s].astype(f32), 0.0)
        grad_in[s] = (top + back).astype(bf16)
    for n in range(8):
        rows[n] = total


vmem = pl.BlockSpec(memory_space=pltpu.VMEM)
smem = pl.BlockSpec(memory_space=pltpu.SMEM)


def call(kernel, specs, out_shape, scratch, args):
    return pl.pallas_call(
        kernel,
        in_specs=specs,
        out_specs=[vmem] * len(out_shape),
        out_shape=out_shape,
        scratch_shapes=scratch,
        compiler_params=pltpu.CompilerParams(vmem_limit_bytes=VMEM_BYTES),
    )(*args)


def shape(*dims, dtype=f32):
    return jax.ShapeDtypeStruct(dims, dtype)


def shifted(value, steps):
    leading, last = max(0, -steps), min(PEERS, PEERS - steps)
    return lax.ppermute(value, "space", [(n, n + steps) for n in range(leading, last)])


def exchange(sends):
    return [sends[0]] + [shifted(block, offset) for block, offset in zip(sends[1:], offsets)]


def spread(stats):
    return lax.all_to_all(stats, "space", 0, 0, tiled=True)


core_groups = [[2 * n, 2 * n + 1] for n in range(PEERS // 2)]
chip_groups = [list(range(core, PEERS, 2)) for core in range(2)]


def per_device(
    features,
    active,
    neighbor_owner,
    record_position,
    send_list,
    conv_first,
    conv_second,
    gain_first,
    bias_first,
    gain_second,
    bias_second,
    grad_output,
):
    feat = features[0]
    gout = grad_output[0]
    owners = neighbor_owner[0]
    positions = record_position[0]
    lists = send_list[0, 0]
    gain1, bias1 = gain_first.reshape(1, C), bias_first.reshape(1, C)
    gain2, bias2 = gain_second.reshape(1, C), bias_second.reshape(1, C)
    field = (SLOTS, VOX, C)
    planes = pltpu.VMEM((24, PLANE, C), f32)
    wide = pltpu.VMEM(field, f32)
    table = pltpu.VMEM((LANES * CAP, PLANE, C), f32)
    pad = pltpu.VMEM((SLOTS, 6, 6, 8, C), f32)
    cols_shape = (9, SLOTS, 6, PLANE, C)
    cols = pltpu.VMEM(cols_shape, bf16)

    stats1, *sends = call(
        send_kernel,
        [vmem, vmem, smem, smem],
        [shape(PEERS, C)] + [shape(2 * CAP, PLANE, C, dtype=bf16)] * 9,
        [wide, wide, planes, planes],
        (feat, gout, active, lists),
    )
    tables0 = exchange(sends)
    stats1 = spread(stats1)

    middle, gas, cols_a, stats2, *sends = call(
        first_kernel,
        [vmem, vmem, smem, smem, smem, smem] + [vmem] * 14,
        [shape(*field), shape(*field), shape(*cols_shape, dtype=bf16), shape(PEERS, C)]
        + [shape(2 * CAP, PLANE, C)] * 9,
        [table, table, pad, cols, wide, planes, planes],
        (feat, gout, active, owners, positions, lists, stats1, gain1, bias1)
        + (conv_first, conv_second, *tables0),
    )
    tables1 = exchange(sends)
    stats2 = spread(stats2)

    block, stats3, grad_w2 = call(
        second_kernel,
        [vmem, vmem, smem, smem, smem] + [vmem] * 15,
        [shape(*field, dtype=bf16), shape(PEERS, C), shape(27 * C, C)],
        [table, pad, cols, wide],
        (feat, gout, active, owners, positions, middle, gas, stats2, gain2, bias2)
        + (conv_second, *tables1),
    )
    stats3 = spread(stats3)

    q1, share = call(
        third_kernel,
        [vmem, smem, smem, smem] + [vmem] * 21,
        [shape(*field), shape(2, PEERS // 2, 112, C)],
        [table, pad, cols, wide, pltpu.VMEM((27 * C, C), f32)],
        (feat, active, owners, positions, middle, gas, stats1, stats2, stats3)
        + (gain1, bias1, gain2, bias2, conv_first, cols_a, grad_w2, *tables1),
    )
    share = lax.all_to_all(share, "space", 0, 0, axis_index_groups=core_groups)
    share = share[0] + share[1]
    share = lax.all_to_all(share, "space", 0, 0, axis_index_groups=chip_groups)

    grad_in, rows = call(
        last_kernel,
        [vmem, vmem, smem, vmem, vmem, vmem, vmem],
        [shape(*field, dtype=bf16), shape(8, 112, C)],
        [],
        (feat, gout, active, stats1, q1, share, gain1),
    )
    rows = lax.all_to_all(rows, "scene", 0, 0)
    rows = jnp.sum(rows, axis=0).astype(bf16)
    return (block[None], grad_in[None], rows[:SHARE], rows[56 : 56 + SHARE])


def solution(mesh):
    return jax.shard_map(
        per_device,
        mesh=mesh,
        in_specs=(
            P("scene", "space", None, None),
            P("scene", "space"),
            P("scene", "space", None),
            P("scene", "space", None),
            P("scene", "space", None, None),
            P(),
            P(),
            P(),
            P(),
            P(),
            P(),
            P("scene", "space", None, None),
        ),
        out_specs=(
            P("scene", "space", None, None),
            P("scene", "space", None, None),
            P("space", None),
            P("space", None),
        ),
        check_vma=False,
    )
```

```python
import jax
import jax.numpy as jnp
from jax import lax
from jax.experimental import pallas as pl
from jax.experimental.pallas import tpu as pltpu
from jax.sharding import PartitionSpec as P

EDGE = 4
SLOTS = 4
VOX = 64
C = 128
CAP = 10
PEERS = 64
PLANE = 16
SHARE = 54
GROUP_COUNT = 64 * 4
EPS = 1e-05

directions = [
    (ordinal // 9 - 1, ordinal // 3 % 3 - 1, ordinal % 3 - 1)
    for ordinal in range(27)
    if ordinal != 13
]
PLANES = 24
LANES = 11
ZERO_PLANE = 3 * PLANES

f32 = jnp.float32
bf16 = jnp.bfloat16
VMEM_BYTES = 40 * 1024 * 1024


def group_total(row):
    lane = lax.broadcasted_iota(jnp.int32, row.shape, 1)
    row = row + jnp.where(lane % 2 == 0, pltpu.roll(row, C - 1, 1), pltpu.roll(row, 1, 1))
    return row + jnp.where(lane % 4 < 2, pltpu.roll(row, C - 2, 1), pltpu.roll(row, 2, 1))


def pack_stats(rows):
    rows = [jnp.broadcast_to(row, (8, C)) for row in rows]
    lane = lax.broadcasted_iota(jnp.int32, (8, C), 1)
    packed = jnp.zeros((8, C), f32)
    for n, row in enumerate(rows):
        packed = jnp.where(lane % 4 == n, group_total(row), packed)
    return packed


def unpack_stat(packed, n):
    lane = lax.broadcasted_iota(jnp.int32, packed.shape, 1)
    return group_total(jnp.where(lane % 4 == n, packed, 0.0))


def total_of(stats_ref):
    return jnp.broadcast_to(jnp.sum(stats_ref[...], axis=0, keepdims=True), (8, C))


def norm_stats(stats_ref):
    packed = total_of(stats_ref)
    count = unpack_stat(packed, 2) * (GROUP_COUNT / 4)
    mean = unpack_stat(packed, 0) / count
    inv = lax.rsqrt(unpack_stat(packed, 1) / count - mean * mean + EPS)
    return mean[0:1], inv[0:1], count[0:1]


def sigmoid(n):
    return 1.0 / (1.0 + jnp.exp(-n))


def slot_weight(active_ref, s):
    return active_ref[0, s].astype(f32)


def planes_of(src, dst, start):
    for s in range(SLOTS):
        dst[start + 6 * s] = src[s, 0:16]
        dst[start + 6 * s + 1] = src[s, 48:64]
        for a in range(4):
            dst[start + 6 * s + 2, 4 * a : 4 * a + 4] = src[s, 16 * a : 16 * a + 4]
            dst[start + 6 * s + 3, 4 * a : 4 * a + 4] = src[s, 16 * a + 12 : 16 * a + 16]
        dst[start + 6 * s + 4] = src[s, pl.ds(0, 16, stride=4)]
        dst[start + 6 * s + 5] = src[s, pl.ds(3, 16, stride=4)]


def far_distance(device):
    return 4 - 8 * ((device >> 2) & 1)


def near_distance(device):
    return 1 - 2 * (device & 1)


def fill_table(table, fields, scratch, me, make):
    near = near_distance(me)
    turn = 0
    for ref, base in zip(fields, (0, near, -near)):
        far = far_distance((me + base) & (PEERS - 1))
        for entry, more in enumerate((0, far, -far)):
            start = (base + more + 5) * PLANES
            buffer = scratch.at[turn % 2]
            turn += 1
            for s in range(SLOTS):
                buffer[s] = make(ref, entry, s)
            planes_of(buffer, table, start)
    table[ZERO_PLANE] = jnp.zeros((PLANE, C), f32)


def place_halo(pad, table, own_ref, pos_ref, ids_ref, me):
    def one_slot(s, carry):
        for n, (d0, d1, d2) in enumerate(directions):
            owner = own_ref[s, n]
            plane = jnp.clip(ids_ref[jnp.maximum(owner, 0), pos_ref[s, n]], 0, PLANES - 1)
            index = jnp.where(owner >= 0, (owner - me + 5) * PLANES + plane, ZERO_PLANE)
            cells = [(5 if d > 0 else 0, 0 if d > 0 else 3) for d in (d0, d1, d2)]
            (a_to, _), (b_to, b_from), (c_to, c_from) = cells

            def row(r, count=1):
                return table[index, r : r + count]

            if d0 != 0:
                if d1 == 0 and d2 == 0:
                    for b in range(4):
                        pad[s, a_to, 1 + b, 1:5] = row(4 * b, 4)
                elif d2 == 0:
                    pad[s, a_to, b_to, 1:5] = row(4 * b_from, 4)
                elif d1 == 0:
                    for b in range(4):
                        pad[s, a_to, 1 + b, c_to : c_to + 1] = row(4 * b + c_from)
                else:
                    pad[s, a_to, b_to, c_to : c_to + 1] = row(4 * b_from + c_from)
            elif d1 != 0:
                for a in range(4):
                    if d2 == 0:
                        pad[s, 1 + a, b_to, 1:5] = row(4 * a, 4)
                    else:
                        pad[s, 1 + a, b_to, c_to : c_to + 1] = row(4 * a + c_from)
            else:
                for a in range(4):
                    for b in range(4):
                        pad[s, 1 + a, 1 + b, c_to : c_to + 1] = row(4 * a + b)
        return carry

    lax.fori_loop(0, SLOTS, one_slot, 0)


def place_interior(pad, field):
    for s in range(SLOTS):
        for a in range(4):
            for b in range(4):
                pad[s, 1 + a, 1 + b, 1:5] = field[s, 16 * a + 4 * b : 16 * a + 4 * b + 4]


def windows_of(pad, cols):
    def one_layer(t, carry):
        s, a = t // 6, t % 6
        sub = lax.broadcasted_iota(jnp.int32, (8, C), 0)
        layer = [pad[s, a, b] for b in range(6)]
        for k2 in range(3):
            low = [pltpu.roll(v, (8 - k2) % 8, 0) if k2 else v for v in layer]
            high = [pltpu.roll(v, 4 - k2, 0) for v in layer]
            pair = [jnp.where(sub < 4, low[b], high[b + 1]) for b in range(5)]
            for k1 in range(3):
                tile = jnp.concatenate([pair[k1], pair[k1 + 2]], axis=0)
                cols[3 * k1 + k2, s, a] = tile.astype(bf16)
        return carry

    lax.fori_loop(0, SLOTS * 6, one_layer, 0)


def window(cols, k0, k1, k2):
    return cols[3 * k1 + k2, :, k0 : k0 + 4].reshape(SLOTS * VOX, C)


def conv(cols, weight):
    total = jnp.zeros((SLOTS * VOX, C), f32)
    for k0 in range(3):
        left = jnp.concatenate([window(cols, k0, j // 3, j % 3) for j in range(9)], axis=1)
        right = weight[9 * k0 : 9 * k0 + 9].reshape(9 * C, C)
        total = total + jnp.dot(left, right, preferred_element_type=f32)
    return total


def conv_back(cols, weight):
    total = jnp.zeros((SLOTS * VOX, C), f32)
    for k0 in range(3):
        left = jnp.concatenate(
            [window(cols, 2 - k0, 2 - j // 3, 2 - j % 3) for j in range(9)], axis=1
        )
        right = jnp.concatenate([weight[9 * k0 + j] for j in range(9)], axis=1)
        total = total + lax.dot_general(
            left, right, (((1,), (1,)), ((), ())), preferred_element_type=f32
        )
    return total


def weight_grad(cols, grad, out):
    for k0 in range(3):
        left = jnp.concatenate([window(cols, k0, j // 3, j % 3) for j in range(9)], axis=1)
        out[9 * C * k0 : 9 * C * (k0 + 1)] = lax.dot_general(
            left, grad, (((0,), (0,)), ((), ())), preferred_element_type=f32
        )


def start_kernel(feat, gout, active, send_list, stats, both):
    both[0] = feat[...]
    both[1] = gout[...]
    total = jnp.zeros((1, C), f32)
    squares = jnp.zeros((1, C), f32)
    slots = 0.0
    for s in range(SLOTS):
        w = slot_weight(active, s)
        x = feat[s].astype(f32)
        total = total + w * jnp.sum(x, axis=0, keepdims=True)
        squares = squares + w * jnp.sum(x * x, axis=0, keepdims=True)
        slots = slots + w
    packed = pack_stats([total, squares, jnp.full((1, C), slots, f32)])
    record = lax.broadcasted_iota(jnp.int32, (CAP, C), 0)
    lane = lax.broadcasted_iota(jnp.int32, (CAP, C), 1)
    select = jnp.where(lane == 4 * record + 3, 1.0, 0.0).astype(bf16)
    ids = jnp.dot(send_list[...].astype(bf16), select, preferred_element_type=f32)
    stats[...] = ids + packed[0:1]


def first_kernel(
    feat, gout, active, owners, positions, ids, stats1, gain1, bias1, w1, w2, *rest
):
    fields, rest = rest[:3], rest[3:]
    middle, gas, cols_a, stats2, both, table, pad, cols_g, act, scratch = rest
    me = lax.axis_index("space")
    mean, inv, _ = norm_stats(stats1)

    def act_of(x):
        n = (x - mean) * inv * gain1[...] + bias1[...]
        return n * sigmoid(n)

    fill_table(table, fields, scratch, me, lambda ref, e, s: act_of(ref[e, 0, s].astype(f32)))
    for s in range(SLOTS):
        act[s] = slot_weight(active, s) * act_of(feat[s].astype(f32))
    place_interior(pad, act)
    place_halo(pad, table, owners, positions, ids, me)
    windows_of(pad, cols_a)
    middle[...] = conv(cols_a, w1).reshape(SLOTS, VOX, C)
    fill_table(table, fields, scratch, me, lambda ref, e, s: ref[e, 1, s].astype(f32))
    for s in range(SLOTS):
        act[s] = jnp.where(active[0, s] > 0, gout[s].astype(f32), 0.0)
    place_interior(pad, act)
    place_halo(pad, table, owners, positions, ids, me)
    windows_of(pad, cols_g)
    gas[...] = conv_back(cols_g, w2).reshape(SLOTS, VOX, C)
    both[0] = middle[...].astype(bf16)
    both[1] = gas[...].astype(bf16)
    total = jnp.zeros((1, C), f32)
    squares = jnp.zeros((1, C), f32)
    slots = 0.0
    for s in range(SLOTS):
        w = slot_weight(active, s)
        x = middle[s]
        total = total + w * jnp.sum(x, axis=0, keepdims=True)
        squares = squares + w * jnp.sum(x * x, axis=0, keepdims=True)
        slots = slots + w
    packed = pack_stats([total, squares, jnp.full((1, C), slots, f32)])
    stats2[...] = jnp.broadcast_to(packed[0:1], (PEERS, C))


def second_kernel(
    feat, gout, active, owners, positions, ids, middle, gas, stats2, gain2, bias2, w2, *rest
):
    fields, rest = rest[:3], rest[3:]
    block, stats3, grad_w, table, pad, cols, act, scratch = rest
    me = lax.axis_index("space")
    mean, inv, _ = norm_stats(stats2)
    gain = gain2[...]
    bias = bias2[...]

    def act_of(ref, e, s):
        n = (ref[e, 0, s].astype(f32) - mean) * inv * gain + bias
        return n * sigmoid(n)

    fill_table(table, fields, scratch, me, act_of)
    sum_q = jnp.zeros((1, C), f32)
    sum_c = jnp.zeros((1, C), f32)
    for s in range(SLOTS):
        w = slot_weight(active, s)
        hat = (middle[s] - mean) * inv
        n = hat * gain + bias
        sg = sigmoid(n)
        act[s] = w * (n * sg)
        q = gas[s] * w * sg * (1.0 + n * (1.0 - sg)) * gain
        sum_q = sum_q + jnp.sum(q, axis=0, keepdims=True)
        sum_c = sum_c + jnp.sum(q * hat, axis=0, keepdims=True)
    packed = pack_stats([sum_q, sum_c])
    stats3[...] = jnp.broadcast_to(packed[0:1], (PEERS, C))
    place_interior(pad, act)
    place_halo(pad, table, owners, positions, ids, me)
    windows_of(pad, cols)
    out = conv(cols, w2).reshape(SLOTS, VOX, C)
    for s in range(SLOTS):
        w = slot_weight(active, s)
        block[s] = ((feat[s].astype(f32) + out[s]) * w).astype(bf16)
        act[s] = jnp.where(active[0, s] > 0, gout[s].astype(f32), 0.0)
    weight_grad(cols, act[...].astype(bf16).reshape(SLOTS * VOX, C), grad_w)


def third_kernel(
    feat,
    active,
    owners,
    positions,
    ids,
    middle,
    gas,
    stats1,
    stats2,
    stats3,
    gain1,
    bias1,
    gain2,
    bias2,
    w1,
    cols_a,
    grad_w2,
    *rest,
):
    fields, rest = rest[:3], rest[3:]
    q1, share, table, pad, cols, act, scratch, grad_w1 = rest
    me = lax.axis_index("space")
    mean, inv, count = norm_stats(stats2)
    gain = gain2[...]
    bias = bias2[...]
    packed = total_of(stats3)
    mean_q = unpack_stat(packed, 0)[0:1] / count
    mean_c = unpack_stat(packed, 1)[0:1] / count

    def grad_of(x, g):
        hat = (x - mean) * inv
        n = hat * gain + bias
        sg = sigmoid(n)
        q = g * sg * (1.0 + n * (1.0 - sg)) * gain
        return (inv * (q - mean_q - hat * mean_c)).astype(bf16).astype(f32)

    fill_table(
        table,
        fields,
        scratch,
        me,
        lambda ref, e, s: grad_of(ref[e, 0, s].astype(f32), ref[e, 1, s].astype(f32)),
    )
    for s in range(SLOTS):
        act[s] = slot_weight(active, s) * grad_of(middle[s], gas[s])
    place_interior(pad, act)
    place_halo(pad, table, owners, positions, ids, me)
    windows_of(pad, cols)
    gaf = conv_back(cols, w1).reshape(SLOTS, VOX, C)
    mean1, inv1, _ = norm_stats(stats1)
    sum_q = jnp.zeros((1, C), f32)
    sum_c = jnp.zeros((1, C), f32)
    for s in range(SLOTS):
        hat = (feat[s].astype(f32) - mean1) * inv1
        n = hat * gain1[...] + bias1[...]
        sg = sigmoid(n)
        q = gaf[s] * slot_weight(active, s) * sg * (1.0 + n * (1.0 - sg)) * gain1[...]
        q1[s] = q
        sum_q = sum_q + jnp.sum(q, axis=0, keepdims=True)
        sum_c = sum_c + jnp.sum(q * hat, axis=0, keepdims=True)
    packed = pack_stats([sum_q, sum_c])
    weight_grad(cols_a, act[...].astype(bf16).reshape(SLOTS * VOX, C), grad_w1)
    for p in range(PEERS):
        core, chip = p % 2, p // 2
        share[core, chip, 0:SHARE] = grad_w1[SHARE * p : SHARE * (p + 1)]
        share[core, chip, 56 : 56 + SHARE] = grad_w2[SHARE * p : SHARE * (p + 1)]
        share[core, chip, SHARE : SHARE + 1] = packed[0:1]
        share[core, chip, SHARE + 1 : SHARE + 2] = packed[0:1]
        share[core, chip, 56 + SHARE : 112] = jnp.zeros((2, C), f32)


def last_kernel(feat, gout, active, stats1, q1, parts, gain1, grad_in, rows):
    total = parts[0]
    for n in range(1, 32):
        total = total + parts[n]
    mean1, inv1, count = norm_stats(stats1)
    packed = jnp.broadcast_to(total[SHARE : SHARE + 1], (8, C))
    mean_q = unpack_stat(packed, 0)[0:1] / count
    mean_c = unpack_stat(packed, 1)[0:1] / count
    for s in range(SLOTS):
        hat = (feat[s].astype(f32) - mean1) * inv1
        back = slot_weight(active, s) * inv1 * (q1[s] - mean_q - hat * mean_c)
        top = jnp.where(active[0, s] > 0, gout[s].astype(f32), 0.0)
        grad_in[s] = (top + back).astype(bf16)
    for n in range(8):
        rows[n] = total


vmem = pl.BlockSpec(memory_space=pltpu.VMEM)
smem = pl.BlockSpec(memory_space=pltpu.SMEM)


def call(kernel, specs, out_shape, scratch, args):
    return pl.pallas_call(
        kernel,
        in_specs=specs,
        out_specs=[vmem] * len(out_shape),
        out_shape=out_shape,
        scratch_shapes=scratch,
        compiler_params=pltpu.CompilerParams(vmem_limit_bytes=VMEM_BYTES),
    )(*args)


def shape(*dims, dtype=f32):
    return jax.ShapeDtypeStruct(dims, dtype)


def pairs_of(step, first):
    lower = [n for n in range(PEERS) if n // step % 2 == first]
    return [(n, (n + step) % PEERS) for n in lower] + [((n + step) % PEERS, n) for n in lower]


far_pairs = (pairs_of(4, 0), pairs_of(4, 1))
near_pairs = (pairs_of(1, 0), pairs_of(1, 1))


def exchange(fields):
    far = [lax.ppermute(fields, "space", pairs) for pairs in far_pairs]
    three = jnp.stack([fields, *far])
    return [three] + [lax.ppermute(three, "space", pairs) for pairs in near_pairs]


def spread(stats):
    return lax.all_to_all(stats, "space", 0, 0, tiled=True)


core_groups = [[2 * n, 2 * n + 1] for n in range(PEERS // 2)]
chip_groups = [list(range(core, PEERS, 2)) for core in range(2)]


def per_device(
    features,
    active,
    neighbor_owner,
    record_position,
    send_list,
    conv_first,
    conv_second,
    gain_first,
    bias_first,
    gain_second,
    bias_second,
    grad_output,
):
    feat = features[0]
    gout = grad_output[0]
    owners = neighbor_owner[0]
    positions = record_position[0]
    lists = send_list[0, 0]
    gain1, bias1 = gain_first.reshape(1, C), bias_first.reshape(1, C)
    gain2, bias2 = gain_second.reshape(1, C), bias_second.reshape(1, C)
    field = (SLOTS, VOX, C)
    wide = pltpu.VMEM(field, f32)
    scratch = pltpu.VMEM((2, *field), f32)
    table = pltpu.VMEM((LANES * PLANES, PLANE, C), f32)
    pad = pltpu.VMEM((SLOTS, 6, 6, 8, C), f32)
    cols_shape = (9, SLOTS, 6, PLANE, C)
    cols = pltpu.VMEM(cols_shape, bf16)

    stats1, both = call(
        start_kernel,
        [vmem, vmem, smem, vmem],
        [shape(PEERS, C), shape(2, *field, dtype=bf16)],
        [],
        (feat, gout, active, lists),
    )
    fields0 = exchange(both)
    stats1 = spread(stats1)
    ids = stats1[:, 3 : 4 * CAP : 4].astype(jnp.int32)

    middle, gas, cols_a, stats2, both = call(
        first_kernel,
        [vmem, vmem, smem, smem, smem, smem] + [vmem] * 8,
        [shape(*field), shape(*field), shape(*cols_shape, dtype=bf16), shape(PEERS, C)]
        + [shape(2, *field, dtype=bf16)],
        [table, pad, cols, wide, scratch],
        (feat, gout, active, owners, positions, ids, stats1, gain1, bias1)
        + (conv_first, conv_second, *fields0),
    )
    fields1 = exchange(both)
    stats2 = spread(stats2)

    block, stats3, grad_w2 = call(
        second_kernel,
        [vmem, vmem, smem, smem, smem, smem] + [vmem] * 9,
        [shape(*field, dtype=bf16), shape(PEERS, C), shape(27 * C, C)],
        [table, pad, cols, wide, scratch],
        (feat, gout, active, owners, positions, ids, middle, gas, stats2, gain2, bias2)
        + (conv_second, *fields1),
    )
    stats3 = spread(stats3)

    q1, share = call(
        third_kernel,
        [vmem, smem, smem, smem, smem] + [vmem] * 15,
        [shape(*field), shape(2, PEERS // 2, 112, C)],
        [table, pad, cols, wide, scratch, pltpu.VMEM((27 * C, C), f32)],
        (feat, active, owners, positions, ids, middle, gas, stats1, stats2, stats3)
        + (gain1, bias1, gain2, bias2, conv_first, cols_a, grad_w2, *fields1),
    )
    share = lax.all_to_all(share, "space", 0, 0, axis_index_groups=core_groups)
    share = share[0] + share[1]
    share = lax.all_to_all(share, "space", 0, 0, axis_index_groups=chip_groups)

    grad_in, rows = call(
        last_kernel,
        [vmem, vmem, smem, vmem, vmem, vmem, vmem],
        [shape(*field, dtype=bf16), shape(8, 112, C)],
        [],
        (feat, gout, active, stats1, q1, share, gain1),
    )
    rows = lax.all_to_all(rows, "scene", 0, 0)
    rows = jnp.sum(rows, axis=0).astype(bf16)
    return (block[None], grad_in[None], rows[:SHARE], rows[56 : 56 + SHARE])


def solution(mesh):
    return jax.shard_map(
        per_device,
        mesh=mesh,
        in_specs=(
            P("scene", "space", None, None),
            P("scene", "space"),
            P("scene", "space", None),
            P("scene", "space", None),
            P("scene", "space", None, None),
            P(),
            P(),
            P(),
            P(),
            P(),
            P(),
            P("scene", "space", None, None),
        ),
        out_specs=(
            P("scene", "space", None, None),
            P("scene", "space", None, None),
            P("space", None),
            P("space", None),
        ),
        check_vma=False,
    )
```

```python
import jax
import jax.numpy as jnp
from jax import lax
from jax.experimental import pallas as pl
from jax.experimental.pallas import tpu as pltpu
from jax.sharding import PartitionSpec as P

EDGE = 4
SLOTS = 4
VOX = 64
C = 128
CAP = 10
PEERS = 64
PLANE = 16
SHARE = 54
GROUP_COUNT = 64 * 4
EPS = 1e-05

directions = [
    (ordinal // 9 - 1, ordinal // 3 % 3 - 1, ordinal % 3 - 1)
    for ordinal in range(27)
    if ordinal != 13
]
PLANES = 24
LANES = 11
ZERO_PLANE = 3 * PLANES

f32 = jnp.float32
bf16 = jnp.bfloat16
VMEM_BYTES = 40 * 1024 * 1024


def group_total(row):
    lane = lax.broadcasted_iota(jnp.int32, row.shape, 1)
    row = row + jnp.where(lane % 2 == 0, pltpu.roll(row, C - 1, 1), pltpu.roll(row, 1, 1))
    return row + jnp.where(lane % 4 < 2, pltpu.roll(row, C - 2, 1), pltpu.roll(row, 2, 1))


def pack_stats(rows):
    rows = [jnp.broadcast_to(row, (8, C)) for row in rows]
    lane = lax.broadcasted_iota(jnp.int32, (8, C), 1)
    packed = jnp.zeros((8, C), f32)
    for n, row in enumerate(rows):
        packed = jnp.where(lane % 4 == n, group_total(row), packed)
    return packed


def unpack_stat(packed, n):
    lane = lax.broadcasted_iota(jnp.int32, packed.shape, 1)
    return group_total(jnp.where(lane % 4 == n, packed, 0.0))


def total_of(stats_ref, part=0):
    row = jnp.sum(stats_ref[:, C * part : C * (part + 1)], axis=0, keepdims=True)
    return jnp.broadcast_to(row, (8, C))


def norm_stats(stats_ref):
    packed = total_of(stats_ref)
    count = unpack_stat(packed, 2) * (GROUP_COUNT / 4)
    mean = unpack_stat(packed, 0) / count
    inv = lax.rsqrt(unpack_stat(packed, 1) / count - mean * mean + EPS)
    return mean[0:1], inv[0:1], count[0:1]


def sigmoid(n):
    return 1.0 / (1.0 + jnp.exp(-n))


def slot_weight(active_ref, s):
    return active_ref[0, s].astype(f32)


def planes_of(src, dst, start):
    for s in range(SLOTS):
        dst[start + 6 * s] = src[s, 0:16]
        dst[start + 6 * s + 1] = src[s, 48:64]
        for a in range(4):
            dst[start + 6 * s + 2, 4 * a : 4 * a + 4] = src[s, 16 * a : 16 * a + 4]
            dst[start + 6 * s + 3, 4 * a : 4 * a + 4] = src[s, 16 * a + 12 : 16 * a + 16]
        dst[start + 6 * s + 4] = src[s, pl.ds(0, 16, stride=4)]
        dst[start + 6 * s + 5] = src[s, pl.ds(3, 16, stride=4)]


def far_distance(device):
    return 4 - 8 * ((device >> 2) & 1)


def near_distance(device):
    return 1 - 2 * (device & 1)


def fill_table(table, fields, scratch, me, make):
    near = near_distance(me)
    turn = 0
    for ref, base in zip(fields, (0, near, -near)):
        far = far_distance((me + base) & (PEERS - 1))
        for entry, more in enumerate((0, far, -far)):
            start = (base + more + 5) * PLANES
            buffer = scratch.at[turn % 2]
            turn += 1
            for s in range(SLOTS):
                buffer[s] = make(ref, entry, s)
            planes_of(buffer, table, start)
    table[ZERO_PLANE] = jnp.zeros((PLANE, C), f32)


def place_halo(pad, table, own_ref, pos_ref, ids_ref, me):
    def one_slot(s, carry):
        for n, (d0, d1, d2) in enumerate(directions):
            owner = own_ref[s, n]
            plane = jnp.clip(ids_ref[jnp.maximum(owner, 0), pos_ref[s, n]], 0, PLANES - 1)
            index = jnp.where(owner >= 0, (owner - me + 5) * PLANES + plane, ZERO_PLANE)
            cells = [(5 if d > 0 else 0, 0 if d > 0 else 3) for d in (d0, d1, d2)]
            (a_to, _), (b_to, b_from), (c_to, c_from) = cells

            def row(r, count=1):
                return table[index, r : r + count]

            if d0 != 0:
                if d1 == 0 and d2 == 0:
                    for b in range(4):
                        pad[s, a_to, 1 + b, 1:5] = row(4 * b, 4)
                elif d2 == 0:
                    pad[s, a_to, b_to, 1:5] = row(4 * b_from, 4)
                elif d1 == 0:
                    for b in range(4):
                        pad[s, a_to, 1 + b, c_to : c_to + 1] = row(4 * b + c_from)
                else:
                    pad[s, a_to, b_to, c_to : c_to + 1] = row(4 * b_from + c_from)
            elif d1 != 0:
                for a in range(4):
                    if d2 == 0:
                        pad[s, 1 + a, b_to, 1:5] = row(4 * a, 4)
                    else:
                        pad[s, 1 + a, b_to, c_to : c_to + 1] = row(4 * a + c_from)
            else:
                for a in range(4):
                    for b in range(4):
                        pad[s, 1 + a, 1 + b, c_to : c_to + 1] = row(4 * a + b)
        return carry

    lax.fori_loop(0, SLOTS, one_slot, 0)


def place_interior(pad, field):
    for s in range(SLOTS):
        for a in range(4):
            for b in range(4):
                pad[s, 1 + a, 1 + b, 1:5] = field[s, 16 * a + 4 * b : 16 * a + 4 * b + 4]


def windows_of(pad, cols):
    def one_layer(t, carry):
        s, a = t // 6, t % 6
        sub = lax.broadcasted_iota(jnp.int32, (8, C), 0)
        layer = [pad[s, a, b] for b in range(6)]
        for k2 in range(3):
            low = [pltpu.roll(v, (8 - k2) % 8, 0) if k2 else v for v in layer]
            high = [pltpu.roll(v, 4 - k2, 0) for v in layer]
            pair = [jnp.where(sub < 4, low[b], high[b + 1]) for b in range(5)]
            for k1 in range(3):
                tile = jnp.concatenate([pair[k1], pair[k1 + 2]], axis=0)
                cols[3 * k1 + k2, s, a] = tile.astype(bf16)
        return carry

    lax.fori_loop(0, SLOTS * 6, one_layer, 0)


def window(cols, k0, k1, k2):
    return cols[3 * k1 + k2, :, k0 : k0 + 4].reshape(SLOTS * VOX, C)


def conv(cols, weight):
    total = jnp.zeros((SLOTS * VOX, C), f32)
    for k0 in range(3):
        left = jnp.concatenate([window(cols, k0, j // 3, j % 3) for j in range(9)], axis=1)
        right = weight[9 * k0 : 9 * k0 + 9].reshape(9 * C, C)
        total = total + jnp.dot(left, right, preferred_element_type=f32)
    return total


def conv_back(cols, weight):
    total = jnp.zeros((SLOTS * VOX, C), f32)
    for k0 in range(3):
        left = jnp.concatenate(
            [window(cols, 2 - k0, 2 - j // 3, 2 - j % 3) for j in range(9)], axis=1
        )
        right = jnp.concatenate([weight[9 * k0 + j] for j in range(9)], axis=1)
        total = total + lax.dot_general(
            left, right, (((1,), (1,)), ((), ())), preferred_element_type=f32
        )
    return total


def weight_grad(cols, grad, centre, out):
    right = jnp.concatenate([grad, jnp.ones((SLOTS * VOX, C), bf16)], axis=1)
    for k0 in range(3):
        left = jnp.concatenate([window(cols, k0, j // 3, j % 3) for j in range(9)], axis=1)
        both = lax.dot_general(
            left, right, (((0,), (0,)), ((), ())), preferred_element_type=f32
        )
        out[9 * C * k0 : 9 * C * (k0 + 1)] = both[:, :C] - both[:, C:] * centre


def window_sums(cols):
    ones = jnp.ones((8, SLOTS * VOX), bf16)
    rows = []
    for k0 in range(3):
        left = jnp.concatenate([window(cols, k0, j // 3, j % 3) for j in range(9)], axis=1)
        total = jnp.dot(ones, left, preferred_element_type=f32)
        rows += [total[0:1, C * j : C * (j + 1)] for j in range(9)]
    return rows


def store_shares(rows, out, part):
    lane = lax.broadcasted_iota(jnp.int32, (1, C), 1)
    for p in range(PEERS):
        k, skip = divmod(SHARE * p, C)
        line = rows[k] if skip == 0 else pltpu.roll(rows[k], C - skip, 1)
        if skip + SHARE > C:
            line = jnp.where(lane < C - skip, line, pltpu.roll(rows[k + 1], C - skip, 1))
        line = jnp.where(lane < SHARE, line, 0.0)
        out[p : p + 1, C * part : C * (part + 1)] = line


def grad_centre(stats1, count):
    return total_of(stats1, 1)[0:1] / (count / 4)


def middle_centre(stats2, stats3, count, mean, inv, mean_q, mean_c):
    voxels = count / 4
    sum_hat = (total_of(stats2, 1)[0:1] - voxels * mean) * inv
    sum_q = total_of(stats3, 1)[0:1]
    return inv * (sum_q - voxels * mean_q - sum_hat * mean_c) / voxels


def outer(shares, centre):
    first = lax.broadcasted_iota(jnp.int32, (8, C), 0) == 0
    left = jnp.where(first, jnp.broadcast_to(shares, (8, C)), 0.0)
    return lax.dot_general(
        left,
        jnp.broadcast_to(centre, (8, C)),
        (((0,), (0,)), ((), ())),
        precision=lax.Precision.HIGHEST,
        preferred_element_type=f32,
    )


def start_kernel(feat, gout, active, send_list, stats, both):
    both[0] = feat[...]
    both[1] = gout[...]
    total = jnp.zeros((1, C), f32)
    squares = jnp.zeros((1, C), f32)
    grads = jnp.zeros((1, C), f32)
    slots = 0.0
    for s in range(SLOTS):
        w = slot_weight(active, s)
        x = feat[s].astype(f32)
        grads = grads + w * jnp.sum(gout[s].astype(f32), axis=0, keepdims=True)
        total = total + w * jnp.sum(x, axis=0, keepdims=True)
        squares = squares + w * jnp.sum(x * x, axis=0, keepdims=True)
        slots = slots + w
    packed = pack_stats([total, squares, jnp.full((1, C), slots, f32)])
    record = lax.broadcasted_iota(jnp.int32, (CAP, C), 0)
    lane = lax.broadcasted_iota(jnp.int32, (CAP, C), 1)
    select = jnp.where(lane == 4 * record + 3, 1.0, 0.0).astype(bf16)
    ids = jnp.dot(send_list[...].astype(bf16), select, preferred_element_type=f32)
    stats[:, 0:C] = ids + packed[0:1]
    stats[:, C : 2 * C] = jnp.broadcast_to(grads, (PEERS, C))


def first_kernel(
    feat, gout, active, owners, positions, ids, stats1, gain1, bias1, w1, w2, *rest
):
    fields, rest = rest[:3], rest[3:]
    middle, gas, cols_a, stats2, both, table, pad, cols_g, act, scratch = rest
    me = lax.axis_index("space")
    mean, inv, _ = norm_stats(stats1)

    def act_of(x):
        n = (x - mean) * inv * gain1[...] + bias1[...]
        return n * sigmoid(n)

    fill_table(table, fields, scratch, me, lambda ref, e, s: act_of(ref[e, 0, s].astype(f32)))
    for s in range(SLOTS):
        act[s] = slot_weight(active, s) * act_of(feat[s].astype(f32))
    place_interior(pad, act)
    place_halo(pad, table, owners, positions, ids, me)
    windows_of(pad, cols_a)
    middle[...] = conv(cols_a, w1).reshape(SLOTS, VOX, C)
    fill_table(table, fields, scratch, me, lambda ref, e, s: ref[e, 1, s].astype(f32))
    for s in range(SLOTS):
        act[s] = jnp.where(active[0, s] > 0, gout[s].astype(f32), 0.0)
    place_interior(pad, act)
    place_halo(pad, table, owners, positions, ids, me)
    windows_of(pad, cols_g)
    gas[...] = conv_back(cols_g, w2).reshape(SLOTS, VOX, C)
    both[0] = middle[...].astype(bf16)
    both[1] = gas[...].astype(bf16)
    total = jnp.zeros((1, C), f32)
    squares = jnp.zeros((1, C), f32)
    slots = 0.0
    for s in range(SLOTS):
        w = slot_weight(active, s)
        x = middle[s]
        total = total + w * jnp.sum(x, axis=0, keepdims=True)
        squares = squares + w * jnp.sum(x * x, axis=0, keepdims=True)
        slots = slots + w
    packed = pack_stats([total, squares, jnp.full((1, C), slots, f32)])
    stats2[:, 0:C] = jnp.broadcast_to(packed[0:1], (PEERS, C))
    stats2[:, C : 2 * C] = jnp.broadcast_to(total, (PEERS, C))
    store_shares(window_sums(cols_a), stats2, 2)


def second_kernel(
    feat,
    gout,
    active,
    owners,
    positions,
    ids,
    middle,
    gas,
    stats1,
    stats2,
    gain2,
    bias2,
    w2,
    *rest,
):
    fields, rest = rest[:3], rest[3:]
    block, stats3, grad_w, table, pad, cols, act, scratch = rest
    me = lax.axis_index("space")
    mean, inv, count = norm_stats(stats2)
    gain = gain2[...]
    bias = bias2[...]

    def act_of(ref, e, s):
        n = (ref[e, 0, s].astype(f32) - mean) * inv * gain + bias
        return n * sigmoid(n)

    fill_table(table, fields, scratch, me, act_of)
    sum_q = jnp.zeros((1, C), f32)
    sum_c = jnp.zeros((1, C), f32)
    for s in range(SLOTS):
        w = slot_weight(active, s)
        hat = (middle[s] - mean) * inv
        n = hat * gain + bias
        sg = sigmoid(n)
        act[s] = w * (n * sg)
        q = gas[s] * w * sg * (1.0 + n * (1.0 - sg)) * gain
        sum_q = sum_q + jnp.sum(q, axis=0, keepdims=True)
        sum_c = sum_c + jnp.sum(q * hat, axis=0, keepdims=True)
    packed = pack_stats([sum_q, sum_c])
    stats3[:, 0:C] = jnp.broadcast_to(packed[0:1], (PEERS, C))
    stats3[:, C : 2 * C] = jnp.broadcast_to(sum_q, (PEERS, C))
    place_interior(pad, act)
    place_halo(pad, table, owners, positions, ids, me)
    windows_of(pad, cols)
    store_shares(window_sums(cols), stats3, 2)
    out = conv(cols, w2).reshape(SLOTS, VOX, C)
    for s in range(SLOTS):
        w = slot_weight(active, s)
        block[s] = ((feat[s].astype(f32) + out[s]) * w).astype(bf16)
        act[s] = jnp.where(active[0, s] > 0, gout[s].astype(f32), 0.0)
    centre = grad_centre(stats1, count)
    weight_grad(cols, act[...].astype(bf16).reshape(SLOTS * VOX, C), centre, grad_w)


def third_kernel(
    feat,
    active,
    owners,
    positions,
    ids,
    middle,
    gas,
    stats1,
    stats2,
    stats3,
    gain1,
    bias1,
    gain2,
    bias2,
    w1,
    cols_a,
    grad_w2,
    *rest,
):
    fields, rest = rest[:3], rest[3:]
    q1, share, table, pad, cols, act, scratch, grad_w1 = rest
    me = lax.axis_index("space")
    mean, inv, count = norm_stats(stats2)
    gain = gain2[...]
    bias = bias2[...]
    packed = total_of(stats3)
    mean_q = unpack_stat(packed, 0)[0:1] / count
    mean_c = unpack_stat(packed, 1)[0:1] / count

    def grad_of(x, g):
        hat = (x - mean) * inv
        n = hat * gain + bias
        sg = sigmoid(n)
        q = g * sg * (1.0 + n * (1.0 - sg)) * gain
        return (inv * (q - mean_q - hat * mean_c)).astype(bf16).astype(f32)

    fill_table(
        table,
        fields,
        scratch,
        me,
        lambda ref, e, s: grad_of(ref[e, 0, s].astype(f32), ref[e, 1, s].astype(f32)),
    )
    for s in range(SLOTS):
        act[s] = slot_weight(active, s) * grad_of(middle[s], gas[s])
    place_interior(pad, act)
    place_halo(pad, table, owners, positions, ids, me)
    windows_of(pad, cols)
    gaf = conv_back(cols, w1).reshape(SLOTS, VOX, C)
    mean1, inv1, _ = norm_stats(stats1)
    sum_q = jnp.zeros((1, C), f32)
    sum_c = jnp.zeros((1, C), f32)
    for s in range(SLOTS):
        hat = (feat[s].astype(f32) - mean1) * inv1
        n = hat * gain1[...] + bias1[...]
        sg = sigmoid(n)
        q = gaf[s] * slot_weight(active, s) * sg * (1.0 + n * (1.0 - sg)) * gain1[...]
        q1[s] = q
        sum_q = sum_q + jnp.sum(q, axis=0, keepdims=True)
        sum_c = sum_c + jnp.sum(q * hat, axis=0, keepdims=True)
    packed = pack_stats([sum_q, sum_c])
    centre = middle_centre(stats2, stats3, count, mean, inv, mean_q, mean_c)
    weight_grad(cols_a, act[...].astype(bf16).reshape(SLOTS * VOX, C), centre, grad_w1)
    for p in range(PEERS):
        core, chip = p % 2, p // 2
        share[core, chip, 0:SHARE] = grad_w1[SHARE * p : SHARE * (p + 1)]
        share[core, chip, 56 : 56 + SHARE] = grad_w2[SHARE * p : SHARE * (p + 1)]
        share[core, chip, SHARE : SHARE + 1] = packed[0:1]
        share[core, chip, SHARE + 1 : SHARE + 2] = packed[0:1]
        share[core, chip, 56 + SHARE : 112] = jnp.zeros((2, C), f32)


def pair_kernel(pair, out):
    for n in range(PEERS // 2):
        total = pair[0, n] + pair[1, n]
        row = total[SHARE : SHARE + 1]
        high = row.astype(bf16)
        left = row - high.astype(f32)
        middle = left.astype(bf16)
        low = (left - middle.astype(f32)).astype(bf16)
        at = lax.broadcasted_iota(jnp.int32, (112, C), 0)
        total = jnp.where(at == SHARE, high.astype(f32), total)
        total = jnp.where(at == SHARE + 1, middle.astype(f32), total)
        total = jnp.where(at == 56 + SHARE, low.astype(f32), total)
        out[n] = total.astype(bf16)


def last_kernel(
    feat, gout, active, stats1, stats2, stats3, q1, parts, gain1, grad_in, rows
):
    total = parts[0].astype(f32)
    for n in range(1, PEERS // 2):
        total = total + parts[n].astype(f32)
    mean1, inv1, count = norm_stats(stats1)
    packed = total[SHARE : SHARE + 1] + total[SHARE + 1 : SHARE + 2] + total[110:111]
    packed = jnp.broadcast_to(packed, (8, C))
    mean_q = unpack_stat(packed, 0)[0:1] / count
    mean_c = unpack_stat(packed, 1)[0:1] / count
    for s in range(SLOTS):
        hat = (feat[s].astype(f32) - mean1) * inv1
        back = slot_weight(active, s) * inv1 * (q1[s] - mean_q - hat * mean_c)
        top = jnp.where(active[0, s] > 0, gout[s].astype(f32), 0.0)
        grad_in[s] = (top + back).astype(bf16)
    mean, inv, _ = norm_stats(stats2)
    packed = total_of(stats3)
    mean_q = unpack_stat(packed, 0)[0:1] / count
    mean_c = unpack_stat(packed, 1)[0:1] / count
    centre1 = middle_centre(stats2, stats3, count, mean, inv, mean_q, mean_c)
    centre2 = grad_centre(stats1, count)
    first = total[0:56] + outer(total_of(stats2, 2)[0:1], centre1)[0:56]
    second = total[56:112] + outer(total_of(stats3, 2)[0:1], centre2)[0:56]
    for n in range(8):
        rows[n, 0:56] = first
        rows[n, 56:112] = second


vmem = pl.BlockSpec(memory_space=pltpu.VMEM)
smem = pl.BlockSpec(memory_space=pltpu.SMEM)


def call(kernel, specs, out_shape, scratch, args):
    return pl.pallas_call(
        kernel,
        in_specs=specs,
        out_specs=[vmem] * len(out_shape),
        out_shape=out_shape,
        scratch_shapes=scratch,
        compiler_params=pltpu.CompilerParams(vmem_limit_bytes=VMEM_BYTES),
    )(*args)


def shape(*dims, dtype=f32):
    return jax.ShapeDtypeStruct(dims, dtype)


def pairs_of(step, first):
    lower = [n for n in range(PEERS) if n // step % 2 == first]
    return [(n, (n + step) % PEERS) for n in lower] + [((n + step) % PEERS, n) for n in lower]


far_pairs = (pairs_of(4, 0), pairs_of(4, 1))
near_pairs = (pairs_of(1, 0), pairs_of(1, 1))


def exchange(fields):
    far = [lax.ppermute(fields, "space", pairs) for pairs in far_pairs]
    three = jnp.stack([fields, *far])
    return [three] + [lax.ppermute(three, "space", pairs) for pairs in near_pairs]


def spread(stats):
    return lax.all_to_all(stats, "space", 0, 0, tiled=True)


core_groups = [[2 * n, 2 * n + 1] for n in range(PEERS // 2)]
chip_groups = [list(range(core, PEERS, 2)) for core in range(2)]


def per_device(
    features,
    active,
    neighbor_owner,
    record_position,
    send_list,
    conv_first,
    conv_second,
    gain_first,
    bias_first,
    gain_second,
    bias_second,
    grad_output,
):
    feat = features[0]
    gout = grad_output[0]
    owners = neighbor_owner[0]
    positions = record_position[0]
    lists = send_list[0, 0]
    gain1, bias1 = gain_first.reshape(1, C), bias_first.reshape(1, C)
    gain2, bias2 = gain_second.reshape(1, C), bias_second.reshape(1, C)
    field = (SLOTS, VOX, C)
    wide = pltpu.VMEM(field, f32)
    scratch = pltpu.VMEM((2, *field), f32)
    table = pltpu.VMEM((LANES * PLANES, PLANE, C), f32)
    pad = pltpu.VMEM((SLOTS, 6, 6, 8, C), f32)
    cols_shape = (9, SLOTS, 6, PLANE, C)
    cols = pltpu.VMEM(cols_shape, bf16)

    stats1, both = call(
        start_kernel,
        [vmem, vmem, smem, vmem],
        [shape(PEERS, 2 * C), shape(2, *field, dtype=bf16)],
        [],
        (feat, gout, active, lists),
    )
    fields0 = exchange(both)
    stats1 = spread(stats1)
    ids = stats1[:, 3 : 4 * CAP : 4].astype(jnp.int32)

    middle, gas, cols_a, stats2, both = call(
        first_kernel,
        [vmem, vmem, smem, smem, smem, smem] + [vmem] * 8,
        [shape(*field), shape(*field), shape(*cols_shape, dtype=bf16), shape(PEERS, 3 * C)]
        + [shape(2, *field, dtype=bf16)],
        [table, pad, cols, wide, scratch],
        (feat, gout, active, owners, positions, ids, stats1, gain1, bias1)
        + (conv_first, conv_second, *fields0),
    )
    fields1 = exchange(both)
    stats2 = spread(stats2)

    block, stats3, grad_w2 = call(
        second_kernel,
        [vmem, vmem, smem, smem, smem, smem] + [vmem] * 10,
        [shape(*field, dtype=bf16), shape(PEERS, 3 * C), shape(27 * C, C)],
        [table, pad, cols, wide, scratch],
        (feat, gout, active, owners, positions, ids, middle, gas, stats1, stats2, gain2, bias2)
        + (conv_second, *fields1),
    )
    stats3 = spread(stats3)

    q1, share = call(
        third_kernel,
        [vmem, smem, smem, smem, smem] + [vmem] * 15,
        [shape(*field), shape(2, PEERS // 2, 112, C)],
        [table, pad, cols, wide, scratch, pltpu.VMEM((27 * C, C), f32)],
        (feat, active, owners, positions, ids, middle, gas, stats1, stats2, stats3)
        + (gain1, bias1, gain2, bias2, conv_first, cols_a, grad_w2, *fields1),
    )
    share = lax.all_to_all(share, "space", 0, 0, axis_index_groups=core_groups)
    (share,) = call(
        pair_kernel, [vmem], [shape(PEERS // 2, 112, C, dtype=bf16)], [], (share,)
    )
    share = lax.all_to_all(share, "space", 0, 0, axis_index_groups=chip_groups)

    grad_in, rows = call(
        last_kernel,
        [vmem, vmem, smem] + [vmem] * 6,
        [shape(*field, dtype=bf16), shape(8, 112, C)],
        [],
        (feat, gout, active, stats1, stats2, stats3, q1, share, gain1),
    )
    rows = lax.all_to_all(rows, "scene", 0, 0)
    rows = jnp.sum(rows, axis=0).astype(bf16)
    return (block[None], grad_in[None], rows[:SHARE], rows[56 : 56 + SHARE])


def solution(mesh):
    return jax.shard_map(
        per_device,
        mesh=mesh,
        in_specs=(
            P("scene", "space", None, None),
            P("scene", "space"),
            P("scene", "space", None),
            P("scene", "space", None),
            P("scene", "space", None, None),
            P(),
            P(),
            P(),
            P(),
            P(),
            P(),
            P("scene", "space", None, None),
        ),
        out_specs=(
            P("scene", "space", None, None),
            P("scene", "space", None, None),
            P("space", None),
            P("space", None),
        ),
        check_vma=False,
    )
```

```python
import jax
import jax.numpy as jnp
from jax import lax
from jax.experimental import pallas as pl
from jax.experimental.pallas import tpu as pltpu
from jax.sharding import PartitionSpec as P

EDGE = 4
SLOTS = 4
VOX = 64
C = 128
CAP = 10
PEERS = 64
PLANE = 16
SHARE = 54
GROUP_COUNT = 64 * 4
EPS = 1e-05

directions = [
    (ordinal // 9 - 1, ordinal // 3 % 3 - 1, ordinal % 3 - 1)
    for ordinal in range(27)
    if ordinal != 13
]
PLANES = 24
LANES = 11
ZERO_PLANE = 3 * PLANES

f32 = jnp.float32
bf16 = jnp.bfloat16
VMEM_BYTES = 40 * 1024 * 1024


def group_total(row):
    lane = lax.broadcasted_iota(jnp.int32, row.shape, 1)
    row = row + jnp.where(lane % 2 == 0, pltpu.roll(row, C - 1, 1), pltpu.roll(row, 1, 1))
    return row + jnp.where(lane % 4 < 2, pltpu.roll(row, C - 2, 1), pltpu.roll(row, 2, 1))


def pack_stats(rows):
    rows = [jnp.broadcast_to(row, (8, C)) for row in rows]
    lane = lax.broadcasted_iota(jnp.int32, (8, C), 1)
    packed = jnp.zeros((8, C), f32)
    for n, row in enumerate(rows):
        packed = jnp.where(lane % 4 == n, group_total(row), packed)
    return packed


def unpack_stat(packed, n):
    lane = lax.broadcasted_iota(jnp.int32, packed.shape, 1)
    return group_total(jnp.where(lane % 4 == n, packed, 0.0))


def total_of(stats_ref, part=0):
    row = jnp.sum(stats_ref[:, C * part : C * (part + 1)], axis=0, keepdims=True)
    return jnp.broadcast_to(row, (8, C))


def norm_stats(stats_ref):
    packed = total_of(stats_ref)
    count = unpack_stat(packed, 2) * (GROUP_COUNT / 4)
    mean = unpack_stat(packed, 0) / count
    inv = lax.rsqrt(unpack_stat(packed, 1) / count - mean * mean + EPS)
    return mean[0:1], inv[0:1], count[0:1]


def sigmoid(n):
    return 1.0 / (1.0 + jnp.exp(-n))


def slot_weight(active_ref, s):
    return active_ref[0, s].astype(f32)


def planes_of(src, dst, start):
    for s in range(SLOTS):
        dst[start + 6 * s] = src[s, 0:16]
        dst[start + 6 * s + 1] = src[s, 48:64]
        for a in range(4):
            dst[start + 6 * s + 2, 4 * a : 4 * a + 4] = src[s, 16 * a : 16 * a + 4]
            dst[start + 6 * s + 3, 4 * a : 4 * a + 4] = src[s, 16 * a + 12 : 16 * a + 16]
        dst[start + 6 * s + 4] = src[s, pl.ds(0, 16, stride=4)]
        dst[start + 6 * s + 5] = src[s, pl.ds(3, 16, stride=4)]


def far_distance(device):
    return 4 - 8 * ((device >> 2) & 1)


def near_distance(device):
    return 1 - 2 * (device & 1)


def fill_table(table, fields, scratch, me, make):
    near = near_distance(me)
    turn = 0
    for ref, base in zip(fields, (0, near, -near)):
        far = far_distance((me + base) & (PEERS - 1))
        for entry, more in enumerate((0, far, -far)):
            start = (base + more + 5) * PLANES
            buffer = scratch.at[turn % 2]
            turn += 1
            for s in range(SLOTS):
                buffer[s] = make(ref, entry, s)
            planes_of(buffer, table, start)
    table[ZERO_PLANE] = jnp.zeros((PLANE, C), f32)


def find_planes(owners, positions, ids, index, me):
    def one_slot(s, carry):
        for n in range(26):
            owner = owners[s, n]
            plane = ids[jnp.maximum(owner, 0), 4 * positions[s, n] + 3]
            plane = jnp.clip(plane, 0, PLANES - 1)
            index[s, n] = jnp.where(
                owner >= 0, (owner - me + 5) * PLANES + plane, ZERO_PLANE
            )
        return carry

    lax.fori_loop(0, SLOTS, one_slot, 0)


def fetch(sources, targets, sems):
    copies = [
        pltpu.make_async_copy(source, target, sems.at[n])
        for n, (source, target) in enumerate(zip(sources, targets))
    ]
    for copy in copies:
        copy.start()
    return copies


def place_halo(pad, table, index_ref):
    def one_slot(s, carry):
        for n, (d0, d1, d2) in enumerate(directions):
            index = index_ref[s, n]
            cells = [(5 if d > 0 else 0, 0 if d > 0 else 3) for d in (d0, d1, d2)]
            (a_to, _), (b_to, b_from), (c_to, c_from) = cells

            def row(r, count=1):
                return table[index, r : r + count]

            if d0 != 0:
                if d1 == 0 and d2 == 0:
                    for b in range(4):
                        pad[s, a_to, 1 + b, 1:5] = row(4 * b, 4)
                elif d2 == 0:
                    pad[s, a_to, b_to, 1:5] = row(4 * b_from, 4)
                elif d1 == 0:
                    for b in range(4):
                        pad[s, a_to, 1 + b, c_to : c_to + 1] = row(4 * b + c_from)
                else:
                    pad[s, a_to, b_to, c_to : c_to + 1] = row(4 * b_from + c_from)
            elif d1 != 0:
                for a in range(4):
                    if d2 == 0:
                        pad[s, 1 + a, b_to, 1:5] = row(4 * a, 4)
                    else:
                        pad[s, 1 + a, b_to, c_to : c_to + 1] = row(4 * a + c_from)
            else:
                for a in range(4):
                    for b in range(4):
                        pad[s, 1 + a, 1 + b, c_to : c_to + 1] = row(4 * a + b)
        return carry

    lax.fori_loop(0, SLOTS, one_slot, 0)


def place_interior(pad, field):
    for s in range(SLOTS):
        for a in range(4):
            for b in range(4):
                pad[s, 1 + a, 1 + b, 1:5] = field[s, 16 * a + 4 * b : 16 * a + 4 * b + 4]


def windows_of(pad, cols):
    def one_layer(t, carry):
        s, a = t // 6, t % 6
        sub = lax.broadcasted_iota(jnp.int32, (8, C), 0)
        layer = [pad[s, a, b] for b in range(6)]
        for k2 in range(3):
            low = [pltpu.roll(v, (8 - k2) % 8, 0) if k2 else v for v in layer]
            high = [pltpu.roll(v, 4 - k2, 0) for v in layer]
            pair = [jnp.where(sub < 4, low[b], high[b + 1]) for b in range(5)]
            for k1 in range(3):
                tile = jnp.concatenate([pair[k1], pair[k1 + 2]], axis=0)
                cols[3 * k1 + k2, s, a] = tile.astype(bf16)
        return carry

    lax.fori_loop(0, SLOTS * 6, one_layer, 0)


def window(cols, k0, k1, k2):
    return cols[3 * k1 + k2, :, k0 : k0 + 4].reshape(SLOTS * VOX, C)


def conv(cols, weight):
    total = jnp.zeros((SLOTS * VOX, C), f32)
    for k0 in range(3):
        left = jnp.concatenate([window(cols, k0, j // 3, j % 3) for j in range(9)], axis=1)
        right = weight[9 * k0 : 9 * k0 + 9].reshape(9 * C, C)
        total = total + jnp.dot(left, right, preferred_element_type=f32)
    return total


def conv_back(cols, weight):
    total = jnp.zeros((SLOTS * VOX, C), f32)
    for k0 in range(3):
        left = jnp.concatenate(
            [window(cols, 2 - k0, 2 - j // 3, 2 - j % 3) for j in range(9)], axis=1
        )
        right = jnp.concatenate([weight[9 * k0 + j] for j in range(9)], axis=1)
        total = total + lax.dot_general(
            left, right, (((1,), (1,)), ((), ())), preferred_element_type=f32
        )
    return total


def weight_grad(cols, grad, centre, out):
    right = jnp.concatenate([grad, jnp.ones((SLOTS * VOX, C), bf16)], axis=1)
    for k0 in range(3):
        left = jnp.concatenate([window(cols, k0, j // 3, j % 3) for j in range(9)], axis=1)
        both = lax.dot_general(
            left, right, (((0,), (0,)), ((), ())), preferred_element_type=f32
        )
        out[9 * C * k0 : 9 * C * (k0 + 1)] = both[:, :C] - both[:, C:] * centre


def window_sums(cols):
    ones = jnp.ones((8, SLOTS * VOX), bf16)
    rows = []
    for k0 in range(3):
        left = jnp.concatenate([window(cols, k0, j // 3, j % 3) for j in range(9)], axis=1)
        total = jnp.dot(ones, left, preferred_element_type=f32)
        rows += [total[0:1, C * j : C * (j + 1)] for j in range(9)]
    return rows


def store_shares(rows, out, part):
    lane = lax.broadcasted_iota(jnp.int32, (1, C), 1)
    for p in range(PEERS):
        k, skip = divmod(SHARE * p, C)
        line = rows[k] if skip == 0 else pltpu.roll(rows[k], C - skip, 1)
        if skip + SHARE > C:
            line = jnp.where(lane < C - skip, line, pltpu.roll(rows[k + 1], C - skip, 1))
        line = jnp.where(lane < SHARE, line, 0.0)
        out[p : p + 1, C * part : C * (part + 1)] = line


def grad_centre(stats1, count):
    return total_of(stats1, 1)[0:1] / (count / 4)


def middle_centre(stats2, stats3, count, mean, inv, mean_q, mean_c):
    voxels = count / 4
    sum_hat = (total_of(stats2, 1)[0:1] - voxels * mean) * inv
    sum_q = total_of(stats3, 1)[0:1]
    return inv * (sum_q - voxels * mean_q - sum_hat * mean_c) / voxels


def outer(shares, centre):
    first = lax.broadcasted_iota(jnp.int32, (8, C), 0) == 0
    left = jnp.where(first, jnp.broadcast_to(shares, (8, C)), 0.0)
    return lax.dot_general(
        left,
        jnp.broadcast_to(centre, (8, C)),
        (((0,), (0,)), ((), ())),
        precision=lax.Precision.HIGHEST,
        preferred_element_type=f32,
    )


def start_kernel(feat_in, gout_in, active_in, list_in, stats, both, active, send_list, sems):
    feat, gout = both.at[0], both.at[1]
    copies = fetch(
        (active_in, list_in, feat_in, gout_in), (active, send_list, feat, gout), sems
    )
    for copy in copies:
        copy.wait()
    total = jnp.zeros((1, C), f32)
    squares = jnp.zeros((1, C), f32)
    grads = jnp.zeros((1, C), f32)
    slots = 0.0
    for s in range(SLOTS):
        w = slot_weight(active, s)
        x = feat[s].astype(f32)
        grads = grads + w * jnp.sum(gout[s].astype(f32), axis=0, keepdims=True)
        total = total + w * jnp.sum(x, axis=0, keepdims=True)
        squares = squares + w * jnp.sum(x * x, axis=0, keepdims=True)
        slots = slots + w
    packed = pack_stats([total, squares, jnp.full((1, C), slots, f32)])
    record = lax.broadcasted_iota(jnp.int32, (CAP, C), 0)
    lane = lax.broadcasted_iota(jnp.int32, (CAP, C), 1)
    select = jnp.where(lane == 4 * record + 3, 1.0, 0.0).astype(bf16)
    ids = jnp.dot(send_list[...].astype(bf16), select, preferred_element_type=f32)
    stats[:, 0:C] = ids + packed[0:1]
    stats[:, C : 2 * C] = jnp.broadcast_to(grads, (PEERS, C))


def first_kernel(
    active_in, own_in, pos_in, gain_in, bias_in, w1_in, w2_in, stats1, *rest
):
    fields, rest = rest[:3], rest[3:]
    middle, gas, cols_a, stats2, both, index = rest[:6]
    table, pad, cols_g, act, scratch, ids_v = rest[6:12]
    active, owners, positions, ids, gain1, bias1, w1, w2, sems = rest[12:]
    me = lax.axis_index("space")
    copies = fetch(
        (gain_in, bias_in, active_in, own_in, pos_in, w1_in, w2_in),
        (gain1, bias1, active, owners, positions, w1, w2),
        sems,
    )
    ids_v[...] = stats1[:, 0:C].astype(jnp.int32)
    ids_copy = pltpu.make_async_copy(ids_v, ids, sems.at[7])
    ids_copy.start()
    feat, gout = fields[0].at[0, 0], fields[0].at[0, 1]
    mean, inv, _ = norm_stats(stats1)
    copies[0].wait()
    copies[1].wait()

    def act_of(x):
        n = (x - mean) * inv * gain1[...] + bias1[...]
        return n * sigmoid(n)

    fill_table(table, fields, scratch, me, lambda ref, e, s: act_of(ref[e, 0, s].astype(f32)))
    for copy in copies[2:5]:
        copy.wait()
    ids_copy.wait()
    find_planes(owners, positions, ids, index, me)
    for s in range(SLOTS):
        act[s] = slot_weight(active, s) * act_of(feat[s].astype(f32))
    place_interior(pad, act)
    place_halo(pad, table, index)
    windows_of(pad, cols_a)
    copies[5].wait()
    middle[...] = conv(cols_a, w1).reshape(SLOTS, VOX, C)
    fill_table(table, fields, scratch, me, lambda ref, e, s: ref[e, 1, s].astype(f32))
    for s in range(SLOTS):
        act[s] = jnp.where(active[0, s] > 0, gout[s].astype(f32), 0.0)
    place_interior(pad, act)
    place_halo(pad, table, index)
    windows_of(pad, cols_g)
    copies[6].wait()
    gas[...] = conv_back(cols_g, w2).reshape(SLOTS, VOX, C)
    both[0] = middle[...].astype(bf16)
    both[1] = gas[...].astype(bf16)
    total = jnp.zeros((1, C), f32)
    squares = jnp.zeros((1, C), f32)
    slots = 0.0
    for s in range(SLOTS):
        w = slot_weight(active, s)
        x = middle[s]
        total = total + w * jnp.sum(x, axis=0, keepdims=True)
        squares = squares + w * jnp.sum(x * x, axis=0, keepdims=True)
        slots = slots + w
    packed = pack_stats([total, squares, jnp.full((1, C), slots, f32)])
    stats2[:, 0:C] = jnp.broadcast_to(packed[0:1], (PEERS, C))
    stats2[:, C : 2 * C] = jnp.broadcast_to(total, (PEERS, C))
    store_shares(window_sums(cols_a), stats2, 2)


def second_kernel(
    feat,
    gout,
    active,
    index,
    middle,
    gas,
    stats1,
    stats2,
    gain2,
    bias2,
    w2,
    *rest,
):
    fields, rest = rest[:3], rest[3:]
    block, stats3, grad_w, table, pad, cols, act, scratch = rest
    me = lax.axis_index("space")
    mean, inv, count = norm_stats(stats2)
    gain = gain2[...]
    bias = bias2[...]

    def act_of(ref, e, s):
        n = (ref[e, 0, s].astype(f32) - mean) * inv * gain + bias
        return n * sigmoid(n)

    fill_table(table, fields, scratch, me, act_of)
    sum_q = jnp.zeros((1, C), f32)
    sum_c = jnp.zeros((1, C), f32)
    for s in range(SLOTS):
        w = slot_weight(active, s)
        hat = (middle[s] - mean) * inv
        n = hat * gain + bias
        sg = sigmoid(n)
        act[s] = w * (n * sg)
        q = gas[s] * w * sg * (1.0 + n * (1.0 - sg)) * gain
        sum_q = sum_q + jnp.sum(q, axis=0, keepdims=True)
        sum_c = sum_c + jnp.sum(q * hat, axis=0, keepdims=True)
    packed = pack_stats([sum_q, sum_c])
    stats3[:, 0:C] = jnp.broadcast_to(packed[0:1], (PEERS, C))
    stats3[:, C : 2 * C] = jnp.broadcast_to(sum_q, (PEERS, C))
    place_interior(pad, act)
    place_halo(pad, table, index)
    windows_of(pad, cols)
    store_shares(window_sums(cols), stats3, 2)
    out = conv(cols, w2).reshape(SLOTS, VOX, C)
    for s in range(SLOTS):
        w = slot_weight(active, s)
        block[s] = ((feat[s].astype(f32) + out[s]) * w).astype(bf16)
        act[s] = jnp.where(active[0, s] > 0, gout[s].astype(f32), 0.0)
    centre = grad_centre(stats1, count)
    weight_grad(cols, act[...].astype(bf16).reshape(SLOTS * VOX, C), centre, grad_w)


def third_kernel(
    feat,
    active,
    index,
    middle,
    gas,
    stats1,
    stats2,
    stats3,
    gain1,
    bias1,
    gain2,
    bias2,
    w1,
    cols_a,
    grad_w2,
    *rest,
):
    fields, rest = rest[:3], rest[3:]
    q1, keep, give, table, pad, cols, act, scratch, grad_w1 = rest
    me = lax.axis_index("space")
    mean, inv, count = norm_stats(stats2)
    gain = gain2[...]
    bias = bias2[...]
    packed = total_of(stats3)
    mean_q = unpack_stat(packed, 0)[0:1] / count
    mean_c = unpack_stat(packed, 1)[0:1] / count

    def grad_of(x, g):
        hat = (x - mean) * inv
        n = hat * gain + bias
        sg = sigmoid(n)
        q = g * sg * (1.0 + n * (1.0 - sg)) * gain
        return (inv * (q - mean_q - hat * mean_c)).astype(bf16).astype(f32)

    fill_table(
        table,
        fields,
        scratch,
        me,
        lambda ref, e, s: grad_of(ref[e, 0, s].astype(f32), ref[e, 1, s].astype(f32)),
    )
    for s in range(SLOTS):
        act[s] = slot_weight(active, s) * grad_of(middle[s], gas[s])
    place_interior(pad, act)
    place_halo(pad, table, index)
    windows_of(pad, cols)
    gaf = conv_back(cols, w1).reshape(SLOTS, VOX, C)
    mean1, inv1, _ = norm_stats(stats1)
    sum_q = jnp.zeros((1, C), f32)
    sum_c = jnp.zeros((1, C), f32)
    for s in range(SLOTS):
        hat = (feat[s].astype(f32) - mean1) * inv1
        n = hat * gain1[...] + bias1[...]
        sg = sigmoid(n)
        q = gaf[s] * slot_weight(active, s) * sg * (1.0 + n * (1.0 - sg)) * gain1[...]
        q1[s] = q
        sum_q = sum_q + jnp.sum(q, axis=0, keepdims=True)
        sum_c = sum_c + jnp.sum(q * hat, axis=0, keepdims=True)
    packed = pack_stats([sum_q, sum_c])
    centre = middle_centre(stats2, stats3, count, mean, inv, mean_q, mean_c)
    weight_grad(cols_a, act[...].astype(bf16).reshape(SLOTS * VOX, C), centre, grad_w1)

    def store(out, core):
        for chip in range(PEERS // 2):
            start = SHARE * (2 * chip + core)
            out[chip, 0:SHARE] = grad_w1[start : start + SHARE]
            out[chip, 56 : 56 + SHARE] = grad_w2[start : start + SHARE]
            out[chip, SHARE : SHARE + 1] = packed[0:1]
            out[chip, SHARE + 1 : SHARE + 2] = packed[0:1]
            out[chip, 56 + SHARE : 112] = jnp.zeros((2, C), f32)

    @pl.when(me % 2 == 0)
    def _():
        store(keep, 0)
        store(give, 1)

    @pl.when(me % 2 == 1)
    def _():
        store(keep, 1)
        store(give, 0)


def pair_kernel(own, other, out):
    for n in range(PEERS // 2):
        total = own[n] + other[n]
        row = total[SHARE : SHARE + 1]
        high = row.astype(bf16)
        left = row - high.astype(f32)
        middle = left.astype(bf16)
        low = (left - middle.astype(f32)).astype(bf16)
        at = lax.broadcasted_iota(jnp.int32, (112, C), 0)
        total = jnp.where(at == SHARE, high.astype(f32), total)
        total = jnp.where(at == SHARE + 1, middle.astype(f32), total)
        total = jnp.where(at == 56 + SHARE, low.astype(f32), total)
        out[n] = total.astype(bf16)


def last_kernel(
    feat, gout, active, stats1, stats2, stats3, q1, parts, gain1, grad_in, rows
):
    total = parts[0].astype(f32)
    for n in range(1, PEERS // 2):
        total = total + parts[n].astype(f32)
    mean1, inv1, count = norm_stats(stats1)
    packed = total[SHARE : SHARE + 1] + total[SHARE + 1 : SHARE + 2] + total[110:111]
    packed = jnp.broadcast_to(packed, (8, C))
    mean_q = unpack_stat(packed, 0)[0:1] / count
    mean_c = unpack_stat(packed, 1)[0:1] / count
    for s in range(SLOTS):
        hat = (feat[s].astype(f32) - mean1) * inv1
        back = slot_weight(active, s) * inv1 * (q1[s] - mean_q - hat * mean_c)
        top = jnp.where(active[0, s] > 0, gout[s].astype(f32), 0.0)
        grad_in[s] = (top + back).astype(bf16)
    mean, inv, _ = norm_stats(stats2)
    packed = total_of(stats3)
    mean_q = unpack_stat(packed, 0)[0:1] / count
    mean_c = unpack_stat(packed, 1)[0:1] / count
    centre1 = middle_centre(stats2, stats3, count, mean, inv, mean_q, mean_c)
    centre2 = grad_centre(stats1, count)
    first = total[0:56] + outer(total_of(stats2, 2)[0:1], centre1)[0:56]
    second = total[56:112] + outer(total_of(stats3, 2)[0:1], centre2)[0:56]
    for n in range(8):
        rows[n, 0:56] = first
        rows[n, 56:112] = second


vmem = pl.BlockSpec(memory_space=pltpu.VMEM)
smem = pl.BlockSpec(memory_space=pltpu.SMEM)
hbm = pl.BlockSpec(memory_space=pl.ANY)


def call(kernel, specs, out_shape, scratch, args, out_specs=None):
    return pl.pallas_call(
        kernel,
        in_specs=specs,
        out_specs=out_specs or [vmem] * len(out_shape),
        out_shape=out_shape,
        scratch_shapes=scratch,
        compiler_params=pltpu.CompilerParams(vmem_limit_bytes=VMEM_BYTES),
    )(*args)


def shape(*dims, dtype=f32):
    return jax.ShapeDtypeStruct(dims, dtype)


def pairs_of(step, first):
    lower = [n for n in range(PEERS) if n // step % 2 == first]
    return [(n, (n + step) % PEERS) for n in lower] + [((n + step) % PEERS, n) for n in lower]


far_pairs = (pairs_of(4, 0), pairs_of(4, 1))
near_pairs = (pairs_of(1, 0), pairs_of(1, 1))


def exchange(fields, stats):
    far = [lax.ppermute(fields, "space", pairs) for pairs in far_pairs]
    stats = spread(stats)
    *far, stats = lax.optimization_barrier((*far, stats))
    three = jnp.stack([fields, *far])
    near = [lax.ppermute(three, "space", pairs) for pairs in near_pairs]
    return [three, *near], stats


def spread(stats):
    return lax.all_to_all(stats, "space", 0, 0, tiled=True)


chip_groups = [list(range(core, PEERS, 2)) for core in range(2)]


def per_device(
    features,
    active,
    neighbor_owner,
    record_position,
    send_list,
    conv_first,
    conv_second,
    gain_first,
    bias_first,
    gain_second,
    bias_second,
    grad_output,
):
    feat = features[0]
    gout = grad_output[0]
    owners = neighbor_owner[0]
    positions = record_position[0]
    lists = send_list[0, 0]
    gain1, bias1 = gain_first.reshape(1, C), bias_first.reshape(1, C)
    gain2, bias2 = gain_second.reshape(1, C), bias_second.reshape(1, C)
    field = (SLOTS, VOX, C)
    wide = pltpu.VMEM(field, f32)
    scratch = pltpu.VMEM((2, *field), f32)
    table = pltpu.VMEM((LANES * PLANES, PLANE, C), f32)
    pad = pltpu.VMEM((SLOTS, 6, 6, 8, C), f32)
    cols_shape = (9, SLOTS, 6, PLANE, C)
    cols = pltpu.VMEM(cols_shape, bf16)

    stats1, both = call(
        start_kernel,
        [hbm, hbm, hbm, hbm],
        [shape(PEERS, 2 * C), shape(2, *field, dtype=bf16)],
        [
            pltpu.SMEM((1, SLOTS), jnp.int32),
            pltpu.VMEM((PEERS, CAP), jnp.int32),
            pltpu.SemaphoreType.DMA((4,)),
        ],
        (feat, gout, active, lists),
    )
    fields0, stats1 = exchange(both, stats1)

    middle, gas, cols_a, stats2, both, index = call(
        first_kernel,
        [hbm] * 7 + [vmem] * 4,
        [shape(*field), shape(*field), shape(*cols_shape, dtype=bf16), shape(PEERS, 3 * C)]
        + [shape(2, *field, dtype=bf16), shape(SLOTS, 26, dtype=jnp.int32)],
        [table, pad, cols, wide, scratch, pltpu.VMEM((PEERS, C), jnp.int32)]
        + [
            pltpu.SMEM((1, SLOTS), jnp.int32),
            pltpu.SMEM((SLOTS, 26), jnp.int32),
            pltpu.SMEM((SLOTS, 26), jnp.int32),
            pltpu.SMEM((PEERS, C), jnp.int32),
            pltpu.VMEM((1, C), f32),
            pltpu.VMEM((1, C), f32),
            pltpu.VMEM((27, C, C), bf16),
            pltpu.VMEM((27, C, C), bf16),
            pltpu.SemaphoreType.DMA((8,)),
        ],
        (active, owners, positions, gain1, bias1, conv_first, conv_second, stats1, *fields0),
        [vmem] * 5 + [smem],
    )
    fields1, stats2 = exchange(both, stats2)

    block, stats3, grad_w2 = call(
        second_kernel,
        [vmem, vmem, smem, smem] + [vmem] * 10,
        [shape(*field, dtype=bf16), shape(PEERS, 3 * C), shape(27 * C, C)],
        [table, pad, cols, wide, scratch],
        (feat, gout, active, index, middle, gas, stats1, stats2, gain2, bias2)
        + (conv_second, *fields1),
    )
    stats3 = spread(stats3)

    q1, keep, give = call(
        third_kernel,
        [vmem, smem, smem] + [vmem] * 15,
        [shape(*field), shape(PEERS // 2, 112, C), shape(PEERS // 2, 112, C)],
        [table, pad, cols, wide, scratch, pltpu.VMEM((27 * C, C), f32)],
        (feat, active, index, middle, gas, stats1, stats2, stats3)
        + (gain1, bias1, gain2, bias2, conv_first, cols_a, grad_w2, *fields1),
    )
    other = lax.ppermute(give, "space", near_pairs[0])
    (share,) = call(
        pair_kernel,
        [vmem, vmem],
        [shape(PEERS // 2, 112, C, dtype=bf16)],
        [],
        (keep, other),
    )
    share = lax.all_to_all(share, "space", 0, 0, axis_index_groups=chip_groups)

    grad_in, rows = call(
        last_kernel,
        [vmem, vmem, smem] + [vmem] * 6,
        [shape(*field, dtype=bf16), shape(8, 112, C)],
        [],
        (feat, gout, active, stats1, stats2, stats3, q1, share, gain1),
    )
    rows = lax.all_to_all(rows, "scene", 0, 0)
    rows = jnp.sum(rows, axis=0).astype(bf16)
    return (block[None], grad_in[None], rows[:SHARE], rows[56 : 56 + SHARE])


def solution(mesh):
    return jax.shard_map(
        per_device,
        mesh=mesh,
        in_specs=(
            P("scene", "space", None, None),
            P("scene", "space"),
            P("scene", "space", None),
            P("scene", "space", None),
            P("scene", "space", None, None),
            P(),
            P(),
            P(),
            P(),
            P(),
            P(),
            P("scene", "space", None, None),
        ),
        out_specs=(
            P("scene", "space", None, None),
            P("scene", "space", None, None),
            P("space", None),
            P("space", None),
        ),
        check_vma=False,
    )
```

```python
import jax
import jax.numpy as jnp
from jax import lax
from jax.experimental import pallas as pl
from jax.experimental.pallas import tpu as pltpu
from jax.sharding import PartitionSpec as P

EDGE = 4
SLOTS = 4
VOX = 64
C = 128
CAP = 10
PEERS = 64
PLANE = 16
SHARE = 54
ROWS = 128
SUM_ROW = 108
CENTRE_ROW = 112
GROUP_COUNT = 64 * 4
EPS = 1e-05

directions = [
    (ordinal // 9 - 1, ordinal // 3 % 3 - 1, ordinal % 3 - 1)
    for ordinal in range(27)
    if ordinal != 13
]
PLANES = 24
LANES = 11
ZERO_PLANE = 3 * PLANES

f32 = jnp.float32
bf16 = jnp.bfloat16
VMEM_BYTES = 40 * 1024 * 1024


def group_total(row):
    lane = lax.broadcasted_iota(jnp.int32, row.shape, 1)
    row = row + jnp.where(lane % 2 == 0, pltpu.roll(row, C - 1, 1), pltpu.roll(row, 1, 1))
    return row + jnp.where(lane % 4 < 2, pltpu.roll(row, C - 2, 1), pltpu.roll(row, 2, 1))


def pack_stats(rows):
    rows = [jnp.broadcast_to(row, (8, C)) for row in rows]
    lane = lax.broadcasted_iota(jnp.int32, (8, C), 1)
    packed = jnp.zeros((8, C), f32)
    for n, row in enumerate(rows):
        packed = jnp.where(lane % 4 == n, group_total(row), packed)
    return packed


def unpack_stat(packed, n):
    lane = lax.broadcasted_iota(jnp.int32, packed.shape, 1)
    return group_total(jnp.where(lane % 4 == n, packed, 0.0))


def total_of(stats_ref):
    return jnp.broadcast_to(jnp.sum(stats_ref[...], axis=0, keepdims=True), (8, C))


def norm_stats(stats_ref):
    packed = total_of(stats_ref)
    count = unpack_stat(packed, 2) * (GROUP_COUNT / 4)
    mean = unpack_stat(packed, 0) / count
    inv = lax.rsqrt(unpack_stat(packed, 1) / count - mean * mean + EPS)
    return mean[0:1], inv[0:1], count[0:1]


def sigmoid(n):
    return 1.0 / (1.0 + jnp.exp(-n))


def slot_weight(active_ref, s):
    return active_ref[0, s].astype(f32)


def planes_of(src, dst, start):
    for s in range(SLOTS):
        dst[start + 6 * s] = src[s, 0:16]
        dst[start + 6 * s + 1] = src[s, 48:64]
        for a in range(4):
            dst[start + 6 * s + 2, 4 * a : 4 * a + 4] = src[s, 16 * a : 16 * a + 4]
            dst[start + 6 * s + 3, 4 * a : 4 * a + 4] = src[s, 16 * a + 12 : 16 * a + 16]
        dst[start + 6 * s + 4] = src[s, pl.ds(0, 16, stride=4)]
        dst[start + 6 * s + 5] = src[s, pl.ds(3, 16, stride=4)]


def far_distance(device):
    return 4 - 8 * ((device >> 2) & 1)


def near_distance(device):
    return 1 - 2 * (device & 1)


def fill_table(table, fields, scratch, me, make):
    near = near_distance(me)
    turn = 0
    for ref, base in zip(fields, (0, near, -near)):
        far = far_distance((me + base) & (PEERS - 1))
        for entry, more in enumerate((0, far, -far)):
            start = (base + more + 5) * PLANES
            buffer = scratch.at[turn % 2]
            turn += 1
            for s in range(SLOTS):
                buffer[s] = make(ref, entry, s)
            planes_of(buffer, table, start)
    table[ZERO_PLANE] = jnp.zeros((PLANE, C), f32)


def find_planes(owners, positions, ids, index, me):
    def one_slot(s, carry):
        for n in range(26):
            owner = owners[s, n]
            plane = ids[jnp.maximum(owner, 0), 4 * positions[s, n] + 3]
            plane = jnp.clip(plane, 0, PLANES - 1)
            index[s, n] = jnp.where(
                owner >= 0, (owner - me + 5) * PLANES + plane, ZERO_PLANE
            )
        return carry

    lax.fori_loop(0, SLOTS, one_slot, 0)


def fetch(sources, targets, sems):
    copies = [
        pltpu.make_async_copy(source, target, sems.at[n])
        for n, (source, target) in enumerate(zip(sources, targets))
    ]
    for copy in copies:
        copy.start()
    return copies


def place_halo(pad, table, index_ref):
    def one_slot(s, carry):
        for n, (d0, d1, d2) in enumerate(directions):
            index = index_ref[s, n]
            cells = [(5 if d > 0 else 0, 0 if d > 0 else 3) for d in (d0, d1, d2)]
            (a_to, _), (b_to, b_from), (c_to, c_from) = cells

            def row(r, count=1):
                return table[index, r : r + count]

            if d0 != 0:
                if d1 == 0 and d2 == 0:
                    for b in range(4):
                        pad[s, a_to, 1 + b, 1:5] = row(4 * b, 4)
                elif d2 == 0:
                    pad[s, a_to, b_to, 1:5] = row(4 * b_from, 4)
                elif d1 == 0:
                    for b in range(4):
                        pad[s, a_to, 1 + b, c_to : c_to + 1] = row(4 * b + c_from)
                else:
                    pad[s, a_to, b_to, c_to : c_to + 1] = row(4 * b_from + c_from)
            elif d1 != 0:
                for a in range(4):
                    if d2 == 0:
                        pad[s, 1 + a, b_to, 1:5] = row(4 * a, 4)
                    else:
                        pad[s, 1 + a, b_to, c_to : c_to + 1] = row(4 * a + c_from)
            else:
                for a in range(4):
                    for b in range(4):
                        pad[s, 1 + a, 1 + b, c_to : c_to + 1] = row(4 * a + b)
        return carry

    lax.fori_loop(0, SLOTS, one_slot, 0)


def place_interior(pad, field):
    for s in range(SLOTS):
        for a in range(4):
            for b in range(4):
                pad[s, 1 + a, 1 + b, 1:5] = field[s, 16 * a + 4 * b : 16 * a + 4 * b + 4]


def windows_of(pad, cols):
    def one_layer(t, carry):
        s, a = t // 6, t % 6
        sub = lax.broadcasted_iota(jnp.int32, (8, C), 0)
        layer = [pad[s, a, b] for b in range(6)]
        for k2 in range(3):
            low = [pltpu.roll(v, (8 - k2) % 8, 0) if k2 else v for v in layer]
            high = [pltpu.roll(v, 4 - k2, 0) for v in layer]
            pair = [jnp.where(sub < 4, low[b], high[b + 1]) for b in range(5)]
            for k1 in range(3):
                tile = jnp.concatenate([pair[k1], pair[k1 + 2]], axis=0)
                cols[3 * k1 + k2, s, a] = tile.astype(bf16)
        return carry

    lax.fori_loop(0, SLOTS * 6, one_layer, 0)


def window(cols, k0, k1, k2):
    return cols[3 * k1 + k2, :, k0 : k0 + 4].reshape(SLOTS * VOX, C)


def conv(cols, weight):
    total = jnp.zeros((SLOTS * VOX, C), f32)
    for k0 in range(3):
        left = jnp.concatenate([window(cols, k0, j // 3, j % 3) for j in range(9)], axis=1)
        right = weight[9 * k0 : 9 * k0 + 9].reshape(9 * C, C)
        total = total + jnp.dot(left, right, preferred_element_type=f32)
    return total


def conv_back(cols, weight):
    total = jnp.zeros((SLOTS * VOX, C), f32)
    for k0 in range(3):
        left = jnp.concatenate(
            [window(cols, 2 - k0, 2 - j // 3, 2 - j % 3) for j in range(9)], axis=1
        )
        right = jnp.concatenate([weight[9 * k0 + j] for j in range(9)], axis=1)
        total = total + lax.dot_general(
            left, right, (((1,), (1,)), ((), ())), preferred_element_type=f32
        )
    return total


def weight_grad(cols, grad, centre, out):
    right = jnp.concatenate([grad, jnp.ones((SLOTS * VOX, C), bf16)], axis=1)
    for k0 in range(3):
        left = jnp.concatenate([window(cols, k0, j // 3, j % 3) for j in range(9)], axis=1)
        both = lax.dot_general(
            left, right, (((0,), (0,)), ((), ())), preferred_element_type=f32
        )
        out[9 * C * k0 : 9 * C * (k0 + 1)] = both[:, :C] - both[:, C:] * centre


def window_sums(cols):
    ones = jnp.ones((8, SLOTS * VOX), bf16)
    rows = []
    for k0 in range(3):
        left = jnp.concatenate([window(cols, k0, j // 3, j % 3) for j in range(9)], axis=1)
        total = jnp.dot(ones, left, preferred_element_type=f32)
        rows += [total[0:1, C * j : C * (j + 1)] for j in range(9)]
    return rows


def store_shares(rows, out):
    lane = lax.broadcasted_iota(jnp.int32, (1, C), 1)
    for p in range(PEERS):
        k, skip = divmod(SHARE * p, C)
        line = rows[k] if skip == 0 else pltpu.roll(rows[k], C - skip, 1)
        if skip + SHARE > C:
            line = jnp.where(lane < C - skip, line, pltpu.roll(rows[k + 1], C - skip, 1))
        out[p : p + 1] = jnp.where(lane < SHARE, line, 0.0)


def centre_of(field, active):
    total = jnp.zeros((1, C), f32)
    slots = 0.0
    for s in range(SLOTS):
        total = total + jnp.sum(field[s], axis=0, keepdims=True)
        slots = slots + slot_weight(active, s)
    return (total / (jnp.maximum(slots, 1.0) * VOX)).astype(bf16).astype(f32)


def start_kernel(feat_in, gout_in, active_in, list_in, stats, both, active, send_list, sems):
    feat, gout = both.at[0], both.at[1]
    copies = fetch(
        (active_in, list_in, feat_in, gout_in), (active, send_list, feat, gout), sems
    )
    for copy in copies:
        copy.wait()
    total = jnp.zeros((1, C), f32)
    squares = jnp.zeros((1, C), f32)
    slots = 0.0
    for s in range(SLOTS):
        w = slot_weight(active, s)
        x = feat[s].astype(f32)
        total = total + w * jnp.sum(x, axis=0, keepdims=True)
        squares = squares + w * jnp.sum(x * x, axis=0, keepdims=True)
        slots = slots + w
    packed = pack_stats([total, squares, jnp.full((1, C), slots, f32)])
    record = lax.broadcasted_iota(jnp.int32, (CAP, C), 0)
    lane = lax.broadcasted_iota(jnp.int32, (CAP, C), 1)
    select = jnp.where(lane == 4 * record + 3, 1.0, 0.0).astype(bf16)
    ids = lax.dot_general(
        send_list[:, 0].astype(bf16),
        select,
        (((0,), (0,)), ((), ())),
        preferred_element_type=f32,
    )
    stats[...] = ids + packed[0:1]


def first_kernel(
    active_in, own_in, pos_in, gain_in, bias_in, w1_in, w2_in, stats1, *rest
):
    fields, rest = rest[:3], rest[3:]
    middle, gas, cols_a, both, index = rest[:5]
    table, pad, cols_g, act, scratch, ids_v = rest[5:11]
    active, owners, positions, ids, gain1, bias1, w1, w2, sems = rest[11:]
    me = lax.axis_index("space")
    copies = fetch(
        (gain_in, bias_in, active_in, own_in, pos_in, w1_in, w2_in),
        (gain1, bias1, active, owners, positions, w1, w2),
        sems,
    )
    ids_v[...] = stats1[...].astype(jnp.int32)
    ids_copy = pltpu.make_async_copy(ids_v, ids, sems.at[7])
    ids_copy.start()
    feat, gout = fields[0].at[0, 0], fields[0].at[0, 1]
    mean, inv, _ = norm_stats(stats1)
    copies[0].wait()
    copies[1].wait()

    def act_of(x):
        n = (x - mean) * inv * gain1[...] + bias1[...]
        return n * sigmoid(n)

    fill_table(table, fields, scratch, me, lambda ref, e, s: act_of(ref[e, 0, s].astype(f32)))
    for copy in copies[2:5]:
        copy.wait()
    ids_copy.wait()
    find_planes(owners, positions, ids, index, me)
    for s in range(SLOTS):
        act[s] = slot_weight(active, s) * act_of(feat[s].astype(f32))
    place_interior(pad, act)
    place_halo(pad, table, index)
    windows_of(pad, cols_a)
    copies[5].wait()
    middle[...] = conv(cols_a, w1).reshape(SLOTS, VOX, C)
    fill_table(table, fields, scratch, me, lambda ref, e, s: ref[e, 1, s].astype(f32))
    for s in range(SLOTS):
        act[s] = jnp.where(active[0, s] > 0, gout[s].astype(f32), 0.0)
    place_interior(pad, act)
    place_halo(pad, table, index)
    windows_of(pad, cols_g)
    copies[6].wait()
    gas[...] = conv_back(cols_g, w2).reshape(SLOTS, VOX, C)
    both[0] = middle[...].astype(bf16)
    both[1] = gas[...].astype(bf16)


def sums_kernel(active, middle, stats2):
    total = jnp.zeros((1, C), f32)
    squares = jnp.zeros((1, C), f32)
    slots = 0.0
    for s in range(SLOTS):
        w = slot_weight(active, s)
        x = middle[s]
        total = total + w * jnp.sum(x, axis=0, keepdims=True)
        squares = squares + w * jnp.sum(x * x, axis=0, keepdims=True)
        slots = slots + w
    packed = pack_stats([total, squares, jnp.full((1, C), slots, f32)])
    stats2[...] = jnp.broadcast_to(packed[0:1], (PEERS, C))


def second_kernel(
    feat,
    gout,
    active,
    index,
    middle,
    gas,
    stats2,
    gain2,
    bias2,
    w2,
    *rest,
):
    fields, rest = rest[:3], rest[3:]
    block, stats3, grad_w, sums2, centre2, table, pad, cols, act, scratch = rest
    me = lax.axis_index("space")
    mean, inv, _ = norm_stats(stats2)
    gain = gain2[...]
    bias = bias2[...]

    def act_of(ref, e, s):
        n = (ref[e, 0, s].astype(f32) - mean) * inv * gain + bias
        return n * sigmoid(n)

    fill_table(table, fields, scratch, me, act_of)
    sum_q = jnp.zeros((1, C), f32)
    sum_c = jnp.zeros((1, C), f32)
    for s in range(SLOTS):
        w = slot_weight(active, s)
        hat = (middle[s] - mean) * inv
        n = hat * gain + bias
        sg = sigmoid(n)
        act[s] = w * (n * sg)
        q = gas[s] * w * sg * (1.0 + n * (1.0 - sg)) * gain
        sum_q = sum_q + jnp.sum(q, axis=0, keepdims=True)
        sum_c = sum_c + jnp.sum(q * hat, axis=0, keepdims=True)
    packed = pack_stats([sum_q, sum_c])
    stats3[...] = jnp.broadcast_to(packed[0:1], (PEERS, C))
    place_interior(pad, act)
    place_halo(pad, table, index)
    windows_of(pad, cols)
    store_shares(window_sums(cols), sums2)
    out = conv(cols, w2).reshape(SLOTS, VOX, C)
    for s in range(SLOTS):
        w = slot_weight(active, s)
        block[s] = ((feat[s].astype(f32) + out[s]) * w).astype(bf16)
        act[s] = jnp.where(active[0, s] > 0, gout[s].astype(f32), 0.0)
    centre = centre_of(act, active)
    centre2[...] = jnp.broadcast_to(centre, (8, C))
    weight_grad(cols, act[...].astype(bf16).reshape(SLOTS * VOX, C), centre, grad_w)


def third_kernel(
    feat,
    active,
    index,
    middle,
    gas,
    stats1,
    stats2,
    stats3,
    gain1,
    bias1,
    gain2,
    bias2,
    w1,
    cols_a,
    grad_w2,
    sums2,
    centre2,
    *rest,
):
    fields, rest = rest[:3], rest[3:]
    q1, keep, give, table, pad, cols, act, scratch, grad_w1, sums1 = rest
    me = lax.axis_index("space")
    mean, inv, count = norm_stats(stats2)
    gain = gain2[...]
    bias = bias2[...]
    packed = total_of(stats3)
    mean_q = unpack_stat(packed, 0)[0:1] / count
    mean_c = unpack_stat(packed, 1)[0:1] / count

    def grad_of(x, g):
        hat = (x - mean) * inv
        n = hat * gain + bias
        sg = sigmoid(n)
        q = g * sg * (1.0 + n * (1.0 - sg)) * gain
        return (inv * (q - mean_q - hat * mean_c)).astype(bf16).astype(f32)

    fill_table(
        table,
        fields,
        scratch,
        me,
        lambda ref, e, s: grad_of(ref[e, 0, s].astype(f32), ref[e, 1, s].astype(f32)),
    )
    for s in range(SLOTS):
        act[s] = slot_weight(active, s) * grad_of(middle[s], gas[s])
    place_interior(pad, act)
    place_halo(pad, table, index)
    windows_of(pad, cols)
    gaf = conv_back(cols, w1).reshape(SLOTS, VOX, C)
    mean1, inv1, _ = norm_stats(stats1)
    sum_q = jnp.zeros((1, C), f32)
    sum_c = jnp.zeros((1, C), f32)
    for s in range(SLOTS):
        hat = (feat[s].astype(f32) - mean1) * inv1
        n = hat * gain1[...] + bias1[...]
        sg = sigmoid(n)
        q = gaf[s] * slot_weight(active, s) * sg * (1.0 + n * (1.0 - sg)) * gain1[...]
        q1[s] = q
        sum_q = sum_q + jnp.sum(q, axis=0, keepdims=True)
        sum_c = sum_c + jnp.sum(q * hat, axis=0, keepdims=True)
    packed = pack_stats([sum_q, sum_c])
    centre = centre_of(act, active)
    store_shares(window_sums(cols_a), sums1)
    weight_grad(cols_a, act[...].astype(bf16).reshape(SLOTS * VOX, C), centre, grad_w1)

    def store(out, core):
        for chip in range(PEERS // 2):
            p = 2 * chip + core
            out[chip, 0:SHARE] = grad_w1[SHARE * p : SHARE * (p + 1)]
            out[chip, SHARE : 2 * SHARE] = grad_w2[SHARE * p : SHARE * (p + 1)]
            out[chip, SUM_ROW : SUM_ROW + 1] = packed[0:1]
            out[chip, SUM_ROW + 1 : CENTRE_ROW] = jnp.zeros((3, C), f32)
            out[chip, CENTRE_ROW : CENTRE_ROW + 1] = sums1[p : p + 1]
            out[chip, CENTRE_ROW + 1 : CENTRE_ROW + 2] = centre
            out[chip, CENTRE_ROW + 2 : CENTRE_ROW + 3] = sums2[p : p + 1]
            out[chip, CENTRE_ROW + 3 : CENTRE_ROW + 4] = centre2[0:1]
            out[chip, CENTRE_ROW + 4 : 120] = jnp.zeros((4, C), f32)

    @pl.when(me % 2 == 0)
    def _():
        store(keep, 0)
        store(give, 1)

    @pl.when(me % 2 == 1)
    def _():
        store(keep, 1)
        store(give, 0)


def pair_kernel(own, other, out):
    def terms(row, count):
        parts = []
        for _ in range(count):
            parts.append(row.astype(bf16).astype(f32))
            row = row - parts[-1]
        return parts

    for n in range(PEERS // 2):
        total = own[n, 0:CENTRE_ROW] + other[n, 0:CENTRE_ROW]
        at = lax.broadcasted_iota(jnp.int32, (CENTRE_ROW, C), 0)
        for k, term in enumerate(terms(total[SUM_ROW : SUM_ROW + 1], 3)):
            total = jnp.where(at == SUM_ROW + k, term, total)
        out[n, 0:CENTRE_ROW] = total.astype(bf16)
        more = jnp.zeros((16, C), f32)
        at = lax.broadcasted_iota(jnp.int32, (16, C), 0)
        for core, ref in enumerate((own, other)):
            rows = ref[n, CENTRE_ROW : CENTRE_ROW + 8]
            lines = terms(rows[0:1], 2) + [rows[1:2]] + terms(rows[2:3], 2) + [rows[3:4]]
            for k, line in enumerate(lines):
                more = jnp.where(at == 6 * core + k, line, more)
        out[n, CENTRE_ROW:ROWS] = more.astype(bf16)


def last_kernel(feat, gout, active, stats1, q1, parts, gain1, grad_in, rows):
    total = parts[0].astype(f32)
    for n in range(1, PEERS // 2):
        total = total + parts[n].astype(f32)
    mean1, inv1, count = norm_stats(stats1)
    packed = jnp.sum(total[SUM_ROW : SUM_ROW + 3], axis=0, keepdims=True)
    packed = jnp.broadcast_to(packed, (8, C))
    mean_q = unpack_stat(packed, 0)[0:1] / count
    mean_c = unpack_stat(packed, 1)[0:1] / count
    for s in range(SLOTS):
        hat = (feat[s].astype(f32) - mean1) * inv1
        back = slot_weight(active, s) * inv1 * (q1[s] - mean_q - hat * mean_c)
        top = jnp.where(active[0, s] > 0, gout[s].astype(f32), 0.0)
        grad_in[s] = (top + back).astype(bf16)
    left = [[], []]
    right = [[], []]
    for n in range(PEERS // 2):
        more = parts[n, CENTRE_ROW:ROWS].astype(f32)
        for core in range(2):
            for weight in range(2):
                first = 6 * core + 3 * weight
                line = more[first + 2 : first + 3]
                left[weight] += [more[first : first + 1], more[first + 1 : first + 2]]
                right[weight] += [line, line]
    for weight in range(2):
        outer = lax.dot_general(
            jnp.concatenate(left[weight], axis=0).astype(bf16),
            jnp.concatenate(right[weight], axis=0).astype(bf16),
            (((0,), (0,)), ((), ())),
            preferred_element_type=f32,
        )
        whole = total[SHARE * weight : SHARE * (weight + 1)] + outer[0:SHARE]
        for n in range(8):
            rows[n, 56 * weight : 56 * weight + SHARE] = whole
            rows[n, 56 * weight + SHARE : 56 * weight + 56] = jnp.zeros((2, C), f32)


vmem = pl.BlockSpec(memory_space=pltpu.VMEM)
smem = pl.BlockSpec(memory_space=pltpu.SMEM)
hbm = pl.BlockSpec(memory_space=pltpu.HBM)


def call(kernel, specs, out_shape, scratch, args, out_specs=None):
    args = [
        pltpu.with_memory_space_constraint(arg, pltpu.HBM) if spec is hbm else arg
        for spec, arg in zip(specs, args)
    ]
    return pl.pallas_call(
        kernel,
        in_specs=specs,
        out_specs=out_specs or [vmem] * len(out_shape),
        out_shape=out_shape,
        scratch_shapes=scratch,
        compiler_params=pltpu.CompilerParams(vmem_limit_bytes=VMEM_BYTES),
    )(*args)


def shape(*dims, dtype=f32):
    return jax.ShapeDtypeStruct(dims, dtype)


def pairs_of(step, first):
    lower = [n for n in range(PEERS) if n // step % 2 == first]
    return [(n, (n + step) % PEERS) for n in lower] + [((n + step) % PEERS, n) for n in lower]


far_pairs = (pairs_of(4, 0), pairs_of(4, 1))
near_pairs = (pairs_of(1, 0), pairs_of(1, 1))


def exchange(fields, stats):
    far = [lax.ppermute(fields, "space", pairs) for pairs in far_pairs]
    stats = spread(stats)
    *far, stats = lax.optimization_barrier((*far, stats))
    three = jnp.stack([fields, *far])
    near = [lax.ppermute(three, "space", pairs) for pairs in near_pairs]
    return [three, *near], stats


def spread(stats):
    return lax.all_to_all(stats, "space", 0, 0, tiled=True)


chip_groups = [list(range(core, PEERS, 2)) for core in range(2)]


def per_device(
    features,
    active,
    neighbor_owner,
    record_position,
    send_list,
    conv_first,
    conv_second,
    gain_first,
    bias_first,
    gain_second,
    bias_second,
    grad_output,
):
    feat = features[0]
    gout = grad_output[0]
    owners = neighbor_owner[0]
    positions = record_position[0]
    lists = send_list[0].transpose(2, 0, 1)
    gain1, bias1 = gain_first.reshape(1, C), bias_first.reshape(1, C)
    gain2, bias2 = gain_second.reshape(1, C), bias_second.reshape(1, C)
    field = (SLOTS, VOX, C)
    wide = pltpu.VMEM(field, f32)
    scratch = pltpu.VMEM((2, *field), f32)
    table = pltpu.VMEM((LANES * PLANES, PLANE, C), f32)
    pad = pltpu.VMEM((SLOTS, 6, 6, 8, C), f32)
    cols_shape = (9, SLOTS, 6, PLANE, C)
    cols = pltpu.VMEM(cols_shape, bf16)

    stats1, both = call(
        start_kernel,
        [hbm, hbm, hbm, hbm],
        [shape(PEERS, C), shape(2, *field, dtype=bf16)],
        [
            pltpu.SMEM((1, SLOTS), jnp.int32),
            pltpu.VMEM((CAP, 1, PEERS), jnp.int32),
            pltpu.SemaphoreType.DMA((4,)),
        ],
        (feat, gout, active, lists),
    )
    fields0, stats1 = exchange(both, stats1)

    middle, gas, cols_a, both, index = call(
        first_kernel,
        [hbm] * 7 + [vmem] * 4,
        [shape(*field), shape(*field), shape(*cols_shape, dtype=bf16)]
        + [shape(2, *field, dtype=bf16), shape(SLOTS, 26, dtype=jnp.int32)],
        [table, pad, cols, wide, scratch, pltpu.VMEM((PEERS, C), jnp.int32)]
        + [
            pltpu.SMEM((1, SLOTS), jnp.int32),
            pltpu.SMEM((SLOTS, 26), jnp.int32),
            pltpu.SMEM((SLOTS, 26), jnp.int32),
            pltpu.SMEM((PEERS, C), jnp.int32),
            pltpu.VMEM((1, C), f32),
            pltpu.VMEM((1, C), f32),
            pltpu.VMEM((27, C, C), bf16),
            pltpu.VMEM((27, C, C), bf16),
            pltpu.SemaphoreType.DMA((8,)),
        ],
        (active, owners, positions, gain1, bias1, conv_first, conv_second, stats1, *fields0),
        [vmem] * 4 + [smem],
    )
    (stats2,) = call(sums_kernel, [smem, vmem], [shape(PEERS, C)], [], (active, middle))
    fields1, stats2 = exchange(both, stats2)

    block, stats3, grad_w2, sums2, centre2 = call(
        second_kernel,
        [vmem, vmem, smem, smem] + [vmem] * 9,
        [shape(*field, dtype=bf16), shape(PEERS, C), shape(27 * C, C)]
        + [shape(PEERS, C), shape(8, C)],
        [table, pad, cols, wide, scratch],
        (feat, gout, active, index, middle, gas, stats2, gain2, bias2)
        + (conv_second, *fields1),
    )
    stats3 = spread(stats3)

    q1, keep, give = call(
        third_kernel,
        [vmem, smem, smem] + [vmem] * 17,
        [shape(*field), shape(PEERS // 2, 120, C), shape(PEERS // 2, 120, C)],
        [table, pad, cols, wide, scratch, pltpu.VMEM((27 * C, C), f32)]
        + [pltpu.VMEM((PEERS, C), f32)],
        (feat, active, index, middle, gas, stats1, stats2, stats3)
        + (gain1, bias1, gain2, bias2, conv_first, cols_a, grad_w2, sums2, centre2, *fields1),
    )
    other = lax.ppermute(give, "space", near_pairs[0])
    (share,) = call(
        pair_kernel,
        [vmem, vmem],
        [shape(PEERS // 2, ROWS, C, dtype=bf16)],
        [],
        (keep, other),
    )
    share = lax.all_to_all(share, "space", 0, 0, axis_index_groups=chip_groups)

    grad_in, rows = call(
        last_kernel,
        [vmem, vmem, smem] + [vmem] * 4,
        [shape(*field, dtype=bf16), shape(8, 112, C)],
        [],
        (feat, gout, active, stats1, q1, share, gain1),
    )
    rows = lax.all_to_all(rows, "scene", 0, 0)
    rows = jnp.sum(rows, axis=0).astype(bf16)
    return (block[None], grad_in[None], rows[:SHARE], rows[56 : 56 + SHARE])


def solution(mesh):
    return jax.shard_map(
        per_device,
        mesh=mesh,
        in_specs=(
            P("scene", "space", None, None),
            P("scene", "space"),
            P("scene", "space", None),
            P("scene", "space", None),
            P("scene", "space", None, None),
            P(),
            P(),
            P(),
            P(),
            P(),
            P(),
            P("scene", "space", None, None),
        ),
        out_specs=(
            P("scene", "space", None, None),
            P("scene", "space", None, None),
            P("space", None),
            P("space", None),
        ),
        check_vma=False,
    )
```

```python
import jax
import jax.numpy as jnp
from jax import lax
from jax.experimental import pallas as pl
from jax.experimental.pallas import tpu as pltpu
from jax.sharding import PartitionSpec as P

EDGE = 4
SLOTS = 4
VOX = 64
C = 128
CAP = 10
PEERS = 64
PLANE = 16
SHARE = 54
ROWS = 128
SUM_ROW = 108
CENTRE_ROW = 112
GROUP_COUNT = 64 * 4
EPS = 1e-05

directions = [
    (ordinal // 9 - 1, ordinal // 3 % 3 - 1, ordinal % 3 - 1)
    for ordinal in range(27)
    if ordinal != 13
]
PLANES = 24
LANES = 11
ZERO_PLANE = 3 * PLANES

f32 = jnp.float32
bf16 = jnp.bfloat16
VMEM_BYTES = 40 * 1024 * 1024


def group_total(row):
    lane = lax.broadcasted_iota(jnp.int32, row.shape, 1)
    row = row + jnp.where(lane % 2 == 0, pltpu.roll(row, C - 1, 1), pltpu.roll(row, 1, 1))
    return row + jnp.where(lane % 4 < 2, pltpu.roll(row, C - 2, 1), pltpu.roll(row, 2, 1))


def pack_stats(rows):
    rows = [jnp.broadcast_to(row, (8, C)) for row in rows]
    lane = lax.broadcasted_iota(jnp.int32, (8, C), 1)
    packed = jnp.zeros((8, C), f32)
    for n, row in enumerate(rows):
        packed = jnp.where(lane % 4 == n, group_total(row), packed)
    return packed


def unpack_stat(packed, n):
    lane = lax.broadcasted_iota(jnp.int32, packed.shape, 1)
    return group_total(jnp.where(lane % 4 == n, packed, 0.0))


def total_of(stats_ref):
    return jnp.broadcast_to(jnp.sum(stats_ref[...], axis=0, keepdims=True), (8, C))


def norm_stats(stats_ref):
    packed = total_of(stats_ref)
    count = unpack_stat(packed, 2) * (GROUP_COUNT / 4)
    mean = unpack_stat(packed, 0) / count
    inv = lax.rsqrt(unpack_stat(packed, 1) / count - mean * mean + EPS)
    return mean[0:1], inv[0:1], count[0:1]


def sigmoid(n):
    return 1.0 / (1.0 + jnp.exp(-n))


def slot_weight(active_ref, s):
    return active_ref[0, s].astype(f32)


def planes_of(src, dst, start):
    for s in range(SLOTS):
        dst[start + 6 * s] = src[s, 0:16]
        dst[start + 6 * s + 1] = src[s, 48:64]
        for a in range(4):
            dst[start + 6 * s + 2, 4 * a : 4 * a + 4] = src[s, 16 * a : 16 * a + 4]
            dst[start + 6 * s + 3, 4 * a : 4 * a + 4] = src[s, 16 * a + 12 : 16 * a + 16]
        dst[start + 6 * s + 4] = src[s, pl.ds(0, 16, stride=4)]
        dst[start + 6 * s + 5] = src[s, pl.ds(3, 16, stride=4)]


def far_distance(device):
    return 4 - 8 * ((device >> 2) & 1)


def near_distance(device):
    return 1 - 2 * (device & 1)


def fill_tables(tables, fields, scratch, me, make):
    near = near_distance(me)
    turn = 0
    for ref, base in zip(fields, (0, near, -near)):
        far = far_distance((me + base) & (PEERS - 1))
        for entry, more in enumerate((0, far, -far)):
            start = (base + more + 5) * PLANES
            buffer = scratch.at[turn % 2]
            turn += 1
            for s in range(SLOTS):
                for t, value in enumerate(make(ref.at[entry], s)):
                    buffer[t, s] = value
            for t, table in enumerate(tables):
                planes_of(buffer.at[t], table, start)
    for table in tables:
        table[ZERO_PLANE] = jnp.zeros((PLANE, C), f32)


def find_planes(owners, positions, ids, index, me):
    def one_slot(s, carry):
        for n in range(26):
            owner = owners[s, n]
            plane = ids[jnp.maximum(owner, 0), 4 * positions[s, n] + 3]
            plane = jnp.clip(plane, 0, PLANES - 1)
            index[s, n] = jnp.where(
                owner >= 0, (owner - me + 5) * PLANES + plane, ZERO_PLANE
            )
        return carry

    lax.fori_loop(0, SLOTS, one_slot, 0)


def fetch(sources, targets, sems):
    copies = [
        pltpu.make_async_copy(source, target, sems.at[n])
        for n, (source, target) in enumerate(zip(sources, targets))
    ]
    for copy in copies:
        copy.start()
    return copies


def place_halo(pad, table, index_ref):
    def one_slot(s, carry):
        for n, (d0, d1, d2) in enumerate(directions):
            index = index_ref[s, n]
            cells = [(5 if d > 0 else 0, 0 if d > 0 else 3) for d in (d0, d1, d2)]
            (a_to, _), (b_to, b_from), (c_to, c_from) = cells

            def row(r, count=1):
                return table[index, r : r + count]

            if d0 != 0:
                if d1 == 0 and d2 == 0:
                    for b in range(4):
                        pad[s, a_to, 1 + b, 1:5] = row(4 * b, 4)
                elif d2 == 0:
                    pad[s, a_to, b_to, 1:5] = row(4 * b_from, 4)
                elif d1 == 0:
                    for b in range(4):
                        pad[s, a_to, 1 + b, c_to : c_to + 1] = row(4 * b + c_from)
                else:
                    pad[s, a_to, b_to, c_to : c_to + 1] = row(4 * b_from + c_from)
            elif d1 != 0:
                for a in range(4):
                    if d2 == 0:
                        pad[s, 1 + a, b_to, 1:5] = row(4 * a, 4)
                    else:
                        pad[s, 1 + a, b_to, c_to : c_to + 1] = row(4 * a + c_from)
            else:
                for a in range(4):
                    for b in range(4):
                        pad[s, 1 + a, 1 + b, c_to : c_to + 1] = row(4 * a + b)
        return carry

    lax.fori_loop(0, SLOTS, one_slot, 0)


def place_interior(pad, field):
    for s in range(SLOTS):
        for a in range(4):
            for b in range(4):
                pad[s, 1 + a, 1 + b, 1:5] = field[s, 16 * a + 4 * b : 16 * a + 4 * b + 4]


def windows_of(pad, cols):
    def one_layer(t, carry):
        s, a = t // 6, t % 6
        sub = lax.broadcasted_iota(jnp.int32, (8, C), 0)
        layer = [pad[s, a, b] for b in range(6)]
        for k2 in range(3):
            low = [pltpu.roll(v, (8 - k2) % 8, 0) if k2 else v for v in layer]
            high = [pltpu.roll(v, 4 - k2, 0) for v in layer]
            pair = [jnp.where(sub < 4, low[b], high[b + 1]) for b in range(5)]
            for k1 in range(3):
                tile = jnp.concatenate([pair[k1], pair[k1 + 2]], axis=0)
                cols[3 * k1 + k2, s, a] = tile.astype(bf16)
        return carry

    lax.fori_loop(0, SLOTS * 6, one_layer, 0)


def window(cols, k0, k1, k2):
    return cols[3 * k1 + k2, :, k0 : k0 + 4].reshape(SLOTS * VOX, C)


def conv(cols, weight):
    total = jnp.zeros((SLOTS * VOX, C), f32)
    for k0 in range(3):
        left = jnp.concatenate([window(cols, k0, j // 3, j % 3) for j in range(9)], axis=1)
        right = weight[9 * k0 : 9 * k0 + 9].reshape(9 * C, C)
        total = total + jnp.dot(left, right, preferred_element_type=f32)
    return total


def conv_back(cols, weight):
    total = jnp.zeros((SLOTS * VOX, C), f32)
    for k0 in range(3):
        left = jnp.concatenate(
            [window(cols, 2 - k0, 2 - j // 3, 2 - j % 3) for j in range(9)], axis=1
        )
        right = jnp.concatenate([weight[9 * k0 + j] for j in range(9)], axis=1)
        total = total + lax.dot_general(
            left, right, (((1,), (1,)), ((), ())), preferred_element_type=f32
        )
    return total


def weight_grad(cols, grad, centre, out):
    right = jnp.concatenate([grad, jnp.ones((SLOTS * VOX, C), bf16)], axis=1)
    for k0 in range(3):
        left = jnp.concatenate([window(cols, k0, j // 3, j % 3) for j in range(9)], axis=1)
        both = lax.dot_general(
            left, right, (((0,), (0,)), ((), ())), preferred_element_type=f32
        )
        out[9 * C * k0 : 9 * C * (k0 + 1)] = both[:, :C] - both[:, C:] * centre


def window_sums(cols):
    ones = jnp.ones((8, SLOTS * VOX), bf16)
    rows = []
    for k0 in range(3):
        left = jnp.concatenate([window(cols, k0, j // 3, j % 3) for j in range(9)], axis=1)
        total = jnp.dot(ones, left, preferred_element_type=f32)
        rows += [total[0:1, C * j : C * (j + 1)] for j in range(9)]
    return rows


def store_shares(rows, out):
    lane = lax.broadcasted_iota(jnp.int32, (1, C), 1)
    for p in range(PEERS):
        k, skip = divmod(SHARE * p, C)
        line = rows[k] if skip == 0 else pltpu.roll(rows[k], C - skip, 1)
        if skip + SHARE > C:
            line = jnp.where(lane < C - skip, line, pltpu.roll(rows[k + 1], C - skip, 1))
        out[p : p + 1] = jnp.where(lane < SHARE, line, 0.0)


def centre_of(field, active):
    total = jnp.zeros((1, C), f32)
    slots = 0.0
    for s in range(SLOTS):
        total = total + jnp.sum(field[s], axis=0, keepdims=True)
        slots = slots + slot_weight(active, s)
    return (total / (jnp.maximum(slots, 1.0) * VOX)).astype(bf16).astype(f32)


def start_kernel(feat_in, gout_in, active_in, list_in, stats, both, active, send_list, sems):
    feat, gout = both.at[0], both.at[1]
    copies = fetch(
        (active_in, list_in, feat_in, gout_in), (active, send_list, feat, gout), sems
    )
    for copy in copies:
        copy.wait()
    total = jnp.zeros((1, C), f32)
    squares = jnp.zeros((1, C), f32)
    slots = 0.0
    for s in range(SLOTS):
        w = slot_weight(active, s)
        x = feat[s].astype(f32)
        total = total + w * jnp.sum(x, axis=0, keepdims=True)
        squares = squares + w * jnp.sum(x * x, axis=0, keepdims=True)
        slots = slots + w
    packed = pack_stats([total, squares, jnp.full((1, C), slots, f32)])
    record = lax.broadcasted_iota(jnp.int32, (CAP, C), 0)
    lane = lax.broadcasted_iota(jnp.int32, (CAP, C), 1)
    select = jnp.where(lane == 4 * record + 3, 1.0, 0.0).astype(bf16)
    ids = lax.dot_general(
        send_list[:, 0].astype(bf16),
        select,
        (((0,), (0,)), ((), ())),
        preferred_element_type=f32,
    )
    stats[...] = ids + packed[0:1]


def first_kernel(
    active_in, own_in, pos_in, gain_in, bias_in, w1_in, w2_in, stats1, *rest
):
    fields, rest = rest[:3], rest[3:]
    middle, gas, cols_a, both, index = rest[:5]
    table_f, table_g, pad, cols_g, act, scratch, ids_v = rest[5:12]
    active, owners, positions, ids, gain1, bias1, w1, w2, sems = rest[12:]
    me = lax.axis_index("space")
    copies = fetch(
        (gain_in, bias_in, active_in, own_in, pos_in, w1_in, w2_in),
        (gain1, bias1, active, owners, positions, w1, w2),
        sems,
    )
    ids_v[...] = stats1[...].astype(jnp.int32)
    ids_copy = pltpu.make_async_copy(ids_v, ids, sems.at[7])
    ids_copy.start()
    feat, gout = fields[0].at[0, 0], fields[0].at[0, 1]
    mean, inv, _ = norm_stats(stats1)
    copies[0].wait()
    copies[1].wait()

    def act_of(x):
        n = (x - mean) * inv * gain1[...] + bias1[...]
        return n * sigmoid(n)

    fill_tables(
        (table_f, table_g),
        fields,
        scratch,
        me,
        lambda ref, s: (act_of(ref[0, s].astype(f32)), ref[1, s].astype(f32)),
    )
    for copy in copies[2:5]:
        copy.wait()
    ids_copy.wait()
    find_planes(owners, positions, ids, index, me)
    for s in range(SLOTS):
        act[s] = slot_weight(active, s) * act_of(feat[s].astype(f32))
    place_interior(pad, act)
    place_halo(pad, table_f, index)
    windows_of(pad, cols_a)
    copies[5].wait()
    middle[...] = conv(cols_a, w1).reshape(SLOTS, VOX, C)
    for s in range(SLOTS):
        act[s] = jnp.where(active[0, s] > 0, gout[s].astype(f32), 0.0)
    place_interior(pad, act)
    place_halo(pad, table_g, index)
    windows_of(pad, cols_g)
    copies[6].wait()
    gas[...] = conv_back(cols_g, w2).reshape(SLOTS, VOX, C)
    both[0] = middle[...].astype(bf16)
    both[1] = gas[...].astype(bf16)


def sums_kernel(active, middle, stats2):
    total = jnp.zeros((1, C), f32)
    squares = jnp.zeros((1, C), f32)
    slots = 0.0
    for s in range(SLOTS):
        w = slot_weight(active, s)
        x = middle[s]
        total = total + w * jnp.sum(x, axis=0, keepdims=True)
        squares = squares + w * jnp.sum(x * x, axis=0, keepdims=True)
        slots = slots + w
    packed = pack_stats([total, squares, jnp.full((1, C), slots, f32)])
    stats2[...] = jnp.broadcast_to(packed[0:1], (PEERS, C))


def second_kernel(active, middle, gas, stats2, gain2, bias2, stats3):
    mean, inv, _ = norm_stats(stats2)
    gain = gain2[...]
    sum_q = jnp.zeros((1, C), f32)
    sum_c = jnp.zeros((1, C), f32)
    for s in range(SLOTS):
        hat = (middle[s] - mean) * inv
        n = hat * gain + bias2[...]
        sg = sigmoid(n)
        q = gas[s] * slot_weight(active, s) * sg * (1.0 + n * (1.0 - sg)) * gain
        sum_q = sum_q + jnp.sum(q, axis=0, keepdims=True)
        sum_c = sum_c + jnp.sum(q * hat, axis=0, keepdims=True)
    packed = pack_stats([sum_q, sum_c])
    stats3[...] = jnp.broadcast_to(packed[0:1], (PEERS, C))


def third_kernel(
    feat,
    gout,
    active,
    index,
    middle,
    gas,
    stats1,
    stats2,
    stats3,
    gain1,
    bias1,
    gain2,
    bias2,
    w1,
    w2,
    cols_a,
    *rest,
):
    fields, rest = rest[:3], rest[3:]
    block, q1, keep, give = rest[:4]
    table_a, table_g, pad, cols, field, own, scratch = rest[4:11]
    grad_w1, grad_w2, sums1, sums2 = rest[11:]
    me = lax.axis_index("space")
    mean, inv, count = norm_stats(stats2)
    gain = gain2[...]
    bias = bias2[...]
    packed = total_of(stats3)
    mean_q = unpack_stat(packed, 0)[0:1] / count
    mean_c = unpack_stat(packed, 1)[0:1] / count

    def both_of(x, g):
        hat = (x - mean) * inv
        n = hat * gain + bias
        sg = sigmoid(n)
        q = g * sg * (1.0 + n * (1.0 - sg)) * gain
        grad = inv * (q - mean_q - hat * mean_c)
        return n * sg, grad.astype(bf16).astype(f32)

    fill_tables(
        (table_a, table_g),
        fields,
        scratch,
        me,
        lambda ref, s: both_of(ref[0, s].astype(f32), ref[1, s].astype(f32)),
    )
    for s in range(SLOTS):
        act, grad = both_of(middle[s], gas[s])
        own[0, s] = slot_weight(active, s) * act
        own[1, s] = slot_weight(active, s) * grad
    place_interior(pad, own.at[0])
    place_halo(pad, table_a, index)
    windows_of(pad, cols)
    out = conv(cols, w2).reshape(SLOTS, VOX, C)
    for s in range(SLOTS):
        w = slot_weight(active, s)
        block[s] = ((feat[s].astype(f32) + out[s]) * w).astype(bf16)
        field[s] = jnp.where(active[0, s] > 0, gout[s].astype(f32), 0.0)
    store_shares(window_sums(cols), sums2)
    centre2 = centre_of(field, active)
    weight_grad(cols, field[...].astype(bf16).reshape(SLOTS * VOX, C), centre2, grad_w2)
    store_shares(window_sums(cols_a), sums1)
    centre1 = centre_of(own.at[1], active)
    weight_grad(cols_a, own[1].astype(bf16).reshape(SLOTS * VOX, C), centre1, grad_w1)
    place_interior(pad, own.at[1])
    place_halo(pad, table_g, index)
    windows_of(pad, cols)
    gaf = conv_back(cols, w1).reshape(SLOTS, VOX, C)
    mean1, inv1, _ = norm_stats(stats1)
    sum_q = jnp.zeros((1, C), f32)
    sum_c = jnp.zeros((1, C), f32)
    for s in range(SLOTS):
        hat = (feat[s].astype(f32) - mean1) * inv1
        n = hat * gain1[...] + bias1[...]
        sg = sigmoid(n)
        q = gaf[s] * slot_weight(active, s) * sg * (1.0 + n * (1.0 - sg)) * gain1[...]
        q1[s] = q
        sum_q = sum_q + jnp.sum(q, axis=0, keepdims=True)
        sum_c = sum_c + jnp.sum(q * hat, axis=0, keepdims=True)
    packed = pack_stats([sum_q, sum_c])

    def store(out, core):
        for chip in range(PEERS // 2):
            p = 2 * chip + core
            out[chip, 0:SHARE] = grad_w1[SHARE * p : SHARE * (p + 1)]
            out[chip, SHARE : 2 * SHARE] = grad_w2[SHARE * p : SHARE * (p + 1)]
            out[chip, SUM_ROW : SUM_ROW + 1] = packed[0:1]
            out[chip, SUM_ROW + 1 : CENTRE_ROW] = jnp.zeros((3, C), f32)
            out[chip, CENTRE_ROW : CENTRE_ROW + 1] = sums1[p : p + 1]
            out[chip, CENTRE_ROW + 1 : CENTRE_ROW + 2] = centre1
            out[chip, CENTRE_ROW + 2 : CENTRE_ROW + 3] = sums2[p : p + 1]
            out[chip, CENTRE_ROW + 3 : CENTRE_ROW + 4] = centre2
            out[chip, CENTRE_ROW + 4 : 120] = jnp.zeros((4, C), f32)

    @pl.when(me % 2 == 0)
    def _():
        store(keep, 0)
        store(give, 1)

    @pl.when(me % 2 == 1)
    def _():
        store(keep, 1)
        store(give, 0)


def pair_kernel(own, other, out):
    def terms(row, count):
        parts = []
        for _ in range(count):
            parts.append(row.astype(bf16).astype(f32))
            row = row - parts[-1]
        return parts

    for n in range(PEERS // 2):
        total = own[n, 0:CENTRE_ROW] + other[n, 0:CENTRE_ROW]
        at = lax.broadcasted_iota(jnp.int32, (CENTRE_ROW, C), 0)
        for k, term in enumerate(terms(total[SUM_ROW : SUM_ROW + 1], 3)):
            total = jnp.where(at == SUM_ROW + k, term, total)
        out[n, 0:CENTRE_ROW] = total.astype(bf16)
        more = jnp.zeros((16, C), f32)
        at = lax.broadcasted_iota(jnp.int32, (16, C), 0)
        for core, ref in enumerate((own, other)):
            rows = ref[n, CENTRE_ROW : CENTRE_ROW + 8]
            lines = terms(rows[0:1], 2) + [rows[1:2]] + terms(rows[2:3], 2) + [rows[3:4]]
            for k, line in enumerate(lines):
                more = jnp.where(at == 6 * core + k, line, more)
        out[n, CENTRE_ROW:ROWS] = more.astype(bf16)


def last_kernel(feat, gout, active, stats1, q1, parts, gain1, grad_in, rows):
    total = parts[0].astype(f32)
    for n in range(1, PEERS // 2):
        total = total + parts[n].astype(f32)
    mean1, inv1, count = norm_stats(stats1)
    packed = jnp.sum(total[SUM_ROW : SUM_ROW + 3], axis=0, keepdims=True)
    packed = jnp.broadcast_to(packed, (8, C))
    mean_q = unpack_stat(packed, 0)[0:1] / count
    mean_c = unpack_stat(packed, 1)[0:1] / count
    for s in range(SLOTS):
        hat = (feat[s].astype(f32) - mean1) * inv1
        back = slot_weight(active, s) * inv1 * (q1[s] - mean_q - hat * mean_c)
        top = jnp.where(active[0, s] > 0, gout[s].astype(f32), 0.0)
        grad_in[s] = (top + back).astype(bf16)
    left = [[], []]
    right = [[], []]
    for n in range(PEERS // 2):
        more = parts[n, CENTRE_ROW:ROWS].astype(f32)
        for core in range(2):
            for weight in range(2):
                first = 6 * core + 3 * weight
                line = more[first + 2 : first + 3]
                left[weight] += [more[first : first + 1], more[first + 1 : first + 2]]
                right[weight] += [line, line]
    for weight in range(2):
        outer = lax.dot_general(
            jnp.concatenate(left[weight], axis=0).astype(bf16),
            jnp.concatenate(right[weight], axis=0).astype(bf16),
            (((0,), (0,)), ((), ())),
            preferred_element_type=f32,
        )
        whole = total[SHARE * weight : SHARE * (weight + 1)] + outer[0:SHARE]
        for n in range(8):
            rows[n, 56 * weight : 56 * weight + SHARE] = whole
            rows[n, 56 * weight + SHARE : 56 * weight + 56] = jnp.zeros((2, C), f32)


vmem = pl.BlockSpec(memory_space=pltpu.VMEM)
smem = pl.BlockSpec(memory_space=pltpu.SMEM)
hbm = pl.BlockSpec(memory_space=pltpu.HBM)


def call(kernel, specs, out_shape, scratch, args, out_specs=None):
    args = [
        pltpu.with_memory_space_constraint(arg, pltpu.HBM) if spec is hbm else arg
        for spec, arg in zip(specs, args)
    ]
    return pl.pallas_call(
        kernel,
        in_specs=specs,
        out_specs=out_specs or [vmem] * len(out_shape),
        out_shape=out_shape,
        scratch_shapes=scratch,
        compiler_params=pltpu.CompilerParams(vmem_limit_bytes=VMEM_BYTES),
    )(*args)


def shape(*dims, dtype=f32):
    return jax.ShapeDtypeStruct(dims, dtype)


def pairs_of(step, first):
    lower = [n for n in range(PEERS) if n // step % 2 == first]
    return [(n, (n + step) % PEERS) for n in lower] + [((n + step) % PEERS, n) for n in lower]


far_pairs = (pairs_of(4, 0), pairs_of(4, 1))
near_pairs = (pairs_of(1, 0), pairs_of(1, 1))


def exchange(fields, stats):
    far = [lax.ppermute(fields, "space", pairs) for pairs in far_pairs]
    stats = spread(stats)
    *far, stats = lax.optimization_barrier((*far, stats))
    three = jnp.stack([fields, *far])
    near = [lax.ppermute(three, "space", pairs) for pairs in near_pairs]
    return [three, *near], stats


def spread(stats):
    return lax.all_to_all(stats, "space", 0, 0, tiled=True)


chip_groups = [list(range(core, PEERS, 2)) for core in range(2)]


def per_device(
    features,
    active,
    neighbor_owner,
    record_position,
    send_list,
    conv_first,
    conv_second,
    gain_first,
    bias_first,
    gain_second,
    bias_second,
    grad_output,
):
    feat = features[0]
    gout = grad_output[0]
    owners = neighbor_owner[0]
    positions = record_position[0]
    lists = send_list[0].transpose(2, 0, 1)
    gain1, bias1 = gain_first.reshape(1, C), bias_first.reshape(1, C)
    gain2, bias2 = gain_second.reshape(1, C), bias_second.reshape(1, C)
    field = (SLOTS, VOX, C)
    wide = pltpu.VMEM(field, f32)
    two = pltpu.VMEM((2, *field), f32)
    scratch = pltpu.VMEM((2, 2, *field), f32)
    table = pltpu.VMEM((LANES * PLANES, PLANE, C), f32)
    pad = pltpu.VMEM((SLOTS, 6, 6, 8, C), f32)
    cols_shape = (9, SLOTS, 6, PLANE, C)
    cols = pltpu.VMEM(cols_shape, bf16)

    stats1, both = call(
        start_kernel,
        [hbm, hbm, hbm, hbm],
        [shape(PEERS, C), shape(2, *field, dtype=bf16)],
        [
            pltpu.SMEM((1, SLOTS), jnp.int32),
            pltpu.VMEM((CAP, 1, PEERS), jnp.int32),
            pltpu.SemaphoreType.DMA((4,)),
        ],
        (feat, gout, active, lists),
    )
    fields0, stats1 = exchange(both, stats1)

    middle, gas, cols_a, both, index = call(
        first_kernel,
        [hbm] * 7 + [vmem] * 4,
        [shape(*field), shape(*field), shape(*cols_shape, dtype=bf16)]
        + [shape(2, *field, dtype=bf16), shape(SLOTS, 26, dtype=jnp.int32)],
        [table, table, pad, cols, wide, scratch, pltpu.VMEM((PEERS, C), jnp.int32)]
        + [
            pltpu.SMEM((1, SLOTS), jnp.int32),
            pltpu.SMEM((SLOTS, 26), jnp.int32),
            pltpu.SMEM((SLOTS, 26), jnp.int32),
            pltpu.SMEM((PEERS, C), jnp.int32),
            pltpu.VMEM((1, C), f32),
            pltpu.VMEM((1, C), f32),
            pltpu.VMEM((27, C, C), bf16),
            pltpu.VMEM((27, C, C), bf16),
            pltpu.SemaphoreType.DMA((8,)),
        ],
        (active, owners, positions, gain1, bias1, conv_first, conv_second, stats1, *fields0),
        [vmem] * 4 + [smem],
    )
    (stats2,) = call(sums_kernel, [smem, vmem], [shape(PEERS, C)], [], (active, middle))
    fields1, stats2 = exchange(both, stats2)

    (stats3,) = call(
        second_kernel,
        [smem] + [vmem] * 5,
        [shape(PEERS, C)],
        [],
        (active, middle, gas, stats2, gain2, bias2),
    )
    stats3 = spread(stats3)

    weight = pltpu.VMEM((27 * C, C), f32)
    line = pltpu.VMEM((PEERS, C), f32)
    block, q1, keep, give = call(
        third_kernel,
        [vmem, vmem, smem, smem] + [vmem] * 15,
        [shape(*field, dtype=bf16), shape(*field)] + [shape(PEERS // 2, 120, C)] * 2,
        [table, table, pad, cols, wide, two, scratch, weight, weight, line, line],
        (feat, gout, active, index, middle, gas, stats1, stats2, stats3)
        + (gain1, bias1, gain2, bias2, conv_first, conv_second, cols_a, *fields1),
    )
    other = lax.ppermute(give, "space", near_pairs[0])
    (share,) = call(
        pair_kernel,
        [vmem, vmem],
        [shape(PEERS // 2, ROWS, C, dtype=bf16)],
        [],
        (keep, other),
    )
    share = lax.all_to_all(share, "space", 0, 0, axis_index_groups=chip_groups)

    grad_in, rows = call(
        last_kernel,
        [vmem, vmem, smem] + [vmem] * 4,
        [shape(*field, dtype=bf16), shape(8, 112, C)],
        [],
        (feat, gout, active, stats1, q1, share, gain1),
    )
    rows = lax.all_to_all(rows, "scene", 0, 0)
    rows = jnp.sum(rows, axis=0).astype(bf16)
    return (block[None], grad_in[None], rows[:SHARE], rows[56 : 56 + SHARE])


def solution(mesh):
    return jax.shard_map(
        per_device,
        mesh=mesh,
        in_specs=(
            P("scene", "space", None, None),
            P("scene", "space"),
            P("scene", "space", None),
            P("scene", "space", None),
            P("scene", "space", None, None),
            P(),
            P(),
            P(),
            P(),
            P(),
            P(),
            P("scene", "space", None, None),
        ),
        out_specs=(
            P("scene", "space", None, None),
            P("scene", "space", None, None),
            P("space", None),
            P("space", None),
        ),
        check_vma=False,
    )
```

```python
import jax
import jax.numpy as jnp
from jax import lax
from jax.experimental import pallas as pl
from jax.experimental.pallas import tpu as pltpu
from jax.sharding import PartitionSpec as P

EDGE = 4
SLOTS = 4
VOX = 64
C = 128
CAP = 10
PEERS = 64
PLANE = 16
SHARE = 54
ROWS = 128
SUM_ROW = 108
CENTRE_ROW = 112
GROUP_COUNT = 64 * 4
EPS = 1e-05

directions = [
    (ordinal // 9 - 1, ordinal // 3 % 3 - 1, ordinal % 3 - 1)
    for ordinal in range(27)
    if ordinal != 13
]
PLANES = 24
LANES = 11
ZERO_PLANE = 3 * PLANES

f32 = jnp.float32
bf16 = jnp.bfloat16
VMEM_BYTES = 40 * 1024 * 1024


def group_total(row):
    lane = lax.broadcasted_iota(jnp.int32, row.shape, 1)
    row = row + jnp.where(lane % 2 == 0, pltpu.roll(row, C - 1, 1), pltpu.roll(row, 1, 1))
    return row + jnp.where(lane % 4 < 2, pltpu.roll(row, C - 2, 1), pltpu.roll(row, 2, 1))


def pack_stats(rows):
    rows = [jnp.broadcast_to(row, (8, C)) for row in rows]
    lane = lax.broadcasted_iota(jnp.int32, (8, C), 1)
    packed = jnp.zeros((8, C), f32)
    for n, row in enumerate(rows):
        packed = jnp.where(lane % 4 == n, group_total(row), packed)
    return packed


def unpack_stat(packed, n):
    lane = lax.broadcasted_iota(jnp.int32, packed.shape, 1)
    return group_total(jnp.where(lane % 4 == n, packed, 0.0))


def total_of(stats_ref):
    return jnp.broadcast_to(jnp.sum(stats_ref[...], axis=0, keepdims=True), (8, C))


def norm_stats(stats_ref):
    packed = total_of(stats_ref)
    count = unpack_stat(packed, 2) * (GROUP_COUNT / 4)
    mean = unpack_stat(packed, 0) / count
    inv = lax.rsqrt(unpack_stat(packed, 1) / count - mean * mean + EPS)
    return mean[0:1], inv[0:1], count[0:1]


def sigmoid(n):
    return 1.0 / (1.0 + jnp.exp(-n))


def terms(row, count):
    parts = []
    for _ in range(count):
        parts.append(row.astype(bf16).astype(f32))
        row = row - parts[-1]
    return parts


def slot_weight(active_ref, s):
    return active_ref[0, s].astype(f32)


def planes_of(src, dst, start):
    for s in range(SLOTS):
        dst[start + 6 * s] = src[s, 0:16]
        dst[start + 6 * s + 1] = src[s, 48:64]
        for a in range(4):
            dst[start + 6 * s + 2, 4 * a : 4 * a + 4] = src[s, 16 * a : 16 * a + 4]
            dst[start + 6 * s + 3, 4 * a : 4 * a + 4] = src[s, 16 * a + 12 : 16 * a + 16]
        dst[start + 6 * s + 4] = src[s, pl.ds(0, 16, stride=4)]
        dst[start + 6 * s + 5] = src[s, pl.ds(3, 16, stride=4)]


def far_distance(device):
    return 4 - 8 * ((device >> 2) & 1)


def near_distance(device):
    return 1 - 2 * (device & 1)


def fill_tables(tables, fields, scratch, me, make):
    near = near_distance(me)
    turn = 0
    for ref, base in zip(fields, (0, near, -near)):
        far = far_distance((me + base) & (PEERS - 1))
        for entry, more in enumerate((0, far, -far)):
            start = (base + more + 5) * PLANES
            buffer = scratch.at[turn % 2]
            turn += 1
            for s in range(SLOTS):
                for t, value in enumerate(make(ref.at[entry], s)):
                    buffer[t, s] = value
            for t, table in enumerate(tables):
                planes_of(buffer.at[t], table, start)
    for table in tables:
        table[ZERO_PLANE] = jnp.zeros((PLANE, C), f32)


def find_planes(owners, positions, ids, index, me):
    def one_slot(s, carry):
        for n in range(26):
            owner = owners[s, n]
            plane = ids[jnp.maximum(owner, 0), 4 * positions[s, n] + 3]
            plane = jnp.clip(plane, 0, PLANES - 1)
            index[s, n] = jnp.where(
                owner >= 0, (owner - me + 5) * PLANES + plane, ZERO_PLANE
            )
        return carry

    lax.fori_loop(0, SLOTS, one_slot, 0)


def fetch(sources, targets, sems):
    copies = [
        pltpu.make_async_copy(source, target, sems.at[n])
        for n, (source, target) in enumerate(zip(sources, targets))
    ]
    for copy in copies:
        copy.start()
    return copies


def place_halo(pad, table, index_ref):
    def one_slot(s, carry):
        for n, (d0, d1, d2) in enumerate(directions):
            index = index_ref[s, n]
            cells = [(5 if d > 0 else 0, 0 if d > 0 else 3) for d in (d0, d1, d2)]
            (a_to, _), (b_to, b_from), (c_to, c_from) = cells

            def row(r, count=1):
                return table[index, r : r + count]

            if d0 != 0:
                if d1 == 0 and d2 == 0:
                    for b in range(4):
                        pad[s, a_to, 1 + b, 1:5] = row(4 * b, 4)
                elif d2 == 0:
                    pad[s, a_to, b_to, 1:5] = row(4 * b_from, 4)
                elif d1 == 0:
                    for b in range(4):
                        pad[s, a_to, 1 + b, c_to : c_to + 1] = row(4 * b + c_from)
                else:
                    pad[s, a_to, b_to, c_to : c_to + 1] = row(4 * b_from + c_from)
            elif d1 != 0:
                for a in range(4):
                    if d2 == 0:
                        pad[s, 1 + a, b_to, 1:5] = row(4 * a, 4)
                    else:
                        pad[s, 1 + a, b_to, c_to : c_to + 1] = row(4 * a + c_from)
            else:
                for a in range(4):
                    for b in range(4):
                        pad[s, 1 + a, 1 + b, c_to : c_to + 1] = row(4 * a + b)
        return carry

    lax.fori_loop(0, SLOTS, one_slot, 0)


def place_interior(pad, field):
    for s in range(SLOTS):
        for a in range(4):
            for b in range(4):
                pad[s, 1 + a, 1 + b, 1:5] = field[s, 16 * a + 4 * b : 16 * a + 4 * b + 4]


def windows_of(pad, cols):
    flat = pad.reshape(SLOTS * 6 * 6 * 8, C)
    sub = lax.broadcasted_iota(jnp.int32, (8, C), 0)
    for t in range(SLOTS * 6):
        s, a = t // 6, t % 6
        for k2 in range(3):
            starts = [(6 * t + b) * 8 + k2 for b in range(5)]
            pair = [
                jnp.where(sub < 4, flat[first : first + 8], flat[first + 4 : first + 12])
                for first in starts
            ]
            for k1 in range(3):
                tile = jnp.concatenate([pair[k1], pair[k1 + 2]], axis=0)
                cols[3 * k1 + k2, s, a] = tile.astype(bf16)


def window(cols, k0, k1, k2):
    return cols[3 * k1 + k2, :, k0 : k0 + 4].reshape(SLOTS * VOX, C)


def conv(cols, weight):
    total = jnp.zeros((SLOTS * VOX, C), f32)
    for k0 in range(3):
        left = jnp.concatenate([window(cols, k0, j // 3, j % 3) for j in range(9)], axis=1)
        right = weight[9 * k0 : 9 * k0 + 9].reshape(9 * C, C)
        total = total + jnp.dot(left, right, preferred_element_type=f32)
    return total


def conv_back(cols, weight):
    total = jnp.zeros((SLOTS * VOX, C), f32)
    for k0 in range(3):
        left = jnp.concatenate(
            [window(cols, 2 - k0, 2 - j // 3, 2 - j % 3) for j in range(9)], axis=1
        )
        right = jnp.concatenate([weight[9 * k0 + j] for j in range(9)], axis=1)
        total = total + lax.dot_general(
            left, right, (((1,), (1,)), ((), ())), preferred_element_type=f32
        )
    return total


def weight_grad(cols, grad, centre, out):
    right = jnp.concatenate([grad, jnp.ones((SLOTS * VOX, C), bf16)], axis=1)
    for k0 in range(3):
        left = jnp.concatenate([window(cols, k0, j // 3, j % 3) for j in range(9)], axis=1)
        both = lax.dot_general(
            left, right, (((0,), (0,)), ((), ())), preferred_element_type=f32
        )
        out[9 * C * k0 : 9 * C * (k0 + 1)] = both[:, :C] - both[:, C:] * centre


def window_sums(cols):
    ones = jnp.ones((8, SLOTS * VOX), bf16)
    rows = []
    for k0 in range(3):
        left = jnp.concatenate([window(cols, k0, j // 3, j % 3) for j in range(9)], axis=1)
        total = jnp.dot(ones, left, preferred_element_type=f32)
        rows += [total[0:1, C * j : C * (j + 1)] for j in range(9)]
    return rows


def store_shares(rows, out):
    lane = lax.broadcasted_iota(jnp.int32, (1, C), 1)
    for p in range(PEERS):
        k, skip = divmod(SHARE * p, C)
        line = rows[k] if skip == 0 else pltpu.roll(rows[k], C - skip, 1)
        if skip + SHARE > C:
            line = jnp.where(lane < C - skip, line, pltpu.roll(rows[k + 1], C - skip, 1))
        out[p : p + 1] = jnp.where(lane < SHARE, line, 0.0)


def centre_of(field, active):
    total = jnp.zeros((1, C), f32)
    slots = 0.0
    for s in range(SLOTS):
        total = total + jnp.sum(field[s], axis=0, keepdims=True)
        slots = slots + slot_weight(active, s)
    return (total / (jnp.maximum(slots, 1.0) * VOX)).astype(bf16).astype(f32)


def start_kernel(feat_in, gout_in, active_in, list_in, stats, both, active, send_list, sems):
    feat, gout = both.at[0], both.at[1]
    copies = fetch(
        (active_in, list_in, feat_in, gout_in), (active, send_list, feat, gout), sems
    )
    for copy in copies:
        copy.wait()
    total = jnp.zeros((1, C), f32)
    squares = jnp.zeros((1, C), f32)
    slots = 0.0
    for s in range(SLOTS):
        w = slot_weight(active, s)
        x = feat[s].astype(f32)
        total = total + w * jnp.sum(x, axis=0, keepdims=True)
        squares = squares + w * jnp.sum(x * x, axis=0, keepdims=True)
        slots = slots + w
    packed = pack_stats([total, squares, jnp.full((1, C), slots, f32)])
    record = lax.broadcasted_iota(jnp.int32, (CAP, C), 0)
    lane = lax.broadcasted_iota(jnp.int32, (CAP, C), 1)
    select = jnp.where(lane == 4 * record + 3, 1.0, 0.0).astype(bf16)
    ids = lax.dot_general(
        send_list[:, 0].astype(bf16),
        select,
        (((0,), (0,)), ((), ())),
        preferred_element_type=f32,
    )
    stats[...] = ids + packed[0:1]


def first_kernel(
    active_in, own_in, pos_in, gain_in, bias_in, w1_in, w2_in, stats1, *rest
):
    fields, rest = rest[:3], rest[3:]
    middle, gas, cols_a, both, index = rest[:5]
    table_f, table_g, pad, cols_g, act, scratch, ids_v = rest[5:12]
    active, owners, positions, ids, gain1, bias1, w1, w2, sems = rest[12:]
    me = lax.axis_index("space")
    copies = fetch(
        (gain_in, bias_in, active_in, own_in, pos_in, w1_in, w2_in),
        (gain1, bias1, active, owners, positions, w1, w2),
        sems,
    )
    ids_v[...] = stats1[...].astype(jnp.int32)
    ids_copy = pltpu.make_async_copy(ids_v, ids, sems.at[7])
    ids_copy.start()
    feat, gout = fields[0].at[0, 0], fields[0].at[0, 1]
    mean, inv, _ = norm_stats(stats1)
    copies[0].wait()
    copies[1].wait()

    def act_of(x):
        n = (x - mean) * inv * gain1[...] + bias1[...]
        return n * sigmoid(n)

    fill_tables(
        (table_f, table_g),
        fields,
        scratch,
        me,
        lambda ref, s: (act_of(ref[0, s].astype(f32)), ref[1, s].astype(f32)),
    )
    for copy in copies[2:5]:
        copy.wait()
    ids_copy.wait()
    find_planes(owners, positions, ids, index, me)
    for s in range(SLOTS):
        act[s] = slot_weight(active, s) * act_of(feat[s].astype(f32))
    place_interior(pad, act)
    place_halo(pad, table_f, index)
    windows_of(pad, cols_a)
    copies[5].wait()
    middle[...] = conv(cols_a, w1).reshape(SLOTS, VOX, C)
    for s in range(SLOTS):
        act[s] = jnp.where(active[0, s] > 0, gout[s].astype(f32), 0.0)
    place_interior(pad, act)
    place_halo(pad, table_g, index)
    windows_of(pad, cols_g)
    copies[6].wait()
    gas[...] = conv_back(cols_g, w2).reshape(SLOTS, VOX, C)
    both[0] = middle[...].astype(bf16)
    both[1] = gas[...].astype(bf16)


def sums_kernel(active, middle, stats2):
    total = jnp.zeros((1, C), f32)
    squares = jnp.zeros((1, C), f32)
    slots = 0.0
    for s in range(SLOTS):
        w = slot_weight(active, s)
        x = middle[s]
        total = total + w * jnp.sum(x, axis=0, keepdims=True)
        squares = squares + w * jnp.sum(x * x, axis=0, keepdims=True)
        slots = slots + w
    packed = pack_stats([total, squares, jnp.full((1, C), slots, f32)])
    stats2[...] = jnp.broadcast_to(packed[0:1], (PEERS, C))


def second_kernel(active, middle, gas, stats2, gain2, bias2, stats3):
    mean, inv, _ = norm_stats(stats2)
    gain = gain2[...]
    sum_q = jnp.zeros((1, C), f32)
    sum_c = jnp.zeros((1, C), f32)
    for s in range(SLOTS):
        hat = (middle[s] - mean) * inv
        n = hat * gain + bias2[...]
        sg = sigmoid(n)
        q = gas[s] * slot_weight(active, s) * sg * (1.0 + n * (1.0 - sg)) * gain
        sum_q = sum_q + jnp.sum(q, axis=0, keepdims=True)
        sum_c = sum_c + jnp.sum(q * hat, axis=0, keepdims=True)
    packed = pack_stats([sum_q, sum_c])
    stats3[...] = jnp.broadcast_to(packed[0:1], (PEERS, C))


def third_kernel(
    feat,
    gout,
    active,
    index,
    middle,
    gas,
    stats1,
    stats2,
    stats3,
    gain1,
    bias1,
    gain2,
    bias2,
    w1,
    w2,
    cols_a,
    *rest,
):
    fields, rest = rest[:3], rest[3:]
    block, q1, keep, give = rest[:4]
    table_a, table_g, pad, cols, field, own, scratch = rest[4:11]
    grad_w1, grad_w2, sums1, sums2 = rest[11:]
    me = lax.axis_index("space")
    mean, inv, count = norm_stats(stats2)
    gain = gain2[...]
    bias = bias2[...]
    packed = total_of(stats3)
    mean_q = unpack_stat(packed, 0)[0:1] / count
    mean_c = unpack_stat(packed, 1)[0:1] / count

    def both_of(x, g):
        hat = (x - mean) * inv
        n = hat * gain + bias
        sg = sigmoid(n)
        q = g * sg * (1.0 + n * (1.0 - sg)) * gain
        grad = inv * (q - mean_q - hat * mean_c)
        return n * sg, grad.astype(bf16).astype(f32)

    fill_tables(
        (table_a, table_g),
        fields,
        scratch,
        me,
        lambda ref, s: both_of(ref[0, s].astype(f32), ref[1, s].astype(f32)),
    )
    for s in range(SLOTS):
        act, grad = both_of(middle[s], gas[s])
        own[0, s] = slot_weight(active, s) * act
        own[1, s] = slot_weight(active, s) * grad
    place_interior(pad, own.at[0])
    place_halo(pad, table_a, index)
    windows_of(pad, cols)
    out = conv(cols, w2).reshape(SLOTS, VOX, C)
    for s in range(SLOTS):
        w = slot_weight(active, s)
        block[s] = ((feat[s].astype(f32) + out[s]) * w).astype(bf16)
        field[s] = jnp.where(active[0, s] > 0, gout[s].astype(f32), 0.0)
    store_shares(window_sums(cols), sums2)
    centre2 = centre_of(field, active)
    weight_grad(cols, field[...].astype(bf16).reshape(SLOTS * VOX, C), centre2, grad_w2)
    store_shares(window_sums(cols_a), sums1)
    centre1 = centre_of(own.at[1], active)
    weight_grad(cols_a, own[1].astype(bf16).reshape(SLOTS * VOX, C), centre1, grad_w1)
    place_interior(pad, own.at[1])
    place_halo(pad, table_g, index)
    windows_of(pad, cols)
    gaf = conv_back(cols, w1).reshape(SLOTS, VOX, C)
    mean1, inv1, _ = norm_stats(stats1)
    sum_q = jnp.zeros((1, C), f32)
    sum_c = jnp.zeros((1, C), f32)
    for s in range(SLOTS):
        hat = (feat[s].astype(f32) - mean1) * inv1
        n = hat * gain1[...] + bias1[...]
        sg = sigmoid(n)
        q = gaf[s] * slot_weight(active, s) * sg * (1.0 + n * (1.0 - sg)) * gain1[...]
        q1[s] = q
        sum_q = sum_q + jnp.sum(q, axis=0, keepdims=True)
        sum_c = sum_c + jnp.sum(q * hat, axis=0, keepdims=True)
    packed = pack_stats([sum_q, sum_c])
    sums = jnp.concatenate(terms(packed[0:1], 3), axis=0)

    def store(out, core):
        kind = out.dtype
        for chip in range(PEERS // 2):
            p = 2 * chip + core
            rows = [
                grad_w1[SHARE * p : SHARE * (p + 1)],
                grad_w2[SHARE * p : SHARE * (p + 1)],
                sums,
                jnp.zeros((1, C), f32),
            ]
            out[chip, 0:CENTRE_ROW] = jnp.concatenate(rows, axis=0).astype(kind)
            rows = [*terms(sums1[p : p + 1], 2), centre1, *terms(sums2[p : p + 1], 2), centre2]
            rows = jnp.concatenate([*rows, jnp.zeros((10, C), f32)], axis=0)
            out[chip, CENTRE_ROW:ROWS] = rows.astype(kind)

    @pl.when(me % 2 == 0)
    def _():
        store(keep, 0)
        store(give, 1)

    @pl.when(me % 2 == 1)
    def _():
        store(keep, 1)
        store(give, 0)


def pair_kernel(own, other, out):
    at = lax.broadcasted_iota(jnp.int32, (CENTRE_ROW, C), 0)
    for n in range(PEERS // 2):
        total = own[n, 0:CENTRE_ROW] + other[n, 0:CENTRE_ROW].astype(f32)
        row = jnp.sum(total[SUM_ROW : SUM_ROW + 3], axis=0, keepdims=True)
        for k, term in enumerate(terms(row, 3)):
            total = jnp.where(at == SUM_ROW + k, term, total)
        out[n, 0:CENTRE_ROW] = total.astype(bf16)
        more = other[n, CENTRE_ROW:ROWS].astype(f32)
        more = own[n, CENTRE_ROW:ROWS] + pltpu.roll(more, 6, 0)
        out[n, CENTRE_ROW:ROWS] = more.astype(bf16)


def last_kernel(feat, gout, active, stats1, q1, parts, gain1, grad_in, rows):
    total = parts[0].astype(f32)
    for n in range(1, PEERS // 2):
        total = total + parts[n].astype(f32)
    mean1, inv1, count = norm_stats(stats1)
    packed = jnp.sum(total[SUM_ROW : SUM_ROW + 3], axis=0, keepdims=True)
    packed = jnp.broadcast_to(packed, (8, C))
    mean_q = unpack_stat(packed, 0)[0:1] / count
    mean_c = unpack_stat(packed, 1)[0:1] / count
    for s in range(SLOTS):
        hat = (feat[s].astype(f32) - mean1) * inv1
        back = slot_weight(active, s) * inv1 * (q1[s] - mean_q - hat * mean_c)
        top = jnp.where(active[0, s] > 0, gout[s].astype(f32), 0.0)
        grad_in[s] = (top + back).astype(bf16)
    left = [[], []]
    right = [[], []]
    for n in range(PEERS // 2):
        more = parts[n, CENTRE_ROW:ROWS].astype(f32)
        for core in range(2):
            for weight in range(2):
                first = 6 * core + 3 * weight
                line = more[first + 2 : first + 3]
                left[weight] += [more[first : first + 1], more[first + 1 : first + 2]]
                right[weight] += [line, line]
    for weight in range(2):
        outer = lax.dot_general(
            jnp.concatenate(left[weight], axis=0).astype(bf16),
            jnp.concatenate(right[weight], axis=0).astype(bf16),
            (((0,), (0,)), ((), ())),
            preferred_element_type=f32,
        )
        whole = total[SHARE * weight : SHARE * (weight + 1)] + outer[0:SHARE]
        for n in range(8):
            rows[n, 56 * weight : 56 * weight + SHARE] = whole
            rows[n, 56 * weight + SHARE : 56 * weight + 56] = jnp.zeros((2, C), f32)


vmem = pl.BlockSpec(memory_space=pltpu.VMEM)
smem = pl.BlockSpec(memory_space=pltpu.SMEM)
hbm = pl.BlockSpec(memory_space=pltpu.HBM)


def call(kernel, specs, out_shape, scratch, args, out_specs=None):
    args = [
        pltpu.with_memory_space_constraint(arg, pltpu.HBM) if spec is hbm else arg
        for spec, arg in zip(specs, args)
    ]
    return pl.pallas_call(
        kernel,
        in_specs=specs,
        out_specs=out_specs or [vmem] * len(out_shape),
        out_shape=out_shape,
        scratch_shapes=scratch,
        compiler_params=pltpu.CompilerParams(vmem_limit_bytes=VMEM_BYTES),
    )(*args)


def shape(*dims, dtype=f32):
    return jax.ShapeDtypeStruct(dims, dtype)


def pairs_of(step, first):
    lower = [n for n in range(PEERS) if n // step % 2 == first]
    return [(n, (n + step) % PEERS) for n in lower] + [((n + step) % PEERS, n) for n in lower]


far_pairs = (pairs_of(4, 0), pairs_of(4, 1))
near_pairs = (pairs_of(1, 0), pairs_of(1, 1))


def exchange(fields, stats):
    far = [lax.ppermute(fields, "space", pairs) for pairs in far_pairs]
    stats = spread(stats)
    *far, stats = lax.optimization_barrier((*far, stats))
    three = jnp.stack([fields, *far])
    near = [lax.ppermute(three, "space", pairs) for pairs in near_pairs]
    return [three, *near], stats


def spread(stats):
    return lax.all_to_all(stats, "space", 0, 0, tiled=True)


chip_groups = [list(range(core, PEERS, 2)) for core in range(2)]


def per_device(
    features,
    active,
    neighbor_owner,
    record_position,
    send_list,
    conv_first,
    conv_second,
    gain_first,
    bias_first,
    gain_second,
    bias_second,
    grad_output,
):
    feat = features[0]
    gout = grad_output[0]
    owners = neighbor_owner[0]
    positions = record_position[0]
    lists = send_list[0].transpose(2, 0, 1)
    gain1, bias1 = gain_first.reshape(1, C), bias_first.reshape(1, C)
    gain2, bias2 = gain_second.reshape(1, C), bias_second.reshape(1, C)
    field = (SLOTS, VOX, C)
    wide = pltpu.VMEM(field, f32)
    two = pltpu.VMEM((2, *field), f32)
    scratch = pltpu.VMEM((2, 2, *field), f32)
    table = pltpu.VMEM((LANES * PLANES, PLANE, C), f32)
    pad = pltpu.VMEM((SLOTS, 6, 6, 8, C), f32)
    cols_shape = (9, SLOTS, 6, PLANE, C)
    cols = pltpu.VMEM(cols_shape, bf16)

    stats1, both = call(
        start_kernel,
        [hbm, hbm, hbm, hbm],
        [shape(PEERS, C), shape(2, *field, dtype=bf16)],
        [
            pltpu.SMEM((1, SLOTS), jnp.int32),
            pltpu.VMEM((CAP, 1, PEERS), jnp.int32),
            pltpu.SemaphoreType.DMA((4,)),
        ],
        (feat, gout, active, lists),
    )
    fields0, stats1 = exchange(both, stats1)

    middle, gas, cols_a, both, index = call(
        first_kernel,
        [hbm] * 7 + [vmem] * 4,
        [shape(*field), shape(*field), shape(*cols_shape, dtype=bf16)]
        + [shape(2, *field, dtype=bf16), shape(SLOTS, 26, dtype=jnp.int32)],
        [table, table, pad, cols, wide, scratch, pltpu.VMEM((PEERS, C), jnp.int32)]
        + [
            pltpu.SMEM((1, SLOTS), jnp.int32),
            pltpu.SMEM((SLOTS, 26), jnp.int32),
            pltpu.SMEM((SLOTS, 26), jnp.int32),
            pltpu.SMEM((PEERS, C), jnp.int32),
            pltpu.VMEM((1, C), f32),
            pltpu.VMEM((1, C), f32),
            pltpu.VMEM((27, C, C), bf16),
            pltpu.VMEM((27, C, C), bf16),
            pltpu.SemaphoreType.DMA((8,)),
        ],
        (active, owners, positions, gain1, bias1, conv_first, conv_second, stats1, *fields0),
        [vmem] * 4 + [smem],
    )
    (stats2,) = call(sums_kernel, [smem, vmem], [shape(PEERS, C)], [], (active, middle))
    fields1, stats2 = exchange(both, stats2)

    (stats3,) = call(
        second_kernel,
        [smem] + [vmem] * 5,
        [shape(PEERS, C)],
        [],
        (active, middle, gas, stats2, gain2, bias2),
    )
    stats3 = spread(stats3)

    weight = pltpu.VMEM((27 * C, C), f32)
    line = pltpu.VMEM((PEERS, C), f32)
    block, q1, keep, give = call(
        third_kernel,
        [vmem, vmem, smem, smem] + [vmem] * 15,
        [shape(*field, dtype=bf16), shape(*field)]
        + [shape(PEERS // 2, ROWS, C), shape(PEERS // 2, ROWS, C, dtype=bf16)],
        [table, table, pad, cols, wide, two, scratch, weight, weight, line, line],
        (feat, gout, active, index, middle, gas, stats1, stats2, stats3)
        + (gain1, bias1, gain2, bias2, conv_first, conv_second, cols_a, *fields1),
    )
    other = lax.ppermute(give, "space", near_pairs[0])
    (share,) = call(
        pair_kernel,
        [vmem, vmem],
        [shape(PEERS // 2, ROWS, C, dtype=bf16)],
        [],
        (keep, other),
    )
    share = lax.all_to_all(share, "space", 0, 0, axis_index_groups=chip_groups)

    grad_in, rows = call(
        last_kernel,
        [vmem, vmem, smem] + [vmem] * 4,
        [shape(*field, dtype=bf16), shape(8, 112, C)],
        [],
        (feat, gout, active, stats1, q1, share, gain1),
    )
    rows = lax.all_to_all(rows, "scene", 0, 0)
    rows = jnp.sum(rows, axis=0).astype(bf16)
    return (block[None], grad_in[None], rows[:SHARE], rows[56 : 56 + SHARE])


def solution(mesh):
    return jax.shard_map(
        per_device,
        mesh=mesh,
        in_specs=(
            P("scene", "space", None, None),
            P("scene", "space"),
            P("scene", "space", None),
            P("scene", "space", None),
            P("scene", "space", None, None),
            P(),
            P(),
            P(),
            P(),
            P(),
            P(),
            P("scene", "space", None, None),
        ),
        out_specs=(
            P("scene", "space", None, None),
            P("scene", "space", None, None),
            P("space", None),
            P("space", None),
        ),
        check_vma=False,
    )
```

```python
import jax
import jax.numpy as jnp
from jax import lax
from jax.experimental import pallas as pl
from jax.experimental.pallas import tpu as pltpu
from jax.sharding import PartitionSpec as P

EDGE = 4
SLOTS = 4
VOX = 64
C = 128
CAP = 10
PEERS = 64
PLANE = 16
SHARE = 54
ROWS = 120
SUM_ROW = 108
CENTRE_ROW = 112
GROUP_COUNT = 64 * 4
EPS = 1e-05

directions = [
    (ordinal // 9 - 1, ordinal // 3 % 3 - 1, ordinal % 3 - 1)
    for ordinal in range(27)
    if ordinal != 13
]
PLANES = 24
LANES = 11
ZERO_PLANE = 3 * PLANES

f32 = jnp.float32
bf16 = jnp.bfloat16
VMEM_BYTES = 40 * 1024 * 1024


def group_total(row):
    lane = lax.broadcasted_iota(jnp.int32, row.shape, 1)
    row = row + jnp.where(lane % 2 == 0, pltpu.roll(row, C - 1, 1), pltpu.roll(row, 1, 1))
    return row + jnp.where(lane % 4 < 2, pltpu.roll(row, C - 2, 1), pltpu.roll(row, 2, 1))


def pack_stats(rows):
    rows = [jnp.broadcast_to(row, (8, C)) for row in rows]
    lane = lax.broadcasted_iota(jnp.int32, (8, C), 1)
    packed = jnp.zeros((8, C), f32)
    for n, row in enumerate(rows):
        packed = jnp.where(lane % 4 == n, group_total(row), packed)
    return packed


def unpack_stat(packed, n):
    lane = lax.broadcasted_iota(jnp.int32, packed.shape, 1)
    return group_total(jnp.where(lane % 4 == n, packed, 0.0))


def total_of(stats_ref):
    return jnp.broadcast_to(jnp.sum(stats_ref[...], axis=0, keepdims=True), (8, C))


def norm_stats(stats_ref):
    packed = total_of(stats_ref)
    count = unpack_stat(packed, 2) * (GROUP_COUNT / 4)
    mean = unpack_stat(packed, 0) / count
    inv = lax.rsqrt(unpack_stat(packed, 1) / count - mean * mean + EPS)
    return mean[0:1], inv[0:1], count[0:1]


def sigmoid(n):
    return 1.0 / (1.0 + jnp.exp(-n))


def terms(row, count):
    parts = []
    for _ in range(count):
        parts.append(row.astype(bf16).astype(f32))
        row = row - parts[-1]
    return parts


def slot_weight(active_ref, s):
    return active_ref[0, s].astype(f32)


def planes_of(src, dst, start):
    for s in range(SLOTS):
        dst[start + 6 * s] = src[s, 0:16]
        dst[start + 6 * s + 1] = src[s, 48:64]
        for a in range(4):
            dst[start + 6 * s + 2, 4 * a : 4 * a + 4] = src[s, 16 * a : 16 * a + 4]
            dst[start + 6 * s + 3, 4 * a : 4 * a + 4] = src[s, 16 * a + 12 : 16 * a + 16]
        dst[start + 6 * s + 4] = src[s, pl.ds(0, 16, stride=4)]
        dst[start + 6 * s + 5] = src[s, pl.ds(3, 16, stride=4)]


def far_distance(device):
    return 4 - 8 * ((device >> 2) & 1)


def near_distance(device):
    return 1 - 2 * (device & 1)


def fill_tables(tables, fields, scratch, me, make):
    near = near_distance(me)
    turn = 0
    for ref, base in zip(fields, (0, near, -near)):
        far = far_distance((me + base) & (PEERS - 1))
        for entry, more in enumerate((0, far, -far)):
            start = (base + more + 5) * PLANES
            buffer = scratch.at[turn % 2]
            turn += 1
            for s in range(SLOTS):
                for t, value in enumerate(make(ref.at[entry], s)):
                    buffer[t, s] = value
            for t, table in enumerate(tables):
                planes_of(buffer.at[t], table, start)
    for table in tables:
        table[ZERO_PLANE] = jnp.zeros((PLANE, C), f32)


def find_planes(owners, positions, ids, index, me):
    def one_slot(s, carry):
        for n in range(26):
            owner = owners[s, n]
            plane = ids[jnp.maximum(owner, 0), 4 * positions[s, n] + 3]
            plane = jnp.clip(plane, 0, PLANES - 1)
            index[s, n] = jnp.where(
                owner >= 0, (owner - me + 5) * PLANES + plane, ZERO_PLANE
            )
        return carry

    lax.fori_loop(0, SLOTS, one_slot, 0)


def fetch(sources, targets, sems):
    copies = [
        pltpu.make_async_copy(source, target, sems.at[n])
        for n, (source, target) in enumerate(zip(sources, targets))
    ]
    for copy in copies:
        copy.start()
    return copies


def place_halo(pad, table, index_ref):
    def one_slot(s, carry):
        for n, (d0, d1, d2) in enumerate(directions):
            index = index_ref[s, n]
            cells = [(5 if d > 0 else 0, 0 if d > 0 else 3) for d in (d0, d1, d2)]
            (a_to, _), (b_to, b_from), (c_to, c_from) = cells

            def row(r, count=1):
                return table[index, r : r + count]

            if d0 != 0:
                if d1 == 0 and d2 == 0:
                    for b in range(4):
                        pad[s, a_to, 1 + b, 1:5] = row(4 * b, 4)
                elif d2 == 0:
                    pad[s, a_to, b_to, 1:5] = row(4 * b_from, 4)
                elif d1 == 0:
                    for b in range(4):
                        pad[s, a_to, 1 + b, c_to : c_to + 1] = row(4 * b + c_from)
                else:
                    pad[s, a_to, b_to, c_to : c_to + 1] = row(4 * b_from + c_from)
            elif d1 != 0:
                for a in range(4):
                    if d2 == 0:
                        pad[s, 1 + a, b_to, 1:5] = row(4 * a, 4)
                    else:
                        pad[s, 1 + a, b_to, c_to : c_to + 1] = row(4 * a + c_from)
            else:
                for a in range(4):
                    for b in range(4):
                        pad[s, 1 + a, 1 + b, c_to : c_to + 1] = row(4 * a + b)
        return carry

    lax.fori_loop(0, SLOTS, one_slot, 0)


def place_interior(pad, field):
    for s in range(SLOTS):
        for a in range(4):
            for b in range(4):
                pad[s, 1 + a, 1 + b, 1:5] = field[s, 16 * a + 4 * b : 16 * a + 4 * b + 4]


def windows_of(pad, cols):
    flat = pad.reshape(SLOTS * 6 * 6 * 8, C)
    sub = lax.broadcasted_iota(jnp.int32, (8, C), 0)
    for t in range(SLOTS * 6):
        s, a = t // 6, t % 6
        for k2 in range(3):
            starts = [(6 * t + b) * 8 + k2 for b in range(5)]
            pair = [
                jnp.where(sub < 4, flat[first : first + 8], flat[first + 4 : first + 12])
                for first in starts
            ]
            for k1 in range(3):
                tile = jnp.concatenate([pair[k1], pair[k1 + 2]], axis=0)
                cols[3 * k1 + k2, s, a] = tile.astype(bf16)


def window(cols, k0, k1, k2):
    return cols[3 * k1 + k2, :, k0 : k0 + 4].reshape(SLOTS * VOX, C)


def conv(cols, weight):
    total = jnp.zeros((SLOTS * VOX, C), f32)
    for k0 in range(3):
        left = jnp.concatenate([window(cols, k0, j // 3, j % 3) for j in range(9)], axis=1)
        right = weight[9 * k0 : 9 * k0 + 9].reshape(9 * C, C)
        total = total + jnp.dot(left, right, preferred_element_type=f32)
    return total


def conv_back(cols, weight):
    total = jnp.zeros((SLOTS * VOX, C), f32)
    for k0 in range(3):
        left = jnp.concatenate(
            [window(cols, 2 - k0, 2 - j // 3, 2 - j % 3) for j in range(9)], axis=1
        )
        right = jnp.concatenate([weight[9 * k0 + j] for j in range(9)], axis=1)
        total = total + lax.dot_general(
            left, right, (((1,), (1,)), ((), ())), preferred_element_type=f32
        )
    return total


def weight_grad(cols, grad, centre, out):
    right = jnp.concatenate([grad, jnp.ones((SLOTS * VOX, C), bf16)], axis=1)
    for k0 in range(3):
        left = jnp.concatenate([window(cols, k0, j // 3, j % 3) for j in range(9)], axis=1)
        both = lax.dot_general(
            left, right, (((0,), (0,)), ((), ())), preferred_element_type=f32
        )
        out[9 * C * k0 : 9 * C * (k0 + 1)] = both[:, :C] - both[:, C:] * centre


def window_sums(cols):
    ones = jnp.ones((8, SLOTS * VOX), bf16)
    rows = []
    for k0 in range(3):
        left = jnp.concatenate([window(cols, k0, j // 3, j % 3) for j in range(9)], axis=1)
        total = jnp.dot(ones, left, preferred_element_type=f32)
        rows += [total[0:1, C * j : C * (j + 1)] for j in range(9)]
    return rows


def store_shares(rows, out):
    lane = lax.broadcasted_iota(jnp.int32, (1, C), 1)
    for p in range(PEERS):
        k, skip = divmod(SHARE * p, C)
        line = rows[k] if skip == 0 else pltpu.roll(rows[k], C - skip, 1)
        if skip + SHARE > C:
            line = jnp.where(lane < C - skip, line, pltpu.roll(rows[k + 1], C - skip, 1))
        out[p : p + 1] = jnp.where(lane < SHARE, line, 0.0)


def centre_of(field, active):
    total = jnp.zeros((1, C), f32)
    slots = 0.0
    for s in range(SLOTS):
        total = total + jnp.sum(field[s], axis=0, keepdims=True)
        slots = slots + slot_weight(active, s)
    return (total / (jnp.maximum(slots, 1.0) * VOX)).astype(bf16).astype(f32)


def start_kernel(feat_in, gout_in, active_in, list_in, stats, both, active, send_list, sems):
    feat, gout = both.at[0], both.at[1]
    copies = fetch(
        (active_in, list_in, feat_in, gout_in), (active, send_list, feat, gout), sems
    )
    for copy in copies:
        copy.wait()
    total = jnp.zeros((1, C), f32)
    squares = jnp.zeros((1, C), f32)
    slots = 0.0
    for s in range(SLOTS):
        w = slot_weight(active, s)
        x = feat[s].astype(f32)
        total = total + w * jnp.sum(x, axis=0, keepdims=True)
        squares = squares + w * jnp.sum(x * x, axis=0, keepdims=True)
        slots = slots + w
    packed = pack_stats([total, squares, jnp.full((1, C), slots, f32)])
    record = lax.broadcasted_iota(jnp.int32, (CAP, C), 0)
    lane = lax.broadcasted_iota(jnp.int32, (CAP, C), 1)
    select = jnp.where(lane == 4 * record + 3, 1.0, 0.0).astype(bf16)
    ids = lax.dot_general(
        send_list[:, 0].astype(bf16),
        select,
        (((0,), (0,)), ((), ())),
        preferred_element_type=f32,
    )
    stats[...] = ids + packed[0:1]


def first_kernel(
    active_in, own_in, pos_in, gain_in, bias_in, w1_in, w2_in, stats1, *rest
):
    fields, rest = rest[:3], rest[3:]
    middle, gas, cols_a, both, index = rest[:5]
    table_f, table_g, pad, cols_g, act, scratch, ids_v = rest[5:12]
    active, owners, positions, ids, gain1, bias1, w1, w2, sems = rest[12:]
    me = lax.axis_index("space")
    copies = fetch(
        (gain_in, bias_in, active_in, own_in, pos_in, w1_in, w2_in),
        (gain1, bias1, active, owners, positions, w1, w2),
        sems,
    )
    ids_v[...] = stats1[...].astype(jnp.int32)
    ids_copy = pltpu.make_async_copy(ids_v, ids, sems.at[7])
    ids_copy.start()
    feat, gout = fields[0].at[0, 0], fields[0].at[0, 1]
    mean, inv, _ = norm_stats(stats1)
    copies[0].wait()
    copies[1].wait()

    def act_of(x):
        n = (x - mean) * inv * gain1[...] + bias1[...]
        return n * sigmoid(n)

    fill_tables(
        (table_f, table_g),
        fields,
        scratch,
        me,
        lambda ref, s: (act_of(ref[0, s].astype(f32)), ref[1, s].astype(f32)),
    )
    for copy in copies[2:5]:
        copy.wait()
    ids_copy.wait()
    find_planes(owners, positions, ids, index, me)
    for s in range(SLOTS):
        act[s] = slot_weight(active, s) * act_of(feat[s].astype(f32))
    place_interior(pad, act)
    place_halo(pad, table_f, index)
    windows_of(pad, cols_a)
    copies[5].wait()
    middle[...] = conv(cols_a, w1).reshape(SLOTS, VOX, C)
    for s in range(SLOTS):
        act[s] = jnp.where(active[0, s] > 0, gout[s].astype(f32), 0.0)
    place_interior(pad, act)
    place_halo(pad, table_g, index)
    windows_of(pad, cols_g)
    copies[6].wait()
    gas[...] = conv_back(cols_g, w2).reshape(SLOTS, VOX, C)
    both[0] = middle[...].astype(bf16)
    both[1] = gas[...].astype(bf16)


def sums_kernel(active, middle, stats2):
    total = jnp.zeros((1, C), f32)
    squares = jnp.zeros((1, C), f32)
    slots = 0.0
    for s in range(SLOTS):
        w = slot_weight(active, s)
        x = middle[s]
        total = total + w * jnp.sum(x, axis=0, keepdims=True)
        squares = squares + w * jnp.sum(x * x, axis=0, keepdims=True)
        slots = slots + w
    packed = pack_stats([total, squares, jnp.full((1, C), slots, f32)])
    stats2[...] = jnp.broadcast_to(packed[0:1], (PEERS, C))


def second_kernel(active, middle, gas, stats2, gain2, bias2, stats3):
    mean, inv, _ = norm_stats(stats2)
    gain = gain2[...]
    sum_q = jnp.zeros((1, C), f32)
    sum_c = jnp.zeros((1, C), f32)
    for s in range(SLOTS):
        hat = (middle[s] - mean) * inv
        n = hat * gain + bias2[...]
        sg = sigmoid(n)
        q = gas[s] * slot_weight(active, s) * sg * (1.0 + n * (1.0 - sg)) * gain
        sum_q = sum_q + jnp.sum(q, axis=0, keepdims=True)
        sum_c = sum_c + jnp.sum(q * hat, axis=0, keepdims=True)
    packed = pack_stats([sum_q, sum_c])
    stats3[...] = jnp.broadcast_to(packed[0:1], (PEERS, C))


def third_kernel(
    feat,
    gout,
    active,
    index,
    middle,
    gas,
    stats1,
    stats2,
    stats3,
    gain1,
    bias1,
    gain2,
    bias2,
    w1,
    w2,
    cols_a,
    *rest,
):
    fields, rest = rest[:3], rest[3:]
    block, q1, keep, give = rest[:4]
    table_a, table_g, pad, cols, field, own, scratch = rest[4:11]
    grad_w1, grad_w2, sums1, sums2 = rest[11:]
    me = lax.axis_index("space")
    mean, inv, count = norm_stats(stats2)
    gain = gain2[...]
    bias = bias2[...]
    packed = total_of(stats3)
    mean_q = unpack_stat(packed, 0)[0:1] / count
    mean_c = unpack_stat(packed, 1)[0:1] / count

    def both_of(x, g):
        hat = (x - mean) * inv
        n = hat * gain + bias
        sg = sigmoid(n)
        q = g * sg * (1.0 + n * (1.0 - sg)) * gain
        grad = inv * (q - mean_q - hat * mean_c)
        return n * sg, grad.astype(bf16).astype(f32)

    fill_tables(
        (table_a, table_g),
        fields,
        scratch,
        me,
        lambda ref, s: both_of(ref[0, s].astype(f32), ref[1, s].astype(f32)),
    )
    for s in range(SLOTS):
        act, grad = both_of(middle[s], gas[s])
        own[0, s] = slot_weight(active, s) * act
        own[1, s] = slot_weight(active, s) * grad
    place_interior(pad, own.at[0])
    place_halo(pad, table_a, index)
    windows_of(pad, cols)
    out = conv(cols, w2).reshape(SLOTS, VOX, C)
    for s in range(SLOTS):
        w = slot_weight(active, s)
        block[s] = ((feat[s].astype(f32) + out[s]) * w).astype(bf16)
        field[s] = jnp.where(active[0, s] > 0, gout[s].astype(f32), 0.0)
    store_shares(window_sums(cols), sums2)
    centre2 = centre_of(field, active)
    weight_grad(cols, field[...].astype(bf16).reshape(SLOTS * VOX, C), centre2, grad_w2)
    store_shares(window_sums(cols_a), sums1)
    centre1 = centre_of(own.at[1], active)
    weight_grad(cols_a, own[1].astype(bf16).reshape(SLOTS * VOX, C), centre1, grad_w1)
    place_interior(pad, own.at[1])
    place_halo(pad, table_g, index)
    windows_of(pad, cols)
    gaf = conv_back(cols, w1).reshape(SLOTS, VOX, C)
    mean1, inv1, _ = norm_stats(stats1)
    sum_q = jnp.zeros((1, C), f32)
    sum_c = jnp.zeros((1, C), f32)
    for s in range(SLOTS):
        hat = (feat[s].astype(f32) - mean1) * inv1
        n = hat * gain1[...] + bias1[...]
        sg = sigmoid(n)
        q = gaf[s] * slot_weight(active, s) * sg * (1.0 + n * (1.0 - sg)) * gain1[...]
        q1[s] = q
        sum_q = sum_q + jnp.sum(q, axis=0, keepdims=True)
        sum_c = sum_c + jnp.sum(q * hat, axis=0, keepdims=True)
    packed = pack_stats([sum_q, sum_c])
    sums = jnp.concatenate(terms(packed[0:1], 3), axis=0)
    sums1[...], sums2[...] = terms(sums1[...] + pltpu.roll(sums2[...], C // 2, 1), 2)

    def store(out, core):
        kind = out.dtype
        for chip in range(PEERS // 2):
            p = 2 * chip + core
            rows = [
                grad_w1[SHARE * p : SHARE * (p + 1)],
                grad_w2[SHARE * p : SHARE * (p + 1)],
                sums,
                jnp.zeros((1, C), f32),
            ]
            out[chip, 0:CENTRE_ROW] = jnp.concatenate(rows, axis=0).astype(kind)
            rows = [sums1[p : p + 1], sums2[p : p + 1], centre1, centre2]
            rows = jnp.concatenate([*rows, jnp.zeros((4, C), f32)], axis=0)
            out[chip, CENTRE_ROW:ROWS] = rows.astype(kind)

    @pl.when(me % 2 == 0)
    def _():
        store(keep, 0)
        store(give, 1)

    @pl.when(me % 2 == 1)
    def _():
        store(keep, 1)
        store(give, 0)


def pair_kernel(own, other, out):
    at = lax.broadcasted_iota(jnp.int32, (CENTRE_ROW, C), 0)
    for n in range(PEERS // 2):
        total = own[n, 0:CENTRE_ROW] + other[n, 0:CENTRE_ROW].astype(f32)
        row = jnp.sum(total[SUM_ROW : SUM_ROW + 3], axis=0, keepdims=True)
        for k, term in enumerate(terms(row, 3)):
            total = jnp.where(at == SUM_ROW + k, term, total)
        out[n, 0:CENTRE_ROW] = total.astype(bf16)
        more = other[n, CENTRE_ROW:ROWS].astype(f32)
        more = own[n, CENTRE_ROW:ROWS] + pltpu.roll(more, 4, 0)
        out[n, CENTRE_ROW:ROWS] = more.astype(bf16)


def last_kernel(feat, gout, active, stats1, q1, parts, gain1, grad_in, rows):
    total = parts[0].astype(f32)
    for n in range(1, PEERS // 2):
        total = total + parts[n].astype(f32)
    mean1, inv1, count = norm_stats(stats1)
    packed = jnp.sum(total[SUM_ROW : SUM_ROW + 3], axis=0, keepdims=True)
    packed = jnp.broadcast_to(packed, (8, C))
    mean_q = unpack_stat(packed, 0)[0:1] / count
    mean_c = unpack_stat(packed, 1)[0:1] / count
    for s in range(SLOTS):
        hat = (feat[s].astype(f32) - mean1) * inv1
        back = slot_weight(active, s) * inv1 * (q1[s] - mean_q - hat * mean_c)
        top = jnp.where(active[0, s] > 0, gout[s].astype(f32), 0.0)
        grad_in[s] = (top + back).astype(bf16)
    left, right = [], []
    at = lax.broadcasted_iota(jnp.int32, (8, C), 0) % 4
    for n in range(PEERS // 2):
        more = parts[n, CENTRE_ROW:ROWS].astype(f32)
        left.append(more)
        line = []
        for weight in range(2):
            near = jnp.where(at == 1, pltpu.roll(more, 7 - weight, 0), 0.0)
            line.append(jnp.where(at == 0, pltpu.roll(more, 6 - weight, 0), near))
        right.append(jnp.concatenate(line, axis=1))
    outer = lax.dot_general(
        jnp.concatenate(left, axis=0).astype(bf16),
        jnp.concatenate(right, axis=0).astype(bf16),
        (((0,), (0,)), ((), ())),
        preferred_element_type=f32,
    )
    for weight in range(2):
        back = outer[64 * weight : 64 * weight + SHARE, C * weight : C * (weight + 1)]
        whole = total[SHARE * weight : SHARE * (weight + 1)] + back
        for n in range(8):
            rows[n, 56 * weight : 56 * weight + SHARE] = whole
            rows[n, 56 * weight + SHARE : 56 * weight + 56] = jnp.zeros((2, C), f32)


vmem = pl.BlockSpec(memory_space=pltpu.VMEM)
smem = pl.BlockSpec(memory_space=pltpu.SMEM)
hbm = pl.BlockSpec(memory_space=pltpu.HBM)


def call(kernel, specs, out_shape, scratch, args, out_specs=None):
    args = [
        pltpu.with_memory_space_constraint(arg, pltpu.HBM) if spec is hbm else arg
        for spec, arg in zip(specs, args)
    ]
    return pl.pallas_call(
        kernel,
        in_specs=specs,
        out_specs=out_specs or [vmem] * len(out_shape),
        out_shape=out_shape,
        scratch_shapes=scratch,
        compiler_params=pltpu.CompilerParams(vmem_limit_bytes=VMEM_BYTES),
    )(*args)


def shape(*dims, dtype=f32):
    return jax.ShapeDtypeStruct(dims, dtype)


def pairs_of(step, first):
    lower = [n for n in range(PEERS) if n // step % 2 == first]
    return [(n, (n + step) % PEERS) for n in lower] + [((n + step) % PEERS, n) for n in lower]


far_pairs = (pairs_of(4, 0), pairs_of(4, 1))
near_pairs = (pairs_of(1, 0), pairs_of(1, 1))


def exchange(fields, stats):
    far = [lax.ppermute(fields, "space", pairs) for pairs in far_pairs]
    stats = spread(stats)
    *far, stats = lax.optimization_barrier((*far, stats))
    three = jnp.stack([fields, *far])
    near = [lax.ppermute(three, "space", pairs) for pairs in near_pairs]
    return [three, *near], stats


def spread(stats):
    return lax.all_to_all(stats, "space", 0, 0, tiled=True)


chip_groups = [list(range(core, PEERS, 2)) for core in range(2)]


def per_device(
    features,
    active,
    neighbor_owner,
    record_position,
    send_list,
    conv_first,
    conv_second,
    gain_first,
    bias_first,
    gain_second,
    bias_second,
    grad_output,
):
    feat = features[0]
    gout = grad_output[0]
    owners = neighbor_owner[0]
    positions = record_position[0]
    lists = send_list[0].transpose(2, 0, 1)
    gain1, bias1 = gain_first.reshape(1, C), bias_first.reshape(1, C)
    gain2, bias2 = gain_second.reshape(1, C), bias_second.reshape(1, C)
    field = (SLOTS, VOX, C)
    wide = pltpu.VMEM(field, f32)
    two = pltpu.VMEM((2, *field), f32)
    scratch = pltpu.VMEM((2, 2, *field), f32)
    table = pltpu.VMEM((LANES * PLANES, PLANE, C), f32)
    pad = pltpu.VMEM((SLOTS, 6, 6, 8, C), f32)
    cols_shape = (9, SLOTS, 6, PLANE, C)
    cols = pltpu.VMEM(cols_shape, bf16)

    stats1, both = call(
        start_kernel,
        [hbm, hbm, hbm, hbm],
        [shape(PEERS, C), shape(2, *field, dtype=bf16)],
        [
            pltpu.SMEM((1, SLOTS), jnp.int32),
            pltpu.VMEM((CAP, 1, PEERS), jnp.int32),
            pltpu.SemaphoreType.DMA((4,)),
        ],
        (feat, gout, active, lists),
    )
    fields0, stats1 = exchange(both, stats1)

    middle, gas, cols_a, both, index = call(
        first_kernel,
        [hbm] * 7 + [vmem] * 4,
        [shape(*field), shape(*field), shape(*cols_shape, dtype=bf16)]
        + [shape(2, *field, dtype=bf16), shape(SLOTS, 26, dtype=jnp.int32)],
        [table, table, pad, cols, wide, scratch, pltpu.VMEM((PEERS, C), jnp.int32)]
        + [
            pltpu.SMEM((1, SLOTS), jnp.int32),
            pltpu.SMEM((SLOTS, 26), jnp.int32),
            pltpu.SMEM((SLOTS, 26), jnp.int32),
            pltpu.SMEM((PEERS, C), jnp.int32),
            pltpu.VMEM((1, C), f32),
            pltpu.VMEM((1, C), f32),
            pltpu.VMEM((27, C, C), bf16),
            pltpu.VMEM((27, C, C), bf16),
            pltpu.SemaphoreType.DMA((8,)),
        ],
        (active, owners, positions, gain1, bias1, conv_first, conv_second, stats1, *fields0),
        [vmem] * 4 + [smem],
    )
    (stats2,) = call(sums_kernel, [smem, vmem], [shape(PEERS, C)], [], (active, middle))
    fields1, stats2 = exchange(both, stats2)

    (stats3,) = call(
        second_kernel,
        [smem] + [vmem] * 5,
        [shape(PEERS, C)],
        [],
        (active, middle, gas, stats2, gain2, bias2),
    )
    stats3 = spread(stats3)

    weight = pltpu.VMEM((27 * C, C), f32)
    line = pltpu.VMEM((PEERS, C), f32)
    block, q1, keep, give = call(
        third_kernel,
        [vmem, vmem, smem, smem] + [vmem] * 15,
        [shape(*field, dtype=bf16), shape(*field)]
        + [shape(PEERS // 2, ROWS, C), shape(PEERS // 2, ROWS, C, dtype=bf16)],
        [table, table, pad, cols, wide, two, scratch, weight, weight, line, line],
        (feat, gout, active, index, middle, gas, stats1, stats2, stats3)
        + (gain1, bias1, gain2, bias2, conv_first, conv_second, cols_a, *fields1),
    )
    other = lax.ppermute(give, "space", near_pairs[0])
    (share,) = call(
        pair_kernel,
        [vmem, vmem],
        [shape(PEERS // 2, ROWS, C, dtype=bf16)],
        [],
        (keep, other),
    )
    share = lax.all_to_all(share, "space", 0, 0, axis_index_groups=chip_groups)

    grad_in, rows = call(
        last_kernel,
        [vmem, vmem, smem] + [vmem] * 4,
        [shape(*field, dtype=bf16), shape(8, 112, C)],
        [],
        (feat, gout, active, stats1, q1, share, gain1),
    )
    rows = lax.all_to_all(rows, "scene", 0, 0)
    rows = jnp.sum(rows, axis=0).astype(bf16)
    return (block[None], grad_in[None], rows[:SHARE], rows[56 : 56 + SHARE])


def solution(mesh):
    return jax.shard_map(
        per_device,
        mesh=mesh,
        in_specs=(
            P("scene", "space", None, None),
            P("scene", "space"),
            P("scene", "space", None),
            P("scene", "space", None),
            P("scene", "space", None, None),
            P(),
            P(),
            P(),
            P(),
            P(),
            P(),
            P("scene", "space", None, None),
        ),
        out_specs=(
            P("scene", "space", None, None),
            P("scene", "space", None, None),
            P("space", None),
            P("space", None),
        ),
        check_vma=False,
    )
```
